32 devices in a mesh: gx: 8 (over z, y), gy: 4 (over x, core).
Axes of the slice: x: 2, y: 2, z: 4, core: 2. Of those that a mesh axis runs over, the one named last changes fastest.
Arguments:
- state: float32 [8, 256, 512], P(None, 'gx', 'gy'), may hold values from -6 to 6
- load_vector: bfloat16 [8, 256, 512], P(None, 'gx', 'gy'), may hold values from -6 to 6
- active: int32 [256, 512], P('gx', 'gy'), may hold values 0 or 1
- stiff_band: float32 [3, 5], replicated, may hold values from -0.6 to 1.2
- mass_band: float32 [3, 5], replicated, may hold values from 0.1 to 0.6
- eig_basis: float32 [3, 16, 16], replicated, may hold values from -1.5 to 1.5
- eig_values: float32 [3, 16], replicated, may hold values from 0.2 to 5
- cut_cols: int32 [8, 4, 2], P('gx', 'gy'), may hold values from -1 to 63, as said below
- cut_inverse: bfloat16 [8, 4, 2, 16, 256, 256], P('gx', 'gy'), may hold values from -0.375 to 0.375
Outputs:
- smoothed: float32 [8, 256, 512], P(None, 'gx', 'gy')
The draws below stay inside these ranges and needn't reach their ends.
Inputs may be any that keep to these rules, and one draw needn't show every extreme that they name: `cut_cols`: on each device the entries that are not -1 name distinct local patch columns; a device holds 0 to 2 such entries and some device holds 2.
All inputs are finite; a program needn't handle non-finite values. No bound on the sum of `active` on one device may be relied on, other than what follows from the above.
Results may differ from the reference program's by a relative error of at most 0.0003.
Values sent between devices are 32-bit elements; how exact they have to be, the bound alone decides.
A program may use at most 64 MiB of HBM per device.

```python
import math
import jax
import jax.numpy as jnp
from jax import lax

BAND = 4
PATCH = 16
CX = 32
CY = 128
NZ = 8
MOST = 2
COLS = 64
NX = 256
NY = 512
N_GX = 8
N_GY = 4


def draw_cut_cols(key, part):
    tiles = N_GX * N_GY
    keys = jax.random.split(jax.random.fold_in(key, 11), tiles)
    orders = jax.vmap(lambda single: jax.random.permutation(single, COLS))(keys)[:, :MOST]
    counts = jax.random.randint(jax.random.fold_in(key, 12), (tiles,), 0, MOST + 1)
    chosen = jax.random.randint(jax.random.fold_in(key, 13), (), 0, tiles)
    counts = jnp.where(jnp.arange(tiles) == chosen, MOST, counts)
    in_use = jnp.arange(MOST)[None, :] < counts[:, None]
    return jnp.where(in_use, orders, -1).astype(jnp.int32).reshape(N_GX, N_GY, MOST)


def place_ends(array, own_key, smallest, top_value):
    dims = array.shape
    index_at = [jax.random.randint(jax.random.fold_in(own_key, axis), (), 0, dims[axis]) for axis in range(len(dims))]
    array = array.at[tuple(index_at)].set(smallest)
    longest = dims.index(max(dims))
    index_at[longest] = (index_at[longest] + 1) % dims[longest]
    return array.at[tuple(index_at)].set(top_value)


def shard_levels(key, dims, shards, low, high):
    def one(dim, shards_of):
        steps = jax.random.uniform(jax.random.fold_in(jax.random.fold_in(key, 6), dim), (shards_of,), jnp.float32, low / len(shards), high / len(shards))
        return jnp.repeat(jnp.exp(steps), dims[dim] // shards_of).reshape((-1,) + (1,) * (len(dims) - dim - 1))

    factor_of = one(*shards[0])
    for cut in shards[1:]:
        factor_of = factor_of * one(*cut)
    return factor_of


def normal_values(stream_key, shape, deviation, limit, shards=(), kind=jnp.bfloat16):
    values = deviation * jax.random.normal(stream_key, shape, jnp.float32)
    if shards:
        values = values * shard_levels(stream_key, shape, shards, -0.22, 0.18)
    return jnp.clip(values, -limit, limit).astype(kind)


def setup_inputs(seed: int = 0) -> dict:
    splits = jax.random.split(jax.random.key(seed), 10)
    return {
        "state": normal_values(splits[0], (NZ, NX, NY), 1.0, 6.0, ((1, 8), (2, 4)), jnp.float32),
        "load_vector": normal_values(splits[1], (NZ, NX, NY), 1.0, 6.0, ((1, 8), (2, 4))),
        "active": place_ends((jax.random.randint(splits[2], (NX, NY), 0, 4) < 3).astype(jnp.int32), jax.random.fold_in(splits[2], 1), 0, 1),
        "stiff_band": jnp.clip(jax.random.uniform(splits[3], (3, BAND + 1), jnp.float32, -0.6, 1.2), -0.6, 1.2),
        "mass_band": jnp.clip(jax.random.uniform(splits[4], (3, BAND + 1), jnp.float32, 0.1, 0.6), 0.1, 0.6),
        "eig_basis": normal_values(splits[5], (3, PATCH, PATCH), PATCH ** -0.5, 1.5, (), jnp.float32),
        "eig_values": jnp.clip(jnp.exp(jax.random.uniform(splits[6], (3, PATCH), jnp.float32, math.log(0.2), math.log(5.0))), 0.2, 5.0),
        "cut_cols": draw_cut_cols(jax.random.fold_in(splits[9], 71), 0),
        "cut_inverse": normal_values(splits[8], (N_GX, N_GY, MOST, PATCH, PATCH * PATCH, PATCH * PATCH), (PATCH * PATCH) ** -0.5, 0.375, ((0, 8), (1, 4))),
    }


damping = 0.5


def band_valid(values, coeffs, along):
    length = values.shape[along] - 2 * BAND
    result = coeffs[0] * lax.slice_in_dim(values, BAND, BAND + length, axis=along)
    for offset in range(1, BAND + 1):
        upper = lax.slice_in_dim(values, BAND + offset, BAND + offset + length, axis=along)
        lower = lax.slice_in_dim(values, BAND - offset, BAND - offset + length, axis=along)
        result = result + coeffs[offset] * (upper + lower)
    return result


def apply_operator(field, stiff_band, mass_band):
    padded = jnp.pad(field, ((BAND, BAND), (0, 0), (0, 0)))
    mass_z = band_valid(padded, mass_band[0], 0)
    stiff_z = band_valid(padded, stiff_band[0], 0)
    mass_xz = band_valid(mass_z, mass_band[1], 1)
    stiff_xz = band_valid(mass_z, stiff_band[1], 1)
    mass_x_stiff_z = band_valid(stiff_z, mass_band[1], 1)
    return band_valid(stiff_xz + mass_x_stiff_z, mass_band[2], 2) + band_valid(mass_xz, stiff_band[2], 2)


def fold_blocks(values, along, half_patch):
    lower = lax.slice_in_dim(values, 0, half_patch, axis=along + 1)
    upper = lax.slice_in_dim(values, half_patch, 2 * half_patch, axis=along + 1)
    widths_low = [(0, 0)] * values.ndim
    widths_high = [(0, 0)] * values.ndim
    widths_low[along] = (0, 1)
    widths_high[along] = (1, 0)
    return jnp.pad(lower, widths_low) + jnp.pad(upper, widths_high)


def reference(state, load_vector, active, stiff_band, mass_band, eig_basis, eig_values, cut_cols, cut_inverse):
    highest = lax.Precision.HIGHEST
    half_patch = PATCH // 2
    quarter = PATCH // 4
    blocks_x = NX // half_patch
    blocks_y = NY // half_patch
    blocks_z = NZ // half_patch
    local_x = CX // half_patch
    local_y = CY // half_patch
    live_mask = active.astype(jnp.float32)
    padded = jnp.pad(state, ((0, 0), (BAND, BAND), (BAND, BAND)))
    resid = live_mask[None] * (load_vector.astype(jnp.float32) - apply_operator(padded, stiff_band, mass_band))
    resid_pad = jnp.pad(resid, ((quarter, quarter), (quarter, quarter), (quarter, quarter)))
    basis_z, basis_x, basis_y = eig_basis[0], eig_basis[1], eig_basis[2]
    denom = 1.0 / (eig_values[0][:, None, None] + eig_values[1][None, :, None] + eig_values[2][None, None, :])
    tile_x = jnp.arange(N_GX, dtype=jnp.int32)[:, None, None]
    tile_y = jnp.arange(N_GY, dtype=jnp.int32)[None, :, None]
    column = jnp.maximum(cut_cols, 0)
    block_a = (tile_x * local_x + column // local_y).astype(jnp.int32)
    block_b = (tile_y * local_y + column % local_y).astype(jnp.int32)
    in_use = (cut_cols >= 0).astype(jnp.float32)
    colmask = jnp.zeros((blocks_x, blocks_y), jnp.float32).at[block_a.ravel(), block_b.ravel()].max(in_use.ravel())

    def add_row(block_row, accum):
        start = (block_row * half_patch).astype(jnp.int32)
        slab = lax.dynamic_slice_in_dim(resid_pad, start, PATCH, axis=1)
        blocks = slab.reshape(blocks_z + 1, half_patch, PATCH, blocks_y + 1, half_patch)
        blocks = jnp.concatenate([blocks[:-1], blocks[1:]], axis=1)
        blocks = jnp.concatenate([blocks[:, :, :, :-1], blocks[:, :, :, 1:]], axis=4)
        modes = jnp.einsum('zk,czxby->ckxby', basis_z, blocks, precision=highest)
        modes = jnp.einsum('xi,ckxby->ckiby', basis_x, modes, precision=highest)
        modes = jnp.einsum('yj,ckiby->ckibj', basis_y, modes, precision=highest)
        modes = modes * denom[None, :, :, None, :]
        modes = jnp.einsum('yj,ckibj->ckiby', basis_y, modes, precision=highest)
        modes = jnp.einsum('xi,ckiby->ckxby', basis_x, modes, precision=highest)
        back = jnp.einsum('zk,ckxby->czxby', basis_z, modes, precision=highest)
        keep = 1.0 - lax.dynamic_index_in_dim(colmask, block_row, 0, keepdims=False)
        back = back * keep[None, None, None, :, None]
        folded = fold_blocks(back, 3, half_patch).reshape(blocks_z, PATCH, PATCH, NY + half_patch)
        folded = fold_blocks(folded, 0, half_patch).reshape(NZ + half_patch, PATCH, NY + half_patch)
        current = lax.dynamic_slice_in_dim(accum, start, PATCH, axis=1)
        return lax.dynamic_update_slice_in_dim(accum, current + folded, start, axis=1)

    accum = jnp.zeros((NZ + half_patch, NX + half_patch, NY + half_patch), jnp.float32)
    accum = lax.fori_loop(0, blocks_x, add_row, accum)
    slots = N_GX * N_GY * MOST
    flat_cols = cut_cols.reshape(slots)
    flat_inverse = cut_inverse.reshape(slots, PATCH, PATCH * PATCH, PATCH * PATCH)

    def add_cut(slot_index, accum):
        entry = flat_cols[slot_index]
        in_use = (entry >= 0).astype(jnp.float32)
        entry = jnp.maximum(entry, 0)
        tile_row = slot_index // (N_GY * MOST)
        tile_col = (slot_index // MOST) % N_GY
        start_x = ((tile_row * local_x + entry // local_y) * half_patch).astype(jnp.int32)
        start_y = ((tile_col * local_y + entry % local_y) * half_patch).astype(jnp.int32)
        anchor = jnp.zeros((), jnp.int32)
        column_cells = lax.dynamic_slice(resid_pad, (anchor, start_x, start_y), (NZ + half_patch, PATCH, PATCH))
        blocks = column_cells.reshape(blocks_z + 1, half_patch, PATCH * PATCH)
        blocks = jnp.concatenate([blocks[:-1], blocks[1:]], axis=1)
        zmodes = jnp.einsum('zk,czq->ckq', basis_z, blocks, precision=highest)
        zmodes = lax.optimization_barrier(zmodes.astype(jnp.bfloat16)).astype(jnp.float32)
        inverse = lax.dynamic_index_in_dim(flat_inverse, slot_index, 0, keepdims=False).astype(jnp.float32)
        dense = jnp.einsum('kpq,ckq->ckp', inverse, zmodes, precision=highest)
        back = jnp.einsum('zk,ckp->czp', basis_z, dense, precision=highest) * in_use
        folded = fold_blocks(back, 0, half_patch).reshape(NZ + half_patch, PATCH, PATCH)
        current = lax.dynamic_slice(accum, (anchor, start_x, start_y), (NZ + half_patch, PATCH, PATCH))
        return lax.dynamic_update_slice(accum, current + folded, (anchor, start_x, start_y))

    accum = lax.fori_loop(0, slots, add_cut, accum)
    total = accum[quarter:quarter + NZ, quarter:quarter + NX, quarter:quarter + NY]
    return state + damping * live_mask[None] * total
```

```python
import functools

import jax
import jax.numpy as jnp
from jax import lax
from jax.experimental import pallas as pl
from jax.experimental.pallas import tpu as pltpu
from jax.sharding import PartitionSpec as P

BAND = 4
PATCH = 16
HALF = PATCH // 2
QUARTER = PATCH // 4
HALO = BAND + QUARTER
LANES = 128
MESH = pl.DeviceIdType.MESH
DIRS = [(dx, dy) for dx in (-1, 0, 1) for dy in (-1, 0, 1) if (dx, dy) != (0, 0)]

damping = 0.5
f32 = jnp.float32
bf16 = jnp.bfloat16


def iota(shape, dim):
    return lax.broadcasted_iota(jnp.int32, shape, dim)


def split(v):
    hi = v.astype(bf16)
    return hi, (v - hi.astype(f32)).astype(bf16)


def dot(a, b):
    return jnp.dot(a, b, preferred_element_type=f32)


def dot_nt(a, b):
    return lax.dot_general(a, b, (((1,), (1,)), ((), ())), preferred_element_type=f32)


def band_of(distance, taps):
    out = jnp.zeros(distance.shape, f32)
    for k in range(BAND + 1):
        out = jnp.where(distance == k, taps[k], out)
    return out


def inner_y(c, ry):
    u = (c - ry) % HALF
    halo = jnp.where(u < QUARTER, u - QUARTER, ry + u - QUARTER)
    return jnp.where(c < ry, c, jnp.where(c < ry + LANES // 2, -1000, halo))


def outer_y(r, ry):
    u = (r - ry) % HALF
    return jnp.where(r < ry, r, jnp.where(r < ry + LANES // 2, u - HALO, ry + u))


def kernel(
    sizes,
    state, load, active, stiff, mass, basis_s, basis, values, cols, inverse,
    out,
    ext, from_left, from_right, pack_left, pack_right,
    inv, yb_hi, yb_lo, wy_hi, wy_lo, sel, dinv,
    s_hi, s_lo, yv, xpq, r_hi, r_lo, uv, vv, tb_hi, tb_lo, tot, edge,
    up, down, left2, right2, corners,
    inv_sem, send1, recv1, send2, recv2,
):
    n_x, n_y = sizes
    nz, rx, ry = state.shape
    wide = rx + 2 * HALO
    slots = inverse.shape[0]
    blocks_x, blocks_y = rx // HALF, ry // HALF
    qx, qy = blocks_x * PATCH, blocks_y * PATCH
    full = ry + LANES
    me_x, me_y = lax.axis_index("gx"), lax.axis_index("gy")

    def exists(dx, dy):
        ok = None
        for d, me, n in ((dx, me_x, n_x), (dy, me_y, n_y)):
            if d:
                part = (me + d >= 0) & (me + d < n)
                ok = part if ok is None else ok & part
        return ok

    def device(dx, dy):
        return (jnp.clip(me_x + dx, 0, n_x - 1), jnp.clip(me_y + dy, 0, n_y - 1))

    fetch = pltpu.make_async_copy(inverse, inv, inv_sem)
    fetch.start()

    own = pl.ds(HALO, rx)
    for z in range(nz):
        ext[z, own, :] = state[z]
        ext[nz + z, own, :] = load[z].astype(f32)
    ext[2 * nz, own, :] = active[...].astype(f32)
    zeros = jnp.zeros((2 * nz + 1, HALO, ry), f32)
    ext[:, pl.ds(0, HALO), :] = zeros
    ext[:, pl.ds(HALO + rx, HALO), :] = zeros
    for ref in (from_left, from_right, up, down, left2, right2, corners):
        ref[...] = jnp.zeros(ref.shape, f32)

    barrier = pltpu.get_barrier_semaphore()
    count = jnp.int32(0)
    for d in DIRS:
        ok = exists(*d)
        count = count + ok.astype(jnp.int32)

        @pl.when(ok)
        def _(d=d):
            pl.semaphore_signal(barrier, inc=1, device_id=device(*d), device_id_type=MESH)

    lane = iota((rx, LANES), 1)
    to_right = jnp.zeros((rx, LANES), f32)
    to_left = jnp.zeros((rx, LANES), f32)
    act = ext[2 * nz, own, :]
    half = LANES // 2
    for z in range(nz):
        s = ext[z, own, :]
        l = pltpu.roll(ext[nz + z, own, :], (half + QUARTER + HALF * z) % LANES, 1)
        group = lane // HALF == z
        first = (lane // HALF == half // HALF + z) & (lane % HALF < QUARTER)
        second = (lane // HALF == half // HALF + z) & (lane % HALF >= QUARTER)
        to_right = jnp.where(group, pltpu.roll(s, (HALF + HALF * z) % LANES, 1), to_right)
        to_right = jnp.where(first, l, to_right)
        to_right = jnp.where(second, pltpu.roll(act, (half + HALF + HALF * z) % LANES, 1), to_right)
        to_left = jnp.where(group, pltpu.roll(s, HALF * z, 1) if z else s, to_left)
        to_left = jnp.where(second, l, to_left)
        to_left = jnp.where(first, pltpu.roll(act, (half + HALF * z) % LANES, 1), to_left)
    pack_right[...] = to_right
    pack_left[...] = to_left

    def copy1(i):
        dx, dy = DIRS[i]
        if dy == 0:
            src = ext.at[:, pl.ds(rx if dx > 0 else HALO, HALO), :]
            dst = ext.at[:, pl.ds(0 if dx > 0 else HALO + rx, HALO), :]
        else:
            pack = pack_right if dy > 0 else pack_left
            land = from_left if dy > 0 else from_right
            if dx == 0:
                src, dst = pack, land.at[pl.ds(HALO, rx), :]
            else:
                src = pack.at[pl.ds(rx - HALO if dx > 0 else 0, HALO), :]
                dst = land.at[pl.ds(0 if dx > 0 else HALO + rx, HALO), :]
        return pltpu.make_async_remote_copy(
            src_ref=src, dst_ref=dst, send_sem=send1.at[i], recv_sem=recv1.at[i],
            device_id=device(dx, dy), device_id_type=MESH,
        )

    def copy2(i):
        dx, dy = DIRS[i]
        if dy == 0:
            src = tot.at[:, pl.ds(HALO + rx if dx > 0 else 0, HALO), :]
            dst = up if dx > 0 else down
        elif dx == 0:
            src = edge.at[pl.ds(HALO, rx), :]
            dst = left2 if dy > 0 else right2
        else:
            src = edge.at[pl.ds(HALO + rx if dx > 0 else 0, HALO), :]
            dst = corners.at[(dx < 0) * 2 + (dy < 0)]
        return pltpu.make_async_remote_copy(
            src_ref=src, dst_ref=dst, send_sem=send2.at[i], recv_sem=recv2.at[i],
            device_id=device(dx, dy), device_id_type=MESH,
        )

    def start_all(copy):
        for i, d in enumerate(DIRS):
            @pl.when(exists(*d))
            def _(i=i):
                copy(i).start()

    def wait_recv_all(copy):
        for i, (dx, dy) in enumerate(DIRS):
            @pl.when(exists(-dx, -dy))
            def _(i=i):
                copy(i).wait_recv()

    def wait_send_all(copy):
        for i, d in enumerate(DIRS):
            @pl.when(exists(*d))
            def _(i=i):
                copy(i).wait_send()

    pl.semaphore_wait(barrier, count)
    start_all(copy1)

    distance = jnp.abs(outer_y(iota((full, full), 0), ry) - inner_y(iota((full, full), 1), ry))
    for j, taps in enumerate((mass, stiff)):
        h, l = split(band_of(distance, [taps[2, k] for k in range(BAND + 1)]))
        yb_hi[:, pl.ds(j * full, full)] = h
        yb_lo[:, pl.ds(j * full, full)] = l

    highest = lax.Precision.HIGHEST
    tile_y = jnp.dot(
        basis[2], (iota((PATCH, qy), 0) == iota((PATCH, qy), 1) % PATCH).astype(f32),
        precision=highest, preferred_element_type=f32,
    )
    place = inner_y(iota((full, qy), 0), ry) + QUARTER - HALF * (iota((full, qy), 1) // PATCH)
    wy = jnp.zeros((full, qy), f32)
    for t in range(PATCH):
        wy = jnp.where(place == t, tile_y[t : t + 1, :], wy)
    h, l = split(wy)
    wy_hi[...] = h
    wy_lo[...] = l

    def wx_of(shape, rows, reps_r, reps_c):
        r, c = iota(shape, 0), iota(shape, 1)
        t = r % wide - (HALO - QUARTER) - HALF * ((c % qx) // PATCH)
        t = jnp.where((r < wide * reps_r) & (c < qx * reps_c), t, -1)
        tile = jnp.dot(
            basis[1], (iota((PATCH, shape[1]), 0) == iota((PATCH, shape[1]), 1) % PATCH).astype(f32),
            precision=highest, preferred_element_type=f32,
        )
        w = jnp.zeros(shape, f32)
        for k in range(PATCH):
            w = jnp.where(t == k, tile[k : k + 1, :], w)
        return w

    pad_r = -(-2 * wide // LANES) * LANES
    pad_c = -(-qx // LANES) * LANES
    gx2 = wx_of((pad_r, pad_c), wide, 2, 1).T[:qx, : 2 * wide]
    g_hi, g_lo = split(gx2)
    g_lo = g_lo[:, :wide]
    b_hi, b_lo = split(wx_of((wide, 2 * qx), wide, 1, 2))
    b_lo = b_lo[:, :qx]

    c = iota((wide, 4 * wide), 1)
    dist_x = jnp.abs(iota((wide, 4 * wide), 0) - c % wide)
    bx = jnp.where(
        (c // wide) % 2 == 0,
        band_of(dist_x, [mass[1, k] for k in range(BAND + 1)]),
        band_of(dist_x, [stiff[1, k] for k in range(BAND + 1)]),
    )
    bx_hi, bx_lo = split(bx)
    bx_lo = bx_lo[:, : 2 * wide]

    lane_q = iota((1, qy), 1)
    cut = [cols[0, 0, m] for m in range(slots)]
    y_in = inner_y(iota((full, PATCH * PATCH), 0), ry)
    y_to = iota((full, PATCH * PATCH), 1) % PATCH
    for m in range(slots):
        b_m = cut[m] & (blocks_y - 1)
        sel[m] = (y_in + QUARTER - HALF * b_m == y_to).astype(f32).astype(bf16)

    def pick(shape, dim, row):
        index = iota(shape, dim)
        v = jnp.zeros(shape, f32)
        for k in range(PATCH):
            v = jnp.where(index % PATCH == k, values[row, k], v)
        return v

    lam = pick((qx, qy), 0, 1) + pick((qx, qy), 1, 2)
    column = (iota((qx, qy), 0) // PATCH) * blocks_y + iota((qx, qy), 1) // PATCH
    keep = jnp.ones((qx, qy), f32)
    for m in range(slots):
        keep = jnp.where(column == cut[m], 0.0, keep)
    for k in range(PATCH):
        dinv[k] = keep / (values[0, k] + lam)

    wait_recv_all(copy1)

    lane_w = iota((wide, LANES), 1)
    halo_l, halo_r = from_left[...], from_right[...]
    comb = jnp.where(lane_w < half, halo_l, pltpu.roll(halo_r, half, 1))
    low = lane_w % HALF < QUARTER
    load_t = jnp.where(low, halo_l, halo_r)
    act_t = jnp.where(low, pltpu.roll(halo_l, LANES - QUARTER, 1), pltpu.roll(halo_r, QUARTER, 1))
    act_w = ext[2 * nz]
    for z in range(nz):
        rows = pl.ds(z * wide, wide)
        h, l = split(ext[z])
        s_hi[rows, pl.ds(0, ry)] = h
        s_lo[rows, pl.ds(0, ry)] = l
        h, l = split(jnp.where((lane_w % half) // HALF == z, comb, 0.0))
        s_hi[rows, pl.ds(ry, LANES)] = h
        s_lo[rows, pl.ds(ry, LANES)] = l
    yv[...] = (
        dot(s_hi[...], yb_hi[...]) + dot(s_lo[...], yb_hi[...]) + dot(s_hi[...], yb_lo[...])
    ).reshape(nz, wide, 2 * full)

    def mix(step, carry):
        rows = pl.ds(pl.multiple_of(step * PATCH, PATCH), PATCH)
        y1 = [yv[z, rows, pl.ds(0, full)] for z in range(nz)]
        y2 = [yv[z, rows, pl.ds(full, full)] for z in range(nz)]
        for z in range(nz):
            p = q = None
            for w in range(nz):
                k = abs(z - w)
                if k > BAND:
                    continue
                m_y1 = mass[0, k] * y1[w]
                term = stiff[0, k] * y1[w] + mass[0, k] * y2[w]
                p = term if p is None else p + term
                q = m_y1 if q is None else q + m_y1
            for j, part in enumerate(split(p)):
                xpq[z, pl.ds(pl.multiple_of(2 * j * wide + step * PATCH, PATCH), PATCH), :] = part
            for j, part in enumerate(split(q)):
                xpq[z, pl.ds(pl.multiple_of((2 * j + 1) * wide + step * PATCH, PATCH), PATCH), :] = part
        return carry

    lax.fori_loop(0, wide // PATCH, mix, 0)

    for z in range(nz):
        applied = dot(bx_hi, xpq[z]) + dot(bx_lo, xpq[z, pl.ds(0, 2 * wide), :])
        rows = pl.ds(z * wide, wide)
        r0 = act_w * (ext[nz + z] - applied[:, :ry])
        mine = lane_w // HALF == half // HALF + z
        r1 = jnp.where(mine, act_t * (load_t - applied[:, ry:]), 0.0)
        h, l = split(r0)
        r_hi[rows, pl.ds(0, ry)] = h
        r_lo[rows, pl.ds(0, ry)] = l
        h, l = split(r1)
        r_hi[rows, pl.ds(ry, LANES)] = h
        r_lo[rows, pl.ds(ry, LANES)] = l

    t1 = dot(r_hi[...], wy_hi[...]) + dot(r_lo[...], wy_hi[...]) + dot(r_hi[...], wy_lo[...])
    for z in range(nz):
        h, l = split(t1[z * wide : (z + 1) * wide])
        uv[z] = dot(g_hi, jnp.concatenate([h, l], axis=0)) + dot(g_lo, h)

    def modes(step, carry):
        rows = pl.ds(pl.multiple_of(step * HALF, HALF), HALF)
        u = [uv[z, rows, :] for z in range(nz)]
        v = [None] * nz
        for k in range(PATCH):
            c = None
            for z in range(nz):
                term = basis_s[0, QUARTER + z, k] * u[z]
                c = term if c is None else c + term
            c = c * dinv[k, rows, :]
            for z in range(nz):
                term = basis_s[0, QUARTER + z, k] * c
                v[z] = term if v[z] is None else v[z] + term
        for z in range(nz):
            vv[z, rows, :] = v[z]
        return carry

    lax.fori_loop(0, qx // HALF, modes, 0)
    for z in range(nz):
        h, l = split(vv[z])
        back = dot(b_hi, jnp.concatenate([h, l], axis=0)) + dot(b_lo, h)
        h, l = split(back)
        tb_hi[pl.ds(z * wide, wide), :] = h
        tb_lo[pl.ds(z * wide, wide), :] = l

    total = (
        dot_nt(tb_hi[...], wy_hi[...]) + dot_nt(tb_lo[...], wy_hi[...]) + dot_nt(tb_hi[...], wy_lo[...])
    )

    fetch.wait()
    cells = PATCH * PATCH
    vz = basis[0, pl.ds(QUARTER, nz), :]
    cell_x = iota((wide, cells), 1) // PATCH
    row_k = iota((PATCH, cells), 0)
    for m in range(slots):
        a_m = cut[m] // blocks_y
        spot = (iota((wide, cells), 0) - (HALO - QUARTER) - HALF * a_m) == cell_x
        taken = (dot(r_hi[...], sel[m]) + dot(r_lo[...], sel[m])).reshape(nz, wide, cells)
        patch = jnp.sum(jnp.where(spot[None], taken, 0.0), axis=1)
        zmodes = lax.dot_general(
            vz, patch, (((0,), (0,)), ((), ())), precision=highest, preferred_element_type=f32
        ).astype(bf16)
        dense = jnp.zeros((PATCH, cells), f32)
        for k in range(PATCH):
            dense = jnp.where(row_k == k, dot_nt(zmodes, inv[m, k]), dense)
        corr = jnp.dot(vz, dense, precision=highest, preferred_element_type=f32)
        corr = jnp.where(cut[m] >= 0, corr, 0.0)
        spread = jnp.where(spot[None], corr[:, None, :], 0.0).reshape(nz * wide, cells)
        h, l = split(spread)
        total = total + dot_nt(h, sel[m]) + dot_nt(l, sel[m])

    total = total.reshape(nz, wide, full)
    packed = jnp.zeros((wide, LANES), f32)
    for z in range(nz):
        tot[z] = total[z, :, :ry]
        packed = jnp.where(lane_w // HALF == half // HALF + z, total[z, :, ry:], packed)
    edge[...] = packed

    start_all(copy2)
    wait_recv_all(copy2)

    lows = lane % HALF < QUARTER
    gap = jnp.zeros((rx - 2 * HALO, LANES), f32)
    l2 = left2[...] + jnp.concatenate([corners[0], gap, corners[2]], axis=0)
    r2 = right2[...] + jnp.concatenate([corners[1], gap, corners[3]], axis=0)
    both = jnp.where(lows, r2, l2)
    rim = (lane < QUARTER) | (lane >= ry - QUARTER)
    scale = damping * ext[2 * nz, own, :]
    for z in range(nz):
        moved = pltpu.roll(both, (LANES - QUARTER - half - HALF * z) % LANES, 1)
        t = tot[z, own, :] + jnp.concatenate([up[z], gap, down[z]], axis=0)
        t = t + jnp.where(rim, moved, 0.0)
        out[z] = state[z] + scale * t

    wait_send_all(copy1)
    wait_send_all(copy2)


def on_device(
    sizes, state, load_vector, active, stiff_band, mass_band, eig_basis, eig_values, cut_cols, cut_inverse
):
    nz, rx, ry = state.shape
    slots = cut_cols.shape[-1]
    assert nz == HALF and ry == LANES and rx % PATCH == 0
    inverse = cut_inverse.reshape(cut_inverse.shape[2:])
    wide = rx + 2 * HALO
    full = ry + LANES
    qx, qy = (rx // HALF) * PATCH, (ry // HALF) * PATCH
    cells = PATCH * PATCH
    vmem = pl.BlockSpec(memory_space=pltpu.VMEM)
    smem = pl.BlockSpec(memory_space=pltpu.SMEM)
    V = pltpu.VMEM
    dma = pltpu.SemaphoreType.DMA
    n = len(DIRS)
    return pl.pallas_call(
        functools.partial(kernel, sizes),
        out_shape=jax.ShapeDtypeStruct(state.shape, f32),
        in_specs=[vmem, vmem, vmem, smem, smem, smem, vmem, smem, smem, pl.BlockSpec(memory_space=pl.ANY)],
        out_specs=vmem,
        scratch_shapes=[
            V((2 * nz + 1, wide, ry), f32),
            V((wide, LANES), f32), V((wide, LANES), f32),
            V((rx, LANES), f32), V((rx, LANES), f32),
            V((slots, PATCH, cells, cells), bf16),
            V((full, 2 * full), bf16), V((full, 2 * full), bf16),
            V((full, qy), bf16), V((full, qy), bf16),
            V((slots, full, cells), bf16),
            V((PATCH, qx, qy), f32),
            V((nz * wide, full), bf16), V((nz * wide, full), bf16),
            V((nz, wide, 2 * full), f32),
            V((nz, 4 * wide, full), bf16),
            V((nz * wide, full), bf16), V((nz * wide, full), bf16),
            V((nz, qx, qy), f32), V((nz, qx, qy), f32),
            V((nz * wide, qy), bf16), V((nz * wide, qy), bf16),
            V((nz, wide, ry), f32), V((wide, LANES), f32),
            V((nz, HALO, ry), f32), V((nz, HALO, ry), f32),
            V((rx, LANES), f32), V((rx, LANES), f32),
            V((4, HALO, LANES), f32),
            dma, dma((n,)), dma((n,)), dma((n,)), dma((n,)),
        ],
        compiler_params=pltpu.CompilerParams(
            collective_id=0, has_side_effects=True, vmem_limit_bytes=40 * 1024 * 1024
        ),
    )(
        state, load_vector, active, stiff_band, mass_band, eig_basis, eig_basis, eig_values, cut_cols, inverse
    )


def solution(mesh):
    placed = (
        P(None, "gx", "gy"),
        P(None, "gx", "gy"),
        P("gx", "gy"),
        P(),
        P(),
        P(),
        P(),
        P("gx", "gy", None),
        P("gx", "gy", None, None, None, None),
    )
    sizes = (mesh.shape["gx"], mesh.shape["gy"])
    return jax.shard_map(
        functools.partial(on_device, sizes),
        mesh=mesh, in_specs=placed, out_specs=P(None, "gx", "gy"), check_vma=False,
    )
```

```python
import functools

import jax
import jax.numpy as jnp
from jax import lax
from jax.experimental import pallas as pl
from jax.experimental.pallas import tpu as pltpu
from jax.sharding import PartitionSpec as P

BAND = 4
PATCH = 16
HALF = PATCH // 2
QUARTER = PATCH // 4
HALO = BAND + QUARTER
LANES = 128
MESH = pl.DeviceIdType.MESH
DIRS = [(dx, dy) for dx in (-1, 0, 1) for dy in (-1, 0, 1) if (dx, dy) != (0, 0)]

damping = 0.5
f32 = jnp.float32
bf16 = jnp.bfloat16


def iota(shape, dim):
    return lax.broadcasted_iota(jnp.int32, shape, dim)


def split(v):
    hi = v.astype(bf16)
    return hi, (v - hi.astype(f32)).astype(bf16)


def dot(a, b):
    return jnp.dot(a, b, preferred_element_type=f32)


def dot_nt(a, b):
    return lax.dot_general(a, b, (((1,), (1,)), ((), ())), preferred_element_type=f32)


def band_of(distance, taps):
    out = jnp.zeros(distance.shape, f32)
    for k in range(BAND + 1):
        out = jnp.where(distance == k, taps[k], out)
    return out


def inner_y(c, ry):
    u = (c - ry) & (HALF - 1)
    halo = jnp.where(u < QUARTER, u - QUARTER, ry + u - QUARTER)
    return jnp.where(c < ry, c, jnp.where(c < ry + LANES // 2, -1000, halo))


def outer_y(r, ry):
    u = (r - ry) & (HALF - 1)
    return jnp.where(r < ry, r, jnp.where(r < ry + LANES // 2, u - HALO, ry + u))


def wrap(v, n, reps):
    out = v
    for j in range(1, reps):
        out = out - jnp.where(v >= n * j, n, 0)
    return out


def kernel(
    sizes,
    state_h, load_h, active_h, stiff_h, mass_h, basis_h, values_h, cols_h, inverse_h,
    out,
    state, load, active, stiff, mass, basis_s, basis, values, cols, inv,
    ext, from_left, from_right, pack_left, pack_right,
    yb_hi, yb_lo, wy_hi, wy_lo, sel, dinv,
    zk, zm, sk_hi, sk_lo, sm_hi, sm_lo, r_hi, r_lo, tb_hi, tb_lo, tot, edge,
    up, down, left2, right2, corners,
    in_sem, send1, recv1, send2, recv2,
):
    n_x, n_y = sizes
    nz, rx, ry = state.shape
    wide = rx + 2 * HALO
    slots = inv.shape[0]
    blocks_x, blocks_y = rx // HALF, ry // HALF
    qx, qy = blocks_x * PATCH, blocks_y * PATCH
    full = ry + LANES
    half = LANES // 2
    groups = half // HALF
    me_x, me_y = lax.axis_index("gx"), lax.axis_index("gy")

    def exists(dx, dy):
        ok = None
        for d, me, n in ((dx, me_x, n_x), (dy, me_y, n_y)):
            if d:
                part = (me + d >= 0) & (me + d < n)
                ok = part if ok is None else ok & part
        return ok

    def device(dx, dy):
        return (jnp.clip(me_x + dx, 0, n_x - 1), jnp.clip(me_y + dy, 0, n_y - 1))

    fetches = [
        pltpu.make_async_copy(src, dst, in_sem.at[i])
        for i, (src, dst) in enumerate((
            (state_h, state), (load_h, load), (active_h, active),
            (stiff_h, stiff), (mass_h, mass), (basis_h, basis_s), (basis_h, basis),
            (values_h, values), (cols_h, cols), (inverse_h, inv),
        ))
    ]
    for fetch in fetches:
        fetch.start()

    own = pl.ds(HALO, rx)
    zeros = jnp.zeros((2 * nz + 1, HALO, ry), f32)
    ext[:, pl.ds(0, HALO), :] = zeros
    ext[:, pl.ds(HALO + rx, HALO), :] = zeros
    for ref in (from_left, from_right, up, down, left2, right2, corners):
        ref[...] = jnp.zeros(ref.shape, f32)

    barrier = pltpu.get_barrier_semaphore()
    count = jnp.int32(0)
    for d in DIRS:
        ok = exists(*d)
        count = count + ok.astype(jnp.int32)

        @pl.when(ok)
        def _(d=d):
            pl.semaphore_signal(barrier, inc=1, device_id=device(*d), device_id_type=MESH)

    for fetch in fetches[:3]:
        fetch.wait()
    for z in range(nz):
        ext[z, own, :] = state[z]
        ext[nz + z, own, :] = load[z].astype(f32)
    ext[2 * nz, own, :] = active[...].astype(f32)

    lane = iota((rx, LANES), 1)
    group = (lane & (half - 1)) >> 3
    high = lane >= half
    lows = (lane & (HALF - 1)) < QUARTER
    to_right = jnp.zeros((rx, LANES), f32)
    to_left = jnp.zeros((rx, LANES), f32)
    act = ext[2 * nz, own, :]
    for z in range(nz):
        s = ext[z, own, :]
        l = pltpu.roll(ext[nz + z, own, :], (half + QUARTER + HALF * z) % LANES, 1)
        mine = group == z
        first = mine & high & lows
        second = mine & high & ~lows
        to_right = jnp.where(mine & ~high, pltpu.roll(s, (HALF + HALF * z) % LANES, 1), to_right)
        to_right = jnp.where(first, l, to_right)
        to_right = jnp.where(second, pltpu.roll(act, (half + HALF + HALF * z) % LANES, 1), to_right)
        to_left = jnp.where(mine & ~high, pltpu.roll(s, HALF * z, 1) if z else s, to_left)
        to_left = jnp.where(second, l, to_left)
        to_left = jnp.where(first, pltpu.roll(act, (half + HALF * z) % LANES, 1), to_left)
    pack_right[...] = to_right
    pack_left[...] = to_left

    def copy1(i):
        dx, dy = DIRS[i]
        if dy == 0:
            src = ext.at[:, pl.ds(rx if dx > 0 else HALO, HALO), :]
            dst = ext.at[:, pl.ds(0 if dx > 0 else HALO + rx, HALO), :]
        else:
            pack = pack_right if dy > 0 else pack_left
            land = from_left if dy > 0 else from_right
            if dx == 0:
                src, dst = pack, land.at[pl.ds(HALO, rx), :]
            else:
                src = pack.at[pl.ds(rx - HALO if dx > 0 else 0, HALO), :]
                dst = land.at[pl.ds(0 if dx > 0 else HALO + rx, HALO), :]
        return pltpu.make_async_remote_copy(
            src_ref=src, dst_ref=dst, send_sem=send1.at[i], recv_sem=recv1.at[i],
            device_id=device(dx, dy), device_id_type=MESH,
        )

    def copy2(i):
        dx, dy = DIRS[i]
        if dy == 0:
            src = tot.at[:, pl.ds(HALO + rx if dx > 0 else 0, HALO), :]
            dst = up if dx > 0 else down
        elif dx == 0:
            src = edge.at[pl.ds(HALO, rx), :]
            dst = left2 if dy > 0 else right2
        else:
            src = edge.at[pl.ds(HALO + rx if dx > 0 else 0, HALO), :]
            dst = corners.at[(dx < 0) * 2 + (dy < 0)]
        return pltpu.make_async_remote_copy(
            src_ref=src, dst_ref=dst, send_sem=send2.at[i], recv_sem=recv2.at[i],
            device_id=device(dx, dy), device_id_type=MESH,
        )

    def start_all(copy):
        for i, d in enumerate(DIRS):
            @pl.when(exists(*d))
            def _(i=i):
                copy(i).start()

    def wait_recv_all(copy):
        for i, (dx, dy) in enumerate(DIRS):
            @pl.when(exists(-dx, -dy))
            def _(i=i):
                copy(i).wait_recv()

    def wait_send_all(copy):
        for i, d in enumerate(DIRS):
            @pl.when(exists(*d))
            def _(i=i):
                copy(i).wait_send()

    pl.semaphore_wait(barrier, count)
    start_all(copy1)

    for fetch in fetches[3:9]:
        fetch.wait()
    distance = jnp.abs(outer_y(iota((full, 1), 0), ry) - inner_y(iota((1, full), 1), ry))
    for j, taps in enumerate((mass, stiff)):
        h, l = split(band_of(distance, [taps[2, k] for k in range(BAND + 1)]))
        yb_hi[:, pl.ds(j * full, full)] = h
        yb_lo[:, pl.ds(j * full, full)] = l

    highest = lax.Precision.HIGHEST
    tile_y = jnp.dot(
        basis[2], (iota((PATCH, qy), 0) == (iota((PATCH, qy), 1) & (PATCH - 1))).astype(f32),
        precision=highest, preferred_element_type=f32,
    )
    place = inner_y(iota((full, 1), 0), ry) + QUARTER - HALF * (iota((1, qy), 1) >> 4)
    wy = jnp.zeros((full, qy), f32)
    for t in range(PATCH):
        wy = jnp.where(place == t, tile_y[t : t + 1, :], wy)
    h, l = split(wy)
    wy_hi[...] = h
    wy_lo[...] = l

    def wx_of(shape, reps_r, reps_c):
        r, c = iota((shape[0], 1), 0), iota((1, shape[1]), 1)
        t = wrap(r, wide, reps_r) - (HALO - QUARTER) - HALF * (wrap(c, qx, reps_c) >> 4)
        t = jnp.where((r < wide * reps_r) & (c < qx * reps_c), t, -1)
        tile = jnp.dot(
            basis[1], (iota((PATCH, shape[1]), 0) == (iota((PATCH, shape[1]), 1) & (PATCH - 1))).astype(f32),
            precision=highest, preferred_element_type=f32,
        )
        w = jnp.zeros(shape, f32)
        for k in range(PATCH):
            w = jnp.where(t == k, tile[k : k + 1, :], w)
        return w

    pad_r = -(-2 * wide // LANES) * LANES
    pad_c = -(-qx // LANES) * LANES
    gx2 = wx_of((pad_r, pad_c), 2, 1).T[:qx, : 2 * wide]
    g_hi, g_lo = split(gx2)
    g_lo = g_lo[:, :wide]
    b_hi, b_lo = split(wx_of((wide, 2 * qx), 1, 2))
    b_lo = b_lo[:, :qx]

    c = iota((1, 4 * wide), 1)
    dist_x = jnp.abs(iota((wide, 1), 0) - wrap(c, wide, 4))
    bx = jnp.where(
        (c < wide) | ((c >= 2 * wide) & (c < 3 * wide)),
        band_of(dist_x, [mass[1, k] for k in range(BAND + 1)]),
        band_of(dist_x, [stiff[1, k] for k in range(BAND + 1)]),
    )
    bx_hi, bx_lo = split(bx)
    bx_lo = bx_lo[:, : 2 * wide]

    cells = PATCH * PATCH
    cut = [cols[0, 0, m] for m in range(slots)]
    cut_a = [lax.div(jnp.maximum(v, 0), jnp.int32(blocks_y)) for v in cut]
    cut_b = [lax.rem(jnp.maximum(v, 0), jnp.int32(blocks_y)) for v in cut]
    y_in = inner_y(iota((full, 1), 0), ry)
    y_to = iota((1, cells), 1) & (PATCH - 1)
    for m in range(slots):
        sel[m] = jnp.where(y_in + QUARTER - HALF * cut_b[m] == y_to, 1.0, 0.0).astype(bf16)

    def pick(shape, dim, row):
        index = iota(shape, dim) & (PATCH - 1)
        v = jnp.zeros(shape, f32)
        for k in range(PATCH):
            v = jnp.where(index == k, values[row, k], v)
        return v

    lam = pick((qx, 1), 0, 1) + pick((1, qy), 1, 2)
    column = (iota((qx, 1), 0) >> 4) * blocks_y + (iota((1, qy), 1) >> 4)
    keep = jnp.ones((qx, qy), f32)
    for m in range(slots):
        keep = jnp.where(column == cut[m], 0.0, keep)
    for k in range(PATCH):
        dinv[k] = keep / (values[0, k] + lam)

    lane1 = iota((1, LANES), 1)
    group1 = (lane1 & (half - 1)) >> 3
    far = [jnp.abs(group1 - z) for z in range(nz)]
    k_vec = [band_of(far[z], [stiff[0, k] for k in range(BAND + 1)]) for z in range(nz)]
    m_vec = [band_of(far[z], [mass[0, k] for k in range(BAND + 1)]) for z in range(nz)]
    v_vec = []
    for k in range(PATCH):
        v = jnp.zeros((1, LANES), f32)
        for z in range(nz):
            v = jnp.where((group1 == z) & (lane1 >= half), basis_s[0, QUARTER + z, k], v)
        v_vec.append(v)

    def mix_z(start, count):
        for r in range(start, start + count, HALF):
            rows = pl.ds(r, HALF)
            s = [ext[z, rows, :] for z in range(nz)]
            for z in range(nz):
                p = q = None
                for w in range(nz):
                    k = abs(z - w)
                    if k > BAND:
                        continue
                    a, b = stiff[0, k] * s[w], mass[0, k] * s[w]
                    p = a if p is None else p + a
                    q = b if q is None else q + b
                zk[z, rows, :] = p
                zm[z, rows, :] = q

    mix_z(HALO, rx)
    wait_recv_all(copy1)
    mix_z(0, HALO)
    mix_z(HALO + rx, HALO)

    lane_w = iota((wide, LANES), 1)
    group_w = (lane_w & (half - 1)) >> 3
    halo_l, halo_r = from_left[...], from_right[...]
    comb = jnp.where(lane_w < half, halo_l, pltpu.roll(halo_r, half, 1))
    low = (lane_w & (HALF - 1)) < QUARTER
    load_t = jnp.where(low, halo_l, halo_r)
    act_t = jnp.where(low, pltpu.roll(halo_l, LANES - QUARTER, 1), pltpu.roll(halo_r, QUARTER, 1))
    act_t = jnp.where(lane_w >= half, act_t, 0.0)
    act_w = ext[2 * nz]
    for z in range(nz):
        rows = pl.ds(z * wide, wide)
        for hi, lo, mixed, vec in ((sk_hi, sk_lo, zk, k_vec), (sm_hi, sm_lo, zm, m_vec)):
            h, l = split(mixed[z])
            hi[rows, pl.ds(0, ry)] = h
            lo[rows, pl.ds(0, ry)] = l
            h, l = split(comb * vec[z])
            hi[rows, pl.ds(ry, LANES)] = h
            lo[rows, pl.ds(ry, LANES)] = l

    def times(hi, lo, w_hi, w_lo):
        return dot(hi, w_hi) + dot(lo, w_hi) + dot(hi, w_lo)

    ym = times(sm_hi[...], sm_lo[...], yb_hi[...], yb_lo[...])
    yp = ym[:, full:] + times(sk_hi[...], sk_lo[...], yb_hi[:, pl.ds(0, full)], yb_lo[:, pl.ds(0, full)])

    r0 = []
    r1 = jnp.zeros((wide, LANES), f32)
    for z in range(nz):
        p_hi, p_lo = split(yp[z * wide : (z + 1) * wide])
        q_hi, q_lo = split(ym[z * wide : (z + 1) * wide, :full])
        applied = dot(bx_hi, jnp.concatenate([p_hi, q_hi, p_lo, q_lo], axis=0))
        applied = applied + dot(bx_lo, jnp.concatenate([p_hi, q_hi], axis=0))
        r0.append(act_w * (ext[nz + z] - applied[:, :ry]))
        r1 = jnp.where(group_w == z, applied[:, ry:], r1)
    r1 = act_t * (load_t - r1)

    for k in range(PATCH):
        rows = pl.ds(k * wide, wide)
        v = None
        for z in range(nz):
            term = basis_s[0, QUARTER + z, k] * r0[z]
            v = term if v is None else v + term
        h, l = split(v)
        r_hi[rows, pl.ds(0, ry)] = h
        r_lo[rows, pl.ds(0, ry)] = l
        h, l = split(r1 * v_vec[k])
        r_hi[rows, pl.ds(ry, LANES)] = h
        r_lo[rows, pl.ds(ry, LANES)] = l

    fetches[9].wait()
    vz = basis[0, pl.ds(QUARTER, nz), :]
    cell_x = iota((1, cells), 1) >> 4
    row_k = iota((PATCH, cells), 0)
    spread = []
    for m in range(slots):
        spot = (iota((wide, 1), 0) - (HALO - QUARTER) - HALF * cut_a[m]) == cell_x
        taken = (dot(r_hi[...], sel[m]) + dot(r_lo[...], sel[m])).reshape(PATCH, wide, cells)
        zmodes = jnp.sum(jnp.where(spot[None], taken, 0.0), axis=1).astype(bf16)
        dense = jnp.zeros((PATCH, cells), f32)
        for k in range(PATCH):
            dense = jnp.where(row_k == k, dot_nt(zmodes, inv[m, k]), dense)
        corr = jnp.dot(vz, dense, precision=highest, preferred_element_type=f32)
        corr = jnp.where(cut[m] >= 0, corr, 0.0)
        spread.append(jnp.where(spot[None], corr[:, None, :], 0.0).reshape(nz * wide, cells))

    t1 = times(r_hi[...], r_lo[...], wy_hi[...], wy_lo[...])
    for k in range(PATCH):
        h, l = split(t1[k * wide : (k + 1) * wide])
        u = (dot(g_hi, jnp.concatenate([h, l], axis=0)) + dot(g_lo, h)) * dinv[k]
        h, l = split(u)
        back = dot(b_hi, jnp.concatenate([h, l], axis=0)) + dot(b_lo, h)
        h, l = split(back)
        tb_hi[pl.ds(k * wide, wide), :] = h
        tb_lo[pl.ds(k * wide, wide), :] = l
    fast = (
        dot_nt(tb_hi[...], wy_hi[...]) + dot_nt(tb_lo[...], wy_hi[...]) + dot_nt(tb_hi[...], wy_lo[...])
    ).reshape(PATCH, wide, full)

    cut_total = None
    for m in range(slots):
        h, l = split(spread[m])
        term = dot_nt(h, sel[m]) + dot_nt(l, sel[m])
        cut_total = term if cut_total is None else cut_total + term
    cut_total = cut_total.reshape(nz, wide, full)

    packed = jnp.zeros((wide, LANES), f32)
    for z in range(nz):
        packed = jnp.where(group_w == z, cut_total[z, :, ry:], packed)
    for k in range(PATCH):
        packed = packed + v_vec[k] * fast[k, :, ry:]
    edge[...] = packed
    for z in range(nz):
        t = cut_total[z, :, :ry]
        for k in range(PATCH):
            t = t + basis_s[0, QUARTER + z, k] * fast[k, :, :ry]
        tot[z] = t

    start_all(copy2)
    wait_recv_all(copy2)

    gap = jnp.zeros((rx - 2 * HALO, LANES), f32)
    l2 = left2[...] + jnp.concatenate([corners[0], gap, corners[2]], axis=0)
    r2 = right2[...] + jnp.concatenate([corners[1], gap, corners[3]], axis=0)
    both = jnp.where(lows, r2, l2)
    rim = (lane < QUARTER) | (lane >= ry - QUARTER)
    scale = damping * ext[2 * nz, own, :]
    for z in range(nz):
        moved = pltpu.roll(both, (LANES - QUARTER - half - HALF * z) % LANES, 1)
        t = tot[z, own, :] + jnp.concatenate([up[z], gap, down[z]], axis=0)
        t = t + jnp.where(rim, moved, 0.0)
        out[z] = state[z] + scale * t

    wait_send_all(copy1)
    wait_send_all(copy2)


def on_device(
    sizes, state, load_vector, active, stiff_band, mass_band, eig_basis, eig_values, cut_cols, cut_inverse
):
    nz, rx, ry = state.shape
    slots = cut_cols.shape[-1]
    assert nz == HALF and ry == LANES and rx % PATCH == 0
    inverse = cut_inverse.reshape(cut_inverse.shape[2:])
    wide = rx + 2 * HALO
    full = ry + LANES
    qx, qy = (rx // HALF) * PATCH, (ry // HALF) * PATCH
    cells = PATCH * PATCH
    anyspace = pl.BlockSpec(memory_space=pl.ANY)
    V, S = pltpu.VMEM, pltpu.SMEM
    dma = pltpu.SemaphoreType.DMA
    n = len(DIRS)
    return pl.pallas_call(
        functools.partial(kernel, sizes),
        out_shape=jax.ShapeDtypeStruct(state.shape, f32),
        in_specs=[anyspace] * 9,
        out_specs=pl.BlockSpec(memory_space=pltpu.VMEM),
        scratch_shapes=[
            V(state.shape, f32), V(load_vector.shape, load_vector.dtype), V(active.shape, active.dtype),
            S(stiff_band.shape, f32), S(mass_band.shape, f32), S(eig_basis.shape, f32),
            V(eig_basis.shape, f32), S(eig_values.shape, f32), S(cut_cols.shape, cut_cols.dtype),
            V((slots, PATCH, cells, cells), bf16),
            V((2 * nz + 1, wide, ry), f32),
            V((wide, LANES), f32), V((wide, LANES), f32),
            V((rx, LANES), f32), V((rx, LANES), f32),
            V((full, 2 * full), bf16), V((full, 2 * full), bf16),
            V((full, qy), bf16), V((full, qy), bf16),
            V((slots, full, cells), bf16),
            V((PATCH, qx, qy), f32),
            V((nz, wide, ry), f32), V((nz, wide, ry), f32),
            V((nz * wide, full), bf16), V((nz * wide, full), bf16),
            V((nz * wide, full), bf16), V((nz * wide, full), bf16),
            V((PATCH * wide, full), bf16), V((PATCH * wide, full), bf16),
            V((PATCH * wide, qy), bf16), V((PATCH * wide, qy), bf16),
            V((nz, wide, ry), f32), V((wide, LANES), f32),
            V((nz, HALO, ry), f32), V((nz, HALO, ry), f32),
            V((rx, LANES), f32), V((rx, LANES), f32),
            V((4, HALO, LANES), f32),
            dma((10,)), dma((n,)), dma((n,)), dma((n,)), dma((n,)),
        ],
        compiler_params=pltpu.CompilerParams(
            collective_id=0, has_side_effects=True, vmem_limit_bytes=56 * 1024 * 1024
        ),
    )(state, load_vector, active, stiff_band, mass_band, eig_basis, eig_values, cut_cols, inverse)


def solution(mesh):
    placed = (
        P(None, "gx", "gy"),
        P(None, "gx", "gy"),
        P("gx", "gy"),
        P(),
        P(),
        P(),
        P(),
        P("gx", "gy", None),
        P("gx", "gy", None, None, None, None),
    )
    sizes = (mesh.shape["gx"], mesh.shape["gy"])
    return jax.shard_map(
        functools.partial(on_device, sizes),
        mesh=mesh, in_specs=placed, out_specs=P(None, "gx", "gy"), check_vma=False,
    )
```

```python
import functools

import jax
import jax.numpy as jnp
from jax import lax
from jax.experimental import pallas as pl
from jax.experimental.pallas import tpu as pltpu
from jax.sharding import PartitionSpec as P

BAND = 4
PATCH = 16
HALF = PATCH // 2
QUARTER = PATCH // 4
HALO = BAND + QUARTER
LANES = 128
MESH = pl.DeviceIdType.MESH
DIRS = [(1, 0), (-1, 0), (1, 1), (1, -1), (-1, 1), (-1, -1), (0, 1), (0, -1)]

damping = 0.5
f32 = jnp.float32
bf16 = jnp.bfloat16


def iota(shape, dim):
    return lax.broadcasted_iota(jnp.int32, shape, dim)


def split(v):
    hi = v.astype(bf16)
    return hi, (v - hi.astype(f32)).astype(bf16)


def dot(a, b):
    return jnp.dot(a, b, preferred_element_type=f32)


def dot_nt(a, b):
    return lax.dot_general(a, b, (((1,), (1,)), ((), ())), preferred_element_type=f32)


def band_of(distance, taps):
    out = jnp.zeros(distance.shape, f32)
    for k in range(BAND + 1):
        out = jnp.where(distance == k, taps[k], out)
    return out


def inner_y(c, ry):
    u = (c - ry) & (HALF - 1)
    halo = jnp.where(u < QUARTER, u - QUARTER, ry + u - QUARTER)
    return jnp.where(c < ry, c, jnp.where(c < ry + LANES // 2, -1000, halo))


def outer_y(r, ry):
    u = (r - ry) & (HALF - 1)
    return jnp.where(r < ry, r, jnp.where(r < ry + LANES // 2, u - HALO, ry + u))


def wrap(v, n, reps):
    out = v
    for j in range(1, reps):
        out = out - jnp.where(v >= n * j, n, 0)
    return out


def kernel(
    sizes,
    state_h, load_h, active_h, stiff_h, mass_h, basis_h, values_h, cols_h, inverse_h,
    out,
    state, load, active, stiff, mass, basis_s, basis, values, cols, inv,
    ext, lf, from_left, from_right, pack_left, pack_right,
    yb, wy3, wyt3, sel, dinv,
    zk, zm, sk3, sm3, r3, tb3, tot, edge,
    rim_x, up, down, left2, right2, corners,
    in_sem, send1, recv1, send2, recv2,
):
    n_x, n_y = sizes
    nz, rx, ry = state.shape
    wide = rx + 2 * HALO
    slots = inv.shape[0]
    blocks_x, blocks_y = rx // HALF, ry // HALF
    qx, qy = blocks_x * PATCH, blocks_y * PATCH
    full = ry + LANES
    half = LANES // 2
    groups = half // HALF
    me_x, me_y = lax.axis_index("gx"), lax.axis_index("gy")

    def exists(dx, dy):
        ok = None
        for d, me, n in ((dx, me_x, n_x), (dy, me_y, n_y)):
            if d:
                part = (me + d >= 0) & (me + d < n)
                ok = part if ok is None else ok & part
        return ok

    def device(dx, dy):
        return (jnp.clip(me_x + dx, 0, n_x - 1), jnp.clip(me_y + dy, 0, n_y - 1))

    fetches = [
        pltpu.make_async_copy(src, dst, in_sem.at[i])
        for i, (src, dst) in enumerate((
            (state_h, state), (load_h, load), (active_h, active),
            (stiff_h, stiff), (mass_h, mass), (basis_h, basis_s), (basis_h, basis),
            (values_h, values), (cols_h, cols), (inverse_h, inv),
        ))
    ]
    for fetch in fetches:
        fetch.start()

    own = pl.ds(HALO, rx)
    planes = nz + 1 + nz // 2
    zeros = jnp.zeros((planes, HALO, ry), f32)
    ext[:, pl.ds(0, HALO), :] = zeros
    ext[:, pl.ds(HALO + rx, HALO), :] = zeros
    for ref in (from_left, from_right, up, down, left2, right2, corners):
        ref[...] = jnp.zeros(ref.shape, f32)

    barrier = pltpu.get_barrier_semaphore()
    count = jnp.int32(0)
    for d in DIRS:
        ok = exists(*d)
        count = count + ok.astype(jnp.int32)

        @pl.when(ok)
        def _(d=d):
            pl.semaphore_signal(barrier, inc=1, device_id=device(*d), device_id_type=MESH)

    for fetch in fetches[:3]:
        fetch.wait()
    for z in range(nz):
        ext[z, own, :] = state[z]
        lf[z, own, :] = load[z].astype(f32)
    ext[nz, own, :] = active[...].astype(f32)
    top = iota((HALO, ry), 0) < QUARTER
    for j in range(nz // 2):
        for r, natural in ((HALO, top), (rx, ~top)):
            odd = pltpu.roll(lf[2 * j + 1, pl.ds(r, HALO), :], QUARTER, 0)
            ext[nz + 1 + j, pl.ds(r, HALO), :] = jnp.where(natural, lf[2 * j, pl.ds(r, HALO), :], odd)

    lane = iota((rx, LANES), 1)
    group = (lane & (half - 1)) >> 3
    high = lane >= half
    lows = (lane & (HALF - 1)) < QUARTER
    to_right = jnp.zeros((rx, LANES), f32)
    to_left = jnp.zeros((rx, LANES), f32)
    act = ext[nz, own, :]
    for z in range(nz):
        s = ext[z, own, :]
        l = pltpu.roll(lf[z, own, :], (half + QUARTER + HALF * z) % LANES, 1)
        mine = group == z
        first = mine & high & lows
        second = mine & high & ~lows
        to_right = jnp.where(mine & ~high, pltpu.roll(s, (HALF + HALF * z) % LANES, 1), to_right)
        to_right = jnp.where(first, l, to_right)
        to_right = jnp.where(second, pltpu.roll(act, (half + HALF + HALF * z) % LANES, 1), to_right)
        to_left = jnp.where(mine & ~high, pltpu.roll(s, HALF * z, 1) if z else s, to_left)
        to_left = jnp.where(second, l, to_left)
        to_left = jnp.where(first, pltpu.roll(act, (half + HALF * z) % LANES, 1), to_left)
    pack_right[...] = to_right
    pack_left[...] = to_left

    def copy1(i):
        dx, dy = DIRS[i]
        if dy == 0:
            src = ext.at[:, pl.ds(rx if dx > 0 else HALO, HALO), :]
            dst = ext.at[:, pl.ds(0 if dx > 0 else HALO + rx, HALO), :]
        else:
            pack = pack_right if dy > 0 else pack_left
            land = from_left if dy > 0 else from_right
            if dx == 0:
                src, dst = pack, land.at[pl.ds(HALO, rx), :]
            else:
                src = pack.at[pl.ds(rx - HALO if dx > 0 else 0, HALO), :]
                dst = land.at[pl.ds(0 if dx > 0 else HALO + rx, HALO), :]
        return pltpu.make_async_remote_copy(
            src_ref=src, dst_ref=dst, send_sem=send1.at[i], recv_sem=recv1.at[i],
            device_id=device(dx, dy), device_id_type=MESH,
        )

    def copy2(i):
        dx, dy = DIRS[i]
        if dy == 0:
            src = rim_x.at[0 if dx > 0 else 1]
            dst = up if dx > 0 else down
        elif dx == 0:
            src = edge.at[pl.ds(HALO, rx), :]
            dst = left2 if dy > 0 else right2
        else:
            src = edge.at[pl.ds(HALO + rx if dx > 0 else 0, HALO), :]
            dst = corners.at[(dx < 0) * 2 + (dy < 0)]
        return pltpu.make_async_remote_copy(
            src_ref=src, dst_ref=dst, send_sem=send2.at[i], recv_sem=recv2.at[i],
            device_id=device(dx, dy), device_id_type=MESH,
        )

    def start_all(copy):
        for i, d in enumerate(DIRS):
            @pl.when(exists(*d))
            def _(i=i):
                copy(i).start()

    def wait_recv_all(copy):
        for i, (dx, dy) in enumerate(DIRS):
            @pl.when(exists(-dx, -dy))
            def _(i=i):
                copy(i).wait_recv()

    def wait_send_all(copy):
        for i, d in enumerate(DIRS):
            @pl.when(exists(*d))
            def _(i=i):
                copy(i).wait_send()

    pl.semaphore_wait(barrier, count)
    start_all(copy1)

    for fetch in fetches[3:9]:
        fetch.wait()
    distance = jnp.abs(outer_y(iota((full, 1), 0), ry) - inner_y(iota((1, full), 1), ry))
    for j, taps in enumerate((mass, stiff)):
        h, l = split(band_of(distance, [taps[2, k] for k in range(BAND + 1)]))
        for i, part in enumerate((h, h, l)):
            yb[pl.ds(i * full, full), pl.ds(j * full, full)] = part

    highest = lax.Precision.HIGHEST
    tile_y = jnp.dot(
        basis[2], (iota((PATCH, qy), 0) == (iota((PATCH, qy), 1) & (PATCH - 1))).astype(f32),
        precision=highest, preferred_element_type=f32,
    )
    place = inner_y(iota((full, 1), 0), ry) + QUARTER - HALF * (iota((1, qy), 1) >> 4)
    wy = jnp.zeros((full, qy), f32)
    for t in range(PATCH):
        wy = jnp.where(place == t, tile_y[t : t + 1, :], wy)
    h, l = split(wy)
    for i, part in enumerate((h, h, l)):
        wy3[pl.ds(i * full, full), :] = part
        wyt3[:, pl.ds(i * qy, qy)] = part

    def wx_of(shape, reps_r, reps_c):
        r, c = iota((shape[0], 1), 0), iota((1, shape[1]), 1)
        t = wrap(r, wide, reps_r) - (HALO - QUARTER) - HALF * (wrap(c, qx, reps_c) >> 4)
        t = jnp.where((r < wide * reps_r) & (c < qx * reps_c), t, -1)
        tile = jnp.dot(
            basis[1], (iota((PATCH, shape[1]), 0) == (iota((PATCH, shape[1]), 1) & (PATCH - 1))).astype(f32),
            precision=highest, preferred_element_type=f32,
        )
        w = jnp.zeros(shape, f32)
        for k in range(PATCH):
            w = jnp.where(t == k, tile[k : k + 1, :], w)
        return w

    pad_r = -(-2 * wide // LANES) * LANES
    pad_c = -(-qx // LANES) * LANES
    gx2 = wx_of((pad_r, pad_c), 2, 1).T[:qx, : 2 * wide]
    g_hi, g_lo = split(gx2)
    g_lo = g_lo[:, :wide]
    b_hi, b_lo = split(wx_of((wide, 2 * qx), 1, 2))
    b_lo = b_lo[:, :qx]

    c = iota((1, 4 * wide), 1)
    dist_x = jnp.abs(iota((wide, 1), 0) - wrap(c, wide, 4))
    bx = jnp.where(
        (c < wide) | ((c >= 2 * wide) & (c < 3 * wide)),
        band_of(dist_x, [mass[1, k] for k in range(BAND + 1)]),
        band_of(dist_x, [stiff[1, k] for k in range(BAND + 1)]),
    )
    bx_hi, bx_lo = split(bx)
    bx_lo = bx_lo[:, : 2 * wide]

    cells = PATCH * PATCH
    cut = [cols[0, 0, m] for m in range(slots)]
    cut_a = [lax.div(jnp.maximum(v, 0), jnp.int32(blocks_y)) for v in cut]
    cut_b = [lax.rem(jnp.maximum(v, 0), jnp.int32(blocks_y)) for v in cut]
    y_in = inner_y(iota((full, 1), 0), ry)
    y_to = iota((1, cells), 1) & (PATCH - 1)
    for m in range(slots):
        one_hot = jnp.where(y_in + QUARTER - HALF * cut_b[m] == y_to, 1.0, 0.0).astype(bf16)
        sel[m, pl.ds(0, full), :] = one_hot
        sel[m, pl.ds(full, full), :] = one_hot

    def pick(shape, dim, row):
        index = iota(shape, dim) & (PATCH - 1)
        v = jnp.zeros(shape, f32)
        for k in range(PATCH):
            v = jnp.where(index == k, values[row, k], v)
        return v

    lam = pick((qx, 1), 0, 1) + pick((1, qy), 1, 2)
    column = (iota((qx, 1), 0) >> 4) * blocks_y + (iota((1, qy), 1) >> 4)
    keep = jnp.ones((qx, qy), f32)
    for m in range(slots):
        keep = jnp.where(column == cut[m], 0.0, keep)
    for k in range(PATCH):
        dinv[k] = keep / (values[0, k] + lam)

    lane1 = iota((1, LANES), 1)
    group1 = (lane1 & (half - 1)) >> 3
    far = [jnp.abs(group1 - z) for z in range(nz)]
    k_vec = [band_of(far[z], [stiff[0, k] for k in range(BAND + 1)]) for z in range(nz)]
    m_vec = [band_of(far[z], [mass[0, k] for k in range(BAND + 1)]) for z in range(nz)]
    v_vec = []
    for k in range(PATCH):
        v = jnp.zeros((1, LANES), f32)
        for z in range(nz):
            v = jnp.where((group1 == z) & (lane1 >= half), basis_s[0, QUARTER + z, k], v)
        v_vec.append(v)

    def put3(ref, rows, start, width, v):
        h, l = split(v)
        for i, part in enumerate((h, l, h)):
            ref[rows, pl.ds(i * width + start, v.shape[1])] = part

    def mix_z(start, count):
        for r in range(start, start + count, HALF):
            rows = pl.ds(r, HALF)
            s = [ext[z, rows, :] for z in range(nz)]
            for z in range(nz):
                p = q = None
                for w in range(nz):
                    k = abs(z - w)
                    if k > BAND:
                        continue
                    a, b = stiff[0, k] * s[w], mass[0, k] * s[w]
                    p = a if p is None else p + a
                    q = b if q is None else q + b
                zk[z, rows, :] = p
                zm[z, rows, :] = q

    mix_z(HALO, rx)
    fetches[9].wait()
    wait_recv_all(copy1)
    mix_z(0, HALO)
    mix_z(HALO + rx, HALO)

    lane_w = iota((wide, LANES), 1)
    group_w = (lane_w & (half - 1)) >> 3
    halo_l, halo_r = from_left[...], from_right[...]
    comb = jnp.where(lane_w < half, halo_l, pltpu.roll(halo_r, half, 1))
    low = (lane_w & (HALF - 1)) < QUARTER
    load_t = jnp.where(low, halo_l, halo_r)
    act_t = jnp.where(low, pltpu.roll(halo_l, LANES - QUARTER, 1), pltpu.roll(halo_r, QUARTER, 1))
    act_t = jnp.where(lane_w >= half, act_t, 0.0)
    act_w = ext[nz]
    for z in range(nz):
        for r in (0, HALO + rx):
            tile = ext[nz + 1 + z // 2, pl.ds(r, HALO), :]
            lf[z, pl.ds(r, HALO), :] = pltpu.roll(tile, QUARTER, 0) if z % 2 else tile
    for z in range(nz):
        rows = pl.ds(z * wide, wide)
        for s3, mixed, vec in ((sk3, zk, k_vec), (sm3, zm, m_vec)):
            put3(s3, rows, 0, full, mixed[z])
            put3(s3, rows, ry, full, comb * vec[z])

    ym = dot(sm3[...], yb[...])
    yp = ym[:, full:] + dot(sk3[...], yb[:, pl.ds(0, full)])

    r0 = []
    r1 = jnp.zeros((wide, LANES), f32)
    for z in range(nz):
        p_hi, p_lo = split(yp[z * wide : (z + 1) * wide])
        q_hi, q_lo = split(ym[z * wide : (z + 1) * wide, :full])
        applied = dot(bx_hi, jnp.concatenate([p_hi, q_hi, p_lo, q_lo], axis=0))
        applied = applied + dot(bx_lo, jnp.concatenate([p_hi, q_hi], axis=0))
        r0.append(act_w * (lf[z] - applied[:, :ry]))
        r1 = jnp.where(group_w == z, applied[:, ry:], r1)
    r1 = act_t * (load_t - r1)

    for k in range(PATCH):
        rows = pl.ds(k * wide, wide)
        v = None
        for z in range(nz):
            term = basis_s[0, QUARTER + z, k] * r0[z]
            v = term if v is None else v + term
        put3(r3, rows, 0, full, v)
        put3(r3, rows, ry, full, r1 * v_vec[k])

    vz = basis[0, pl.ds(QUARTER, nz), :]
    cell_x = iota((1, cells), 1) >> 4
    row_k = iota((PATCH, cells), 0)
    spread = []
    for m in range(slots):
        spot = (iota((wide, 1), 0) - (HALO - QUARTER) - HALF * cut_a[m]) == cell_x
        taken = dot(r3[:, pl.ds(0, 2 * full)], sel[m]).reshape(PATCH, wide, cells)
        zmodes = jnp.sum(jnp.where(spot[None], taken, 0.0), axis=1).astype(bf16)
        dense = jnp.zeros((PATCH, cells), f32)
        for k in range(PATCH):
            dense = jnp.where(row_k == k, dot_nt(zmodes, inv[m, k]), dense)
        corr = jnp.dot(vz, dense, precision=highest, preferred_element_type=f32)
        corr = jnp.where(cut[m] >= 0, corr, 0.0)
        spread.append(jnp.where(spot[None], corr[:, None, :], 0.0).reshape(nz * wide, cells))

    t1 = dot(r3[...], wy3[...])
    for k in range(PATCH):
        h, l = split(t1[k * wide : (k + 1) * wide])
        u = (dot(g_hi, jnp.concatenate([h, l], axis=0)) + dot(g_lo, h)) * dinv[k]
        h, l = split(u)
        back = dot(b_hi, jnp.concatenate([h, l], axis=0)) + dot(b_lo, h)
        put3(tb3, pl.ds(k * wide, wide), 0, qy, back)
    fast = dot_nt(tb3[...], wyt3[...]).reshape(PATCH, wide, full)

    cut_total = None
    for m in range(slots):
        h, l = split(spread[m])
        term = dot_nt(h, sel[m, pl.ds(0, full), :]) + dot_nt(l, sel[m, pl.ds(0, full), :])
        cut_total = term if cut_total is None else cut_total + term
    cut_total = cut_total.reshape(nz, wide, full)

    packed = jnp.zeros((wide, LANES), f32)
    for z in range(nz):
        packed = jnp.where(group_w == z, cut_total[z, :, ry:], packed)
    for k in range(PATCH):
        packed = packed + v_vec[k] * fast[k, :, ry:]
    edge[...] = packed
    for z in range(nz):
        t = cut_total[z, :, :ry]
        for k in range(PATCH):
            t = t + basis_s[0, QUARTER + z, k] * fast[k, :, :ry]
        tot[z] = t
    for j in range(nz // 2):
        for i, r, natural in ((0, HALO + rx, top), (1, 0, ~top)):
            odd = pltpu.roll(tot[2 * j + 1, pl.ds(r, HALO), :], QUARTER, 0)
            rim_x[i, j] = jnp.where(natural, tot[2 * j, pl.ds(r, HALO), :], odd)

    start_all(copy2)
    wait_send_all(copy1)
    wait_recv_all(copy2)

    gap = jnp.zeros((rx - 2 * HALO, LANES), f32)
    l2 = left2[...] + jnp.concatenate([corners[0], gap, corners[2]], axis=0)
    r2 = right2[...] + jnp.concatenate([corners[1], gap, corners[3]], axis=0)
    both = jnp.where(lows, r2, l2)
    rim = (lane < QUARTER) | (lane >= ry - QUARTER)
    scale = damping * ext[nz, own, :]
    for z in range(nz):
        moved = pltpu.roll(both, (LANES - QUARTER - half - HALF * z) % LANES, 1)
        u, d = up[z // 2], down[z // 2]
        if z % 2:
            u, d = pltpu.roll(u, QUARTER, 0), pltpu.roll(d, QUARTER, 0)
        t = tot[z, own, :] + jnp.concatenate([jnp.where(top, u, 0.0), gap, jnp.where(top, 0.0, d)], axis=0)
        t = t + jnp.where(rim, moved, 0.0)
        out[z] = state[z] + scale * t

    wait_send_all(copy2)


def on_device(
    sizes, state, load_vector, active, stiff_band, mass_band, eig_basis, eig_values, cut_cols, cut_inverse
):
    nz, rx, ry = state.shape
    slots = cut_cols.shape[-1]
    assert nz == HALF and ry == LANES and rx % PATCH == 0
    inverse = cut_inverse.reshape(cut_inverse.shape[2:])
    wide = rx + 2 * HALO
    full = ry + LANES
    qx, qy = (rx // HALF) * PATCH, (ry // HALF) * PATCH
    cells = PATCH * PATCH
    anyspace = pl.BlockSpec(memory_space=pltpu.HBM)
    V, S = pltpu.VMEM, pltpu.SMEM
    dma = pltpu.SemaphoreType.DMA
    n = len(DIRS)
    return pl.pallas_call(
        functools.partial(kernel, sizes),
        out_shape=pltpu.VMEM(state.shape, f32),
        in_specs=[anyspace] * 9,
        out_specs=pl.BlockSpec(memory_space=pltpu.VMEM),
        scratch_shapes=[
            V(state.shape, f32), V(load_vector.shape, load_vector.dtype), V(active.shape, active.dtype),
            S(stiff_band.shape, f32), S(mass_band.shape, f32), S(eig_basis.shape, f32),
            V(eig_basis.shape, f32), S(eig_values.shape, f32), S(cut_cols.shape, cut_cols.dtype),
            V((slots, PATCH, cells, cells), bf16),
            V((nz + 1 + nz // 2, wide, ry), f32), V((nz, wide, ry), f32),
            V((wide, LANES), f32), V((wide, LANES), f32),
            V((rx, LANES), f32), V((rx, LANES), f32),
            V((3 * full, 2 * full), bf16), V((3 * full, qy), bf16), V((full, 3 * qy), bf16),
            V((slots, 2 * full, cells), bf16),
            V((PATCH, qx, qy), f32),
            V((nz, wide, ry), f32), V((nz, wide, ry), f32),
            V((nz * wide, 3 * full), bf16), V((nz * wide, 3 * full), bf16),
            V((PATCH * wide, 3 * full), bf16), V((PATCH * wide, 3 * qy), bf16),
            V((nz, wide, ry), f32), V((wide, LANES), f32),
            V((2, nz // 2, HALO, ry), f32),
            V((nz // 2, HALO, ry), f32), V((nz // 2, HALO, ry), f32),
            V((rx, LANES), f32), V((rx, LANES), f32),
            V((4, HALO, LANES), f32),
            dma((10,)), dma((n,)), dma((n,)), dma((n,)), dma((n,)),
        ],
        compiler_params=pltpu.CompilerParams(
            collective_id=0, has_side_effects=True, vmem_limit_bytes=56 * 1024 * 1024
        ),
    )(state, load_vector, active, stiff_band, mass_band, eig_basis, eig_values, cut_cols, inverse)


def solution(mesh):
    placed = (
        P(None, "gx", "gy"),
        P(None, "gx", "gy"),
        P("gx", "gy"),
        P(),
        P(),
        P(),
        P(),
        P("gx", "gy", None),
        P("gx", "gy", None, None, None, None),
    )
    sizes = (mesh.shape["gx"], mesh.shape["gy"])
    return jax.shard_map(
        functools.partial(on_device, sizes),
        mesh=mesh, in_specs=placed, out_specs=P(None, "gx", "gy"), check_vma=False,
    )
```

```python
import functools

import jax
import jax.numpy as jnp
from jax import lax
from jax.experimental import pallas as pl
from jax.experimental.pallas import tpu as pltpu
from jax.sharding import PartitionSpec as P

BAND = 4
PATCH = 16
HALF = PATCH // 2
QUARTER = PATCH // 4
HALO = BAND + QUARTER
LANES = 128
MESH = pl.DeviceIdType.MESH
DIRS = [(1, 0), (-1, 0), (1, 1), (1, -1), (-1, 1), (-1, -1), (0, 1), (0, -1)]

damping = 0.5
f32 = jnp.float32
bf16 = jnp.bfloat16


def iota(shape, dim):
    return lax.broadcasted_iota(jnp.int32, shape, dim)


def split(v):
    hi = v.astype(bf16)
    return hi, (v - hi.astype(f32)).astype(bf16)


def dot(a, b):
    return jnp.dot(a, b, preferred_element_type=f32)


def dot_nt(a, b):
    return lax.dot_general(a, b, (((1,), (1,)), ((), ())), preferred_element_type=f32)


def band_of(distance, taps):
    out = jnp.zeros(distance.shape, f32)
    for k in range(BAND + 1):
        out = jnp.where(distance == k, taps[k], out)
    return out


def inner_y(c, ry):
    u = (c - ry) & (HALF - 1)
    halo = jnp.where(u < QUARTER, u - QUARTER, ry + u - QUARTER)
    return jnp.where(c < ry, c, jnp.where(c < ry + LANES // 2, -1000, halo))


def outer_y(r, ry):
    u = (r - ry) & (HALF - 1)
    return jnp.where(r < ry, r, jnp.where(r < ry + LANES // 2, u - HALO, ry + u))


def wrap(v, n, reps):
    out = v
    for j in range(1, reps):
        out = out - jnp.where(v >= n * j, n, 0)
    return out


def kernel(
    sizes,
    state_h, load_h, active_h, stiff_h, mass_h, basis_h, values_h, cols_h, inverse_h,
    out,
    state, load, active, stiff, mass, basis_s, basis, values, cols, inv,
    ext, lf, from_left, from_right, pack_left, pack_right,
    yb, wy3, wyt3, sel, sel_t, dinv, rs, cw,
    zk, zm, sk3, sm3, r3, tb3, tot, edge,
    rim_x, up, down, left2, right2, corners,
    in_sem, send1, recv1, send2, recv2,
):
    n_x, n_y = sizes
    nz, rx, ry = state.shape
    wide = rx + 2 * HALO
    slots = inv.shape[0]
    blocks_x, blocks_y = rx // HALF, ry // HALF
    qx, qy = blocks_x * PATCH, blocks_y * PATCH
    full = ry + LANES
    half = LANES // 2
    groups = half // HALF
    me_x, me_y = lax.axis_index("gx"), lax.axis_index("gy")

    def exists(dx, dy):
        ok = None
        for d, me, n in ((dx, me_x, n_x), (dy, me_y, n_y)):
            if d:
                part = (me + d >= 0) & (me + d < n)
                ok = part if ok is None else ok & part
        return ok

    def device(dx, dy):
        return (jnp.clip(me_x + dx, 0, n_x - 1), jnp.clip(me_y + dy, 0, n_y - 1))

    fetches = [
        pltpu.make_async_copy(src, dst, in_sem.at[i])
        for i, (src, dst) in enumerate((
            (state_h, state), (load_h, load), (active_h, active),
            (stiff_h, stiff), (mass_h, mass), (basis_h, basis_s), (basis_h, basis),
            (values_h, values), (cols_h, cols), (inverse_h, inv),
        ))
    ]
    for fetch in fetches:
        fetch.start()

    own = pl.ds(HALO, rx)
    planes = nz + 1 + nz // 2
    zeros = jnp.zeros((planes, HALO, ry), f32)
    ext[:, pl.ds(0, HALO), :] = zeros
    ext[:, pl.ds(HALO + rx, HALO), :] = zeros
    for ref in (from_left, from_right, up, down, left2, right2, corners):
        ref[...] = jnp.zeros(ref.shape, f32)

    barrier = pltpu.get_barrier_semaphore()
    count = jnp.int32(0)
    for d in DIRS:
        ok = exists(*d)
        count = count + ok.astype(jnp.int32)

        @pl.when(ok)
        def _(d=d):
            pl.semaphore_signal(barrier, inc=1, device_id=device(*d), device_id_type=MESH)

    for fetch in fetches[:3]:
        fetch.wait()
    for z in range(nz):
        ext[z, own, :] = state[z]
        lf[z, own, :] = load[z].astype(f32)
    ext[nz, own, :] = active[...].astype(f32)
    top = iota((HALO, ry), 0) < QUARTER
    for j in range(nz // 2):
        for r, natural in ((HALO, top), (rx, ~top)):
            odd = pltpu.roll(lf[2 * j + 1, pl.ds(r, HALO), :], QUARTER, 0)
            ext[nz + 1 + j, pl.ds(r, HALO), :] = jnp.where(natural, lf[2 * j, pl.ds(r, HALO), :], odd)

    lane = iota((rx, LANES), 1)
    group = (lane & (half - 1)) >> 3
    high = lane >= half
    lows = (lane & (HALF - 1)) < QUARTER
    to_right = jnp.zeros((rx, LANES), f32)
    to_left = jnp.zeros((rx, LANES), f32)
    act = ext[nz, own, :]
    for z in range(nz):
        s = ext[z, own, :]
        l = pltpu.roll(lf[z, own, :], (half + QUARTER + HALF * z) % LANES, 1)
        mine = group == z
        first = mine & high & lows
        second = mine & high & ~lows
        to_right = jnp.where(mine & ~high, pltpu.roll(s, (HALF + HALF * z) % LANES, 1), to_right)
        to_right = jnp.where(first, l, to_right)
        to_right = jnp.where(second, pltpu.roll(act, (half + HALF + HALF * z) % LANES, 1), to_right)
        to_left = jnp.where(mine & ~high, pltpu.roll(s, HALF * z, 1) if z else s, to_left)
        to_left = jnp.where(second, l, to_left)
        to_left = jnp.where(first, pltpu.roll(act, (half + HALF * z) % LANES, 1), to_left)
    pack_right[...] = to_right
    pack_left[...] = to_left

    def copy1(i):
        dx, dy = DIRS[i]
        if dy == 0:
            src = ext.at[:, pl.ds(rx if dx > 0 else HALO, HALO), :]
            dst = ext.at[:, pl.ds(0 if dx > 0 else HALO + rx, HALO), :]
        else:
            pack = pack_right if dy > 0 else pack_left
            land = from_left if dy > 0 else from_right
            if dx == 0:
                src, dst = pack, land.at[pl.ds(HALO, rx), :]
            else:
                src = pack.at[pl.ds(rx - HALO if dx > 0 else 0, HALO), :]
                dst = land.at[pl.ds(0 if dx > 0 else HALO + rx, HALO), :]
        return pltpu.make_async_remote_copy(
            src_ref=src, dst_ref=dst, send_sem=send1.at[i], recv_sem=recv1.at[i],
            device_id=device(dx, dy), device_id_type=MESH,
        )

    def copy2(i):
        dx, dy = DIRS[i]
        if dy == 0:
            src = rim_x.at[0 if dx > 0 else 1]
            dst = up if dx > 0 else down
        elif dx == 0:
            src = edge.at[pl.ds(HALO, rx), :]
            dst = left2 if dy > 0 else right2
        else:
            src = edge.at[pl.ds(HALO + rx if dx > 0 else 0, HALO), :]
            dst = corners.at[(dx < 0) * 2 + (dy < 0)]
        return pltpu.make_async_remote_copy(
            src_ref=src, dst_ref=dst, send_sem=send2.at[i], recv_sem=recv2.at[i],
            device_id=device(dx, dy), device_id_type=MESH,
        )

    def start_all(copy):
        for i, d in enumerate(DIRS):
            @pl.when(exists(*d))
            def _(i=i):
                copy(i).start()

    def wait_recv_all(copy):
        for i, (dx, dy) in enumerate(DIRS):
            @pl.when(exists(-dx, -dy))
            def _(i=i):
                copy(i).wait_recv()

    def wait_send_all(copy):
        for i, d in enumerate(DIRS):
            @pl.when(exists(*d))
            def _(i=i):
                copy(i).wait_send()

    pl.semaphore_wait(barrier, count)
    start_all(copy1)

    for fetch in fetches[3:9]:
        fetch.wait()
    distance = jnp.abs(outer_y(iota((full, 1), 0), ry) - inner_y(iota((1, full), 1), ry))
    for j, taps in enumerate((mass, stiff)):
        h, l = split(band_of(distance, [taps[2, k] for k in range(BAND + 1)]))
        for i, part in enumerate((h, h, l)):
            yb[pl.ds(i * full, full), pl.ds(j * full, full)] = part

    highest = lax.Precision.HIGHEST
    tile_y = jnp.dot(
        basis[2], (iota((PATCH, qy), 0) == (iota((PATCH, qy), 1) & (PATCH - 1))).astype(f32),
        precision=highest, preferred_element_type=f32,
    )
    place = inner_y(iota((full, 1), 0), ry) + QUARTER - HALF * (iota((1, qy), 1) >> 4)
    wy = jnp.zeros((full, qy), f32)
    for t in range(PATCH):
        wy = jnp.where(place == t, tile_y[t : t + 1, :], wy)
    h, l = split(wy)
    for i, part in enumerate((h, h, l)):
        wy3[pl.ds(i * full, full), :] = part

    h, l = split(wy.T)
    for i, part in enumerate((h, h, l)):
        wyt3[pl.ds(i * qy, qy), :] = part

    def wx_of(shape, reps_r, reps_c):
        r, c = iota((shape[0], 1), 0), iota((1, shape[1]), 1)
        t = wrap(r, wide, reps_r) - (HALO - QUARTER) - HALF * (wrap(c, qx, reps_c) >> 4)
        t = jnp.where((r < wide * reps_r) & (c < qx * reps_c), t, -1)
        tile = jnp.dot(
            basis[1], (iota((PATCH, shape[1]), 0) == (iota((PATCH, shape[1]), 1) & (PATCH - 1))).astype(f32),
            precision=highest, preferred_element_type=f32,
        )
        w = jnp.zeros(shape, f32)
        for k in range(PATCH):
            w = jnp.where(t == k, tile[k : k + 1, :], w)
        return w

    def split3(v, width):
        h, l = split(v)
        return jnp.where(iota((1, v.shape[1]), 1) < 2 * width, h.astype(f32), l.astype(f32)).astype(bf16)

    pad_r = -(-3 * wide // LANES) * LANES
    pad_c = -(-qx // LANES) * LANES
    g3 = split3(wx_of((pad_r, pad_c), 3, 1).T[:qx, : 3 * wide], wide)
    b3 = split3(wx_of((wide, 3 * qx), 1, 3), qx)

    c = iota((1, 4 * wide), 1)
    dist_x = jnp.abs(iota((wide, 1), 0) - wrap(c, wide, 4))
    bx = jnp.where(
        (c < wide) | ((c >= 2 * wide) & (c < 3 * wide)),
        band_of(dist_x, [mass[1, k] for k in range(BAND + 1)]),
        band_of(dist_x, [stiff[1, k] for k in range(BAND + 1)]),
    )
    bx_hi, bx_lo = split(bx)
    bx_lo = bx_lo[:, : 2 * wide]

    cells = PATCH * PATCH
    cut = [cols[0, 0, m] for m in range(slots)]
    cut_a = [lax.div(jnp.maximum(v, 0), jnp.int32(blocks_y)) for v in cut]
    cut_b = [lax.rem(jnp.maximum(v, 0), jnp.int32(blocks_y)) for v in cut]
    y_in = inner_y(iota((full, 1), 0), ry)
    y_to = iota((1, cells), 1) & (PATCH - 1)
    y_in_t = inner_y(iota((1, full), 1), ry)
    y_to_t = iota((cells, 1), 0) & (PATCH - 1)
    for m in range(slots):
        sel[m] = jnp.where(y_in + QUARTER - HALF * cut_b[m] == y_to, 1.0, 0.0).astype(bf16)
        sel_t[m] = jnp.where(y_in_t + QUARTER - HALF * cut_b[m] == y_to_t, 1.0, 0.0).astype(bf16)

    near = PATCH + HALF
    spot = iota((near, 1), 0) - QUARTER == (iota((1, cells), 1) >> 4)
    vz_t = []
    for z in range(nz):
        v = jnp.zeros((PATCH, 1), f32)
        for k in range(PATCH):
            v = jnp.where(iota((PATCH, 1), 0) == k, basis_s[0, QUARTER + z, k], v)
        vz_t.append(v)

    def pick(shape, dim, row):
        index = iota(shape, dim) & (PATCH - 1)
        v = jnp.zeros(shape, f32)
        for k in range(PATCH):
            v = jnp.where(index == k, values[row, k], v)
        return v

    lam = pick((qx, 1), 0, 1) + pick((1, qy), 1, 2)
    column = (iota((qx, 1), 0) >> 4) * blocks_y + (iota((1, qy), 1) >> 4)
    keep = jnp.ones((qx, qy), f32)
    for m in range(slots):
        keep = jnp.where(column == cut[m], 0.0, keep)
    for k in range(PATCH):
        dinv[k] = keep / (values[0, k] + lam)

    lane1 = iota((1, LANES), 1)
    group1 = (lane1 & (half - 1)) >> 3
    far = [jnp.abs(group1 - z) for z in range(nz)]
    k_vec = [band_of(far[z], [stiff[0, k] for k in range(BAND + 1)]) for z in range(nz)]
    m_vec = [band_of(far[z], [mass[0, k] for k in range(BAND + 1)]) for z in range(nz)]
    v_vec = []
    for k in range(PATCH):
        v = jnp.zeros((1, LANES), f32)
        for z in range(nz):
            v = jnp.where((group1 == z) & (lane1 >= half), basis_s[0, QUARTER + z, k], v)
        v_vec.append(v)

    def put3(ref, rows, start, width, v):
        h, l = split(v)
        for i, part in enumerate((h, l, h)):
            ref[rows, pl.ds(i * width + start, v.shape[1])] = part

    def mix_z(start, count):
        for r in range(start, start + count, HALF):
            rows = pl.ds(r, HALF)
            s = [ext[z, rows, :] for z in range(nz)]
            for z in range(nz):
                p = q = None
                for w in range(nz):
                    k = abs(z - w)
                    if k > BAND:
                        continue
                    a, b = stiff[0, k] * s[w], mass[0, k] * s[w]
                    p = a if p is None else p + a
                    q = b if q is None else q + b
                zk[z, rows, :] = p
                zm[z, rows, :] = q

    mix_z(HALO, rx)
    fetches[9].wait()
    wait_recv_all(copy1)
    mix_z(0, HALO)
    mix_z(HALO + rx, HALO)

    lane_w = iota((wide, LANES), 1)
    group_w = (lane_w & (half - 1)) >> 3
    halo_l, halo_r = from_left[...], from_right[...]
    comb = jnp.where(lane_w < half, halo_l, pltpu.roll(halo_r, half, 1))
    low = (lane_w & (HALF - 1)) < QUARTER
    load_t = jnp.where(low, halo_l, halo_r)
    act_t = jnp.where(low, pltpu.roll(halo_l, LANES - QUARTER, 1), pltpu.roll(halo_r, QUARTER, 1))
    act_t = jnp.where(lane_w >= half, act_t, 0.0)
    act_w = ext[nz]
    for z in range(nz):
        for r in (0, HALO + rx):
            tile = ext[nz + 1 + z // 2, pl.ds(r, HALO), :]
            lf[z, pl.ds(r, HALO), :] = pltpu.roll(tile, QUARTER, 0) if z % 2 else tile
    for z in range(nz):
        rows = pl.ds(z * wide, wide)
        for s3, mixed, vec in ((sk3, zk, k_vec), (sm3, zm, m_vec)):
            put3(s3, rows, 0, full, mixed[z])
            put3(s3, rows, ry, full, comb * vec[z])

    ym = dot(sm3[...], yb[...])
    yp = ym[:, full:] + dot(sk3[...], yb[:, pl.ds(0, full)])

    r0 = []
    r1 = jnp.zeros((wide, LANES), f32)
    for z in range(nz):
        p_hi, p_lo = split(yp[z * wide : (z + 1) * wide])
        q_hi, q_lo = split(ym[z * wide : (z + 1) * wide, :full])
        applied = dot(bx_hi, jnp.concatenate([p_hi, q_hi, p_lo, q_lo], axis=0))
        applied = applied + dot(bx_lo, jnp.concatenate([p_hi, q_hi], axis=0))
        r0.append(act_w * (lf[z] - applied[:, :ry]))
        r1 = jnp.where(group_w == z, applied[:, ry:], r1)
    r1 = act_t * (load_t - r1)

    for k in range(PATCH):
        rows = pl.ds(k * wide, wide)
        v = None
        for z in range(nz):
            term = basis_s[0, QUARTER + z, k] * r0[z]
            v = term if v is None else v + term
        put3(r3, rows, 0, full, v)
        put3(r3, rows, ry, full, r1 * v_vec[k])

    for z in range(nz):
        rs[z, :, pl.ds(0, ry)] = r0[z]
        rs[z, :, pl.ds(ry, LANES)] = jnp.where(group_w == z, r1, 0.0)
    vz = basis[0, pl.ds(QUARTER, nz), :]
    for m in range(slots):
        window = rs[:, pl.ds(0, near), :]
        for a in range(1, blocks_x):
            window = jnp.where(cut_a[m] == a, rs[:, pl.ds(a * HALF, near), :], window)
        h, l = split(window.reshape(nz * near, full))
        taken = (dot(h, sel[m]) + dot(l, sel[m])).reshape(nz, near, cells)
        patch = jnp.sum(jnp.where(spot[None], taken, 0.0), axis=1)
        zmodes = None
        for z in range(nz):
            term = vz_t[z] * patch[z : z + 1, :]
            zmodes = term if zmodes is None else zmodes + term
        zmodes = zmodes.astype(bf16)
        corr = jnp.zeros((nz, cells), f32)
        for k in range(PATCH):
            corr = corr + vz[:, k : k + 1] * dot_nt(zmodes, inv[m, k])[k : k + 1, :]
        corr = jnp.where(cut[m] >= 0, corr, 0.0)
        h, l = split(jnp.where(spot[None], corr[:, None, :], 0.0).reshape(nz * near, cells))
        placed = (dot(h, sel_t[m]) + dot(l, sel_t[m])).reshape(nz, near, full)
        cw[m] = placed

    t1 = dot(r3[...], wy3[...])
    for k in range(PATCH):
        h, l = split(t1[k * wide : (k + 1) * wide])
        h, l = split(dot(g3, jnp.concatenate([h, l, h], axis=0)) * dinv[k])
        back = dot(b3, jnp.concatenate([h, l, h], axis=0))
        put3(tb3, pl.ds(k * wide, wide), 0, qy, back)
    fast = dot(tb3[...], wyt3[...]).reshape(PATCH, wide, full)

    def cut_part(z, start, count, lanes):
        tiles = []
        for r in range(start // HALF, (start + count) // HALF):
            out = jnp.zeros((HALF, LANES), f32)
            for m in range(slots):
                for a in range(blocks_x):
                    if 0 <= r - a < near // HALF:
                        out = out + jnp.where(cut_a[m] == a, cw[m, z, pl.ds((r - a) * HALF, HALF), lanes], 0.0)
            tiles.append(out)
        return jnp.concatenate(tiles, axis=0)

    def total_rows(z, start, count):
        t = cut_part(z, start, count, pl.ds(0, ry))
        for k in range(PATCH):
            t = t + basis_s[0, QUARTER + z, k] * fast[k, start : start + count, :ry]
        tot[z, pl.ds(start, count), :] = t

    packed = jnp.zeros((wide, LANES), f32)
    for z in range(nz):
        packed = jnp.where(group_w == z, cut_part(z, 0, wide, pl.ds(ry, LANES)), packed)
    for k in range(PATCH):
        packed = packed + v_vec[k] * fast[k, :, ry:]
    edge[...] = packed
    for z in range(nz):
        total_rows(z, 0, HALO)
        total_rows(z, HALO + rx, HALO)
    for j in range(nz // 2):
        for i, r, natural in ((0, HALO + rx, top), (1, 0, ~top)):
            odd = pltpu.roll(tot[2 * j + 1, pl.ds(r, HALO), :], QUARTER, 0)
            rim_x[i, j] = jnp.where(natural, tot[2 * j, pl.ds(r, HALO), :], odd)

    start_all(copy2)
    for z in range(nz):
        total_rows(z, HALO, rx)
    wait_send_all(copy1)
    wait_recv_all(copy2)

    gap = jnp.zeros((rx - 2 * HALO, LANES), f32)
    l2 = left2[...] + jnp.concatenate([corners[0], gap, corners[2]], axis=0)
    r2 = right2[...] + jnp.concatenate([corners[1], gap, corners[3]], axis=0)
    both = jnp.where(lows, r2, l2)
    rim = (lane < QUARTER) | (lane >= ry - QUARTER)
    scale = damping * ext[nz, own, :]
    for z in range(nz):
        moved = pltpu.roll(both, (LANES - QUARTER - half - HALF * z) % LANES, 1)
        u, d = up[z // 2], down[z // 2]
        if z % 2:
            u, d = pltpu.roll(u, QUARTER, 0), pltpu.roll(d, QUARTER, 0)
        t = tot[z, own, :] + jnp.concatenate([jnp.where(top, u, 0.0), gap, jnp.where(top, 0.0, d)], axis=0)
        t = t + jnp.where(rim, moved, 0.0)
        out[z] = state[z] + scale * t

    wait_send_all(copy2)


def on_device(
    sizes, state, load_vector, active, stiff_band, mass_band, eig_basis, eig_values, cut_cols, cut_inverse
):
    nz, rx, ry = state.shape
    slots = cut_cols.shape[-1]
    assert nz == HALF and ry == LANES and rx % PATCH == 0
    inverse = cut_inverse.reshape(cut_inverse.shape[2:])
    wide = rx + 2 * HALO
    full = ry + LANES
    qx, qy = (rx // HALF) * PATCH, (ry // HALF) * PATCH
    cells = PATCH * PATCH
    anyspace = pl.BlockSpec(memory_space=pltpu.HBM)
    V, S = pltpu.VMEM, pltpu.SMEM
    dma = pltpu.SemaphoreType.DMA
    n = len(DIRS)
    return pl.pallas_call(
        functools.partial(kernel, sizes),
        out_shape=pltpu.VMEM(state.shape, f32),
        in_specs=[anyspace] * 9,
        out_specs=pl.BlockSpec(memory_space=pltpu.VMEM),
        scratch_shapes=[
            V(state.shape, f32), V(load_vector.shape, load_vector.dtype), V(active.shape, active.dtype),
            S(stiff_band.shape, f32), S(mass_band.shape, f32), S(eig_basis.shape, f32),
            V(eig_basis.shape, f32), S(eig_values.shape, f32), S(cut_cols.shape, cut_cols.dtype),
            V((slots, PATCH, cells, cells), bf16),
            V((nz + 1 + nz // 2, wide, ry), f32), V((nz, wide, ry), f32),
            V((wide, LANES), f32), V((wide, LANES), f32),
            V((rx, LANES), f32), V((rx, LANES), f32),
            V((3 * full, 2 * full), bf16), V((3 * full, qy), bf16), V((3 * qy, full), bf16),
            V((slots, full, cells), bf16), V((slots, cells, full), bf16),
            V((PATCH, qx, qy), f32),
            V((nz, wide, full), f32), V((slots, nz, PATCH + HALF, full), f32),
            V((nz, wide, ry), f32), V((nz, wide, ry), f32),
            V((nz * wide, 3 * full), bf16), V((nz * wide, 3 * full), bf16),
            V((PATCH * wide, 3 * full), bf16), V((PATCH * wide, 3 * qy), bf16),
            V((nz, wide, ry), f32), V((wide, LANES), f32),
            V((2, nz // 2, HALO, ry), f32),
            V((nz // 2, HALO, ry), f32), V((nz // 2, HALO, ry), f32),
            V((rx, LANES), f32), V((rx, LANES), f32),
            V((4, HALO, LANES), f32),
            dma((10,)), dma((n,)), dma((n,)), dma((n,)), dma((n,)),
        ],
        compiler_params=pltpu.CompilerParams(
            collective_id=0, has_side_effects=True, vmem_limit_bytes=56 * 1024 * 1024
        ),
    )(state, load_vector, active, stiff_band, mass_band, eig_basis, eig_values, cut_cols, inverse)


def solution(mesh):
    placed = (
        P(None, "gx", "gy"),
        P(None, "gx", "gy"),
        P("gx", "gy"),
        P(),
        P(),
        P(),
        P(),
        P("gx", "gy", None),
        P("gx", "gy", None, None, None, None),
    )
    sizes = (mesh.shape["gx"], mesh.shape["gy"])
    return jax.shard_map(
        functools.partial(on_device, sizes),
        mesh=mesh, in_specs=placed, out_specs=P(None, "gx", "gy"), check_vma=False,
    )
```

```python
import functools

import jax
import jax.numpy as jnp
from jax import lax
from jax.experimental import pallas as pl
from jax.experimental.pallas import tpu as pltpu
from jax.sharding import PartitionSpec as P

BAND = 4
PATCH = 16
HALF = PATCH // 2
QUARTER = PATCH // 4
HALO = BAND + QUARTER
LANES = 128
MESH = pl.DeviceIdType.MESH
DIRS = [(1, 0), (-1, 0), (1, 1), (1, -1), (-1, 1), (-1, -1), (0, 1), (0, -1)]

damping = 0.5
f32 = jnp.float32
bf16 = jnp.bfloat16


def iota(shape, dim):
    return lax.broadcasted_iota(jnp.int32, shape, dim)


def split(v):
    hi = v.astype(bf16)
    return hi, (v - hi.astype(f32)).astype(bf16)


def dot(a, b):
    return jnp.dot(a, b, preferred_element_type=f32)


def band_of(distance, taps):
    out = jnp.zeros(distance.shape, f32)
    for k in range(BAND + 1):
        out = jnp.where(distance == k, taps[k], out)
    return out


def inner_y(c, ry):
    u = (c - ry) & (HALF - 1)
    halo = jnp.where(u < QUARTER, u - QUARTER, ry + u - QUARTER)
    return jnp.where(c < ry, c, jnp.where(c < ry + LANES // 2, -1000, halo))


def outer_y(r, ry):
    u = (r - ry) & (HALF - 1)
    return jnp.where(r < ry, r, jnp.where(r < ry + LANES // 2, u - HALO, ry + u))


def wrap(v, n, reps):
    out = v
    for j in range(1, reps):
        out = out - jnp.where(v >= n * j, n, 0)
    return out


def kernel(
    sizes,
    state_h, load_h, active_h, stiff_h, mass_h, basis_h, values_h, cols_h, inverse_h,
    out,
    state, load, active, stiff, mass, basis_s, basis, values, cols, inv,
    ext, lf, from_left, from_right, pack_left, pack_right,
    yb, wy3, wyt3, sel, sel_t, dinv, rs, cw,
    zk, zm, sk3, sm3, r3, tb3, tot, edge,
    rim_x, up, down, left2, right2, corners,
    in_sem, send1, recv1, send2, recv2,
):
    n_x, n_y = sizes
    nz, rx, ry = state.shape
    wide = rx + 2 * HALO
    slots = inv.shape[0]
    blocks_x, blocks_y = rx // HALF, ry // HALF
    qx, qy = blocks_x * PATCH, blocks_y * PATCH
    full = ry + LANES
    half = LANES // 2
    groups = half // HALF
    me_x, me_y = lax.axis_index("gx"), lax.axis_index("gy")

    def exists(dx, dy):
        ok = None
        for d, me, n in ((dx, me_x, n_x), (dy, me_y, n_y)):
            if d:
                part = (me + d >= 0) & (me + d < n)
                ok = part if ok is None else ok & part
        return ok

    def device(dx, dy):
        return (jnp.clip(me_x + dx, 0, n_x - 1), jnp.clip(me_y + dy, 0, n_y - 1))

    fetches = [
        pltpu.make_async_copy(src, dst, in_sem.at[i])
        for i, (src, dst) in enumerate((
            (state_h, state), (load_h, load), (active_h, active),
            (stiff_h, stiff), (mass_h, mass), (basis_h, basis_s), (basis_h, basis),
            (values_h, values), (cols_h, cols), (inverse_h, inv),
        ))
    ]
    for fetch in fetches:
        fetch.start()

    own = pl.ds(HALO, rx)
    planes = nz + 1 + nz // 2
    zeros = jnp.zeros((planes, HALO, ry), f32)
    ext[:, pl.ds(0, HALO), :] = zeros
    ext[:, pl.ds(HALO + rx, HALO), :] = zeros
    for ref in (from_left, from_right, up, down, left2, right2, corners):
        ref[...] = jnp.zeros(ref.shape, f32)

    barrier = pltpu.get_barrier_semaphore()
    count = jnp.int32(0)
    for d in DIRS:
        ok = exists(*d)
        count = count + ok.astype(jnp.int32)

        @pl.when(ok)
        def _(d=d):
            pl.semaphore_signal(barrier, inc=1, device_id=device(*d), device_id_type=MESH)

    for fetch in fetches[:3]:
        fetch.wait()
    for z in range(nz):
        ext[z, own, :] = state[z]
        lf[z, own, :] = load[z].astype(f32)
    ext[nz, own, :] = active[...].astype(f32)
    top = iota((HALO, ry), 0) < QUARTER
    for j in range(nz // 2):
        for r, natural in ((HALO, top), (rx, ~top)):
            odd = pltpu.roll(lf[2 * j + 1, pl.ds(r, HALO), :], QUARTER, 0)
            ext[nz + 1 + j, pl.ds(r, HALO), :] = jnp.where(natural, lf[2 * j, pl.ds(r, HALO), :], odd)

    lane = iota((rx, LANES), 1)
    group = (lane & (half - 1)) >> 3
    high = lane >= half
    lows = (lane & (HALF - 1)) < QUARTER
    to_right = jnp.zeros((rx, LANES), f32)
    to_left = jnp.zeros((rx, LANES), f32)
    act = ext[nz, own, :]
    for z in range(nz):
        s = ext[z, own, :]
        l = pltpu.roll(lf[z, own, :], (half + QUARTER + HALF * z) % LANES, 1)
        mine = group == z
        first = mine & high & lows
        second = mine & high & ~lows
        to_right = jnp.where(mine & ~high, pltpu.roll(s, (HALF + HALF * z) % LANES, 1), to_right)
        to_right = jnp.where(first, l, to_right)
        to_right = jnp.where(second, pltpu.roll(act, (half + HALF + HALF * z) % LANES, 1), to_right)
        to_left = jnp.where(mine & ~high, pltpu.roll(s, HALF * z, 1) if z else s, to_left)
        to_left = jnp.where(second, l, to_left)
        to_left = jnp.where(first, pltpu.roll(act, (half + HALF * z) % LANES, 1), to_left)
    pack_right[...] = to_right
    pack_left[...] = to_left

    def copy1(i):
        dx, dy = DIRS[i]
        if dy == 0:
            src = ext.at[:, pl.ds(rx if dx > 0 else HALO, HALO), :]
            dst = ext.at[:, pl.ds(0 if dx > 0 else HALO + rx, HALO), :]
        else:
            pack = pack_right if dy > 0 else pack_left
            land = from_left if dy > 0 else from_right
            if dx == 0:
                src, dst = pack, land.at[pl.ds(HALO, rx), :]
            else:
                src = pack.at[pl.ds(rx - HALO if dx > 0 else 0, HALO), :]
                dst = land.at[pl.ds(0 if dx > 0 else HALO + rx, HALO), :]
        return pltpu.make_async_remote_copy(
            src_ref=src, dst_ref=dst, send_sem=send1.at[i], recv_sem=recv1.at[i],
            device_id=device(dx, dy), device_id_type=MESH,
        )

    def copy2(i):
        dx, dy = DIRS[i]
        if dy == 0:
            src = rim_x.at[0 if dx > 0 else 1]
            dst = up if dx > 0 else down
        elif dx == 0:
            src = edge.at[pl.ds(HALO, rx), :]
            dst = left2 if dy > 0 else right2
        else:
            src = edge.at[pl.ds(HALO + rx if dx > 0 else 0, HALO), :]
            dst = corners.at[(dx < 0) * 2 + (dy < 0)]
        return pltpu.make_async_remote_copy(
            src_ref=src, dst_ref=dst, send_sem=send2.at[i], recv_sem=recv2.at[i],
            device_id=device(dx, dy), device_id_type=MESH,
        )

    def start_all(copy):
        for i, d in enumerate(DIRS):
            @pl.when(exists(*d))
            def _(i=i):
                copy(i).start()

    def wait_recv_all(copy):
        for i, (dx, dy) in enumerate(DIRS):
            @pl.when(exists(-dx, -dy))
            def _(i=i):
                copy(i).wait_recv()

    def wait_send_all(copy):
        for i, d in enumerate(DIRS):
            @pl.when(exists(*d))
            def _(i=i):
                copy(i).wait_send()

    pl.semaphore_wait(barrier, count)
    start_all(copy1)

    for fetch in fetches[3:9]:
        fetch.wait()
    distance = jnp.abs(outer_y(iota((full, 1), 0), ry) - inner_y(iota((1, full), 1), ry))
    for j, taps in enumerate((mass, stiff)):
        h, l = split(band_of(distance, [taps[2, k] for k in range(BAND + 1)]))
        for i, part in enumerate((h, h, l)):
            yb[pl.ds(i * full, full), pl.ds(j * full, full)] = part

    highest = lax.Precision.HIGHEST
    tile_y = jnp.dot(
        basis[2], (iota((PATCH, qy), 0) == (iota((PATCH, qy), 1) & (PATCH - 1))).astype(f32),
        precision=highest, preferred_element_type=f32,
    )
    place = inner_y(iota((full, 1), 0), ry) + QUARTER - HALF * (iota((1, qy), 1) >> 4)
    wy = jnp.zeros((full, qy), f32)
    for t in range(PATCH):
        wy = jnp.where(place == t, tile_y[t : t + 1, :], wy)
    h, l = split(wy)
    for i, part in enumerate((h, h, l)):
        wy3[pl.ds(i * full, full), :] = part

    h, l = split(wy.T)
    for i, part in enumerate((h, h, l)):
        wyt3[pl.ds(i * qy, qy), :] = part

    def wx_of(shape, reps_r, reps_c):
        r, c = iota((shape[0], 1), 0), iota((1, shape[1]), 1)
        t = wrap(r, wide, reps_r) - (HALO - QUARTER) - HALF * (wrap(c, qx, reps_c) >> 4)
        t = jnp.where((r < wide * reps_r) & (c < qx * reps_c), t, -1)
        tile = jnp.dot(
            basis[1], (iota((PATCH, shape[1]), 0) == (iota((PATCH, shape[1]), 1) & (PATCH - 1))).astype(f32),
            precision=highest, preferred_element_type=f32,
        )
        w = jnp.zeros(shape, f32)
        for k in range(PATCH):
            w = jnp.where(t == k, tile[k : k + 1, :], w)
        return w

    def split3(v, width):
        h, l = split(v)
        return jnp.where(iota((1, v.shape[1]), 1) < 2 * width, h.astype(f32), l.astype(f32)).astype(bf16)

    pad_r = -(-3 * wide // LANES) * LANES
    pad_c = -(-qx // LANES) * LANES
    g3 = split3(wx_of((pad_r, pad_c), 3, 1).T[:qx, : 3 * wide], wide)
    b3 = split3(wx_of((wide, 3 * qx), 1, 3), qx)

    c = iota((1, 4 * wide), 1)
    dist_x = jnp.abs(iota((wide, 1), 0) - wrap(c, wide, 4))
    bx = jnp.where(
        (c < wide) | ((c >= 2 * wide) & (c < 3 * wide)),
        band_of(dist_x, [mass[1, k] for k in range(BAND + 1)]),
        band_of(dist_x, [stiff[1, k] for k in range(BAND + 1)]),
    )
    bx_hi, bx_lo = split(bx)
    bx_lo = bx_lo[:, : 2 * wide]

    cells = PATCH * PATCH
    cut = [cols[0, 0, m] for m in range(slots)]
    cut_a = [lax.div(jnp.maximum(v, 0), jnp.int32(blocks_y)) for v in cut]
    cut_b = [lax.rem(jnp.maximum(v, 0), jnp.int32(blocks_y)) for v in cut]
    y_in = inner_y(iota((full, 1), 0), ry)
    y_to = iota((1, cells), 1) & (PATCH - 1)
    y_in_t = inner_y(iota((1, full), 1), ry)
    y_to_t = iota((cells, 1), 0) & (PATCH - 1)
    for m in range(slots):
        sel[m] = jnp.where(y_in + QUARTER - HALF * cut_b[m] == y_to, 1.0, 0.0).astype(bf16)
        sel_t[m] = jnp.where(y_in_t + QUARTER - HALF * cut_b[m] == y_to_t, 1.0, 0.0).astype(bf16)

    near = PATCH + HALF
    spot = iota((near, 1), 0) - QUARTER == (iota((1, cells), 1) >> 4)
    vz_t = []
    for z in range(nz):
        v = jnp.zeros((PATCH, 1), f32)
        for k in range(PATCH):
            v = jnp.where(iota((PATCH, 1), 0) == k, basis_s[0, QUARTER + z, k], v)
        vz_t.append(v)

    def pick(shape, dim, row):
        index = iota(shape, dim) & (PATCH - 1)
        v = jnp.zeros(shape, f32)
        for k in range(PATCH):
            v = jnp.where(index == k, values[row, k], v)
        return v

    lam = pick((qx, 1), 0, 1) + pick((1, qy), 1, 2)
    column = (iota((qx, 1), 0) >> 4) * blocks_y + (iota((1, qy), 1) >> 4)
    keep = jnp.ones((qx, qy), f32)
    for m in range(slots):
        keep = jnp.where(column == cut[m], 0.0, keep)
    for k in range(PATCH):
        dinv[k] = keep / (values[0, k] + lam)

    lane1 = iota((1, LANES), 1)
    group1 = (lane1 & (half - 1)) >> 3
    far = [jnp.abs(group1 - z) for z in range(nz)]
    k_vec = [band_of(far[z], [stiff[0, k] for k in range(BAND + 1)]) for z in range(nz)]
    m_vec = [band_of(far[z], [mass[0, k] for k in range(BAND + 1)]) for z in range(nz)]
    v_vec = []
    for k in range(PATCH):
        v = jnp.zeros((1, LANES), f32)
        for z in range(nz):
            v = jnp.where((group1 == z) & (lane1 >= half), basis_s[0, QUARTER + z, k], v)
        v_vec.append(v)

    def put3(ref, rows, start, width, v):
        h, l = split(v)
        for i, part in enumerate((h, l, h)):
            ref[rows, pl.ds(i * width + start, v.shape[1])] = part

    def mix_z(start, count):
        for r in range(start, start + count, HALF):
            rows = pl.ds(r, HALF)
            s = [ext[z, rows, :] for z in range(nz)]
            for z in range(nz):
                p = q = None
                for w in range(nz):
                    k = abs(z - w)
                    if k > BAND:
                        continue
                    a, b = stiff[0, k] * s[w], mass[0, k] * s[w]
                    p = a if p is None else p + a
                    q = b if q is None else q + b
                zk[z, rows, :] = p
                zm[z, rows, :] = q

    mix_z(HALO, rx)
    fetches[9].wait()
    wait_recv_all(copy1)
    mix_z(0, HALO)
    mix_z(HALO + rx, HALO)

    lane_w = iota((wide, LANES), 1)
    group_w = (lane_w & (half - 1)) >> 3
    halo_l, halo_r = from_left[...], from_right[...]
    comb = jnp.where(lane_w < half, halo_l, pltpu.roll(halo_r, half, 1))
    low = (lane_w & (HALF - 1)) < QUARTER
    load_t = jnp.where(low, halo_l, halo_r)
    act_t = jnp.where(low, pltpu.roll(halo_l, LANES - QUARTER, 1), pltpu.roll(halo_r, QUARTER, 1))
    act_t = jnp.where(lane_w >= half, act_t, 0.0)
    act_w = ext[nz]
    for z in range(nz):
        for r in (0, HALO + rx):
            tile = ext[nz + 1 + z // 2, pl.ds(r, HALO), :]
            lf[z, pl.ds(r, HALO), :] = pltpu.roll(tile, QUARTER, 0) if z % 2 else tile
    for z in range(nz):
        rows = pl.ds(z * wide, wide)
        for s3, mixed, vec in ((sk3, zk, k_vec), (sm3, zm, m_vec)):
            put3(s3, rows, 0, full, mixed[z])
            put3(s3, rows, ry, full, comb * vec[z])

    ym = dot(sm3[...], yb[...])
    yp = ym[:, full:] + dot(sk3[...], yb[:, pl.ds(0, full)])

    r0 = []
    r1 = jnp.zeros((wide, LANES), f32)
    for z in range(nz):
        p_hi, p_lo = split(yp[z * wide : (z + 1) * wide])
        q_hi, q_lo = split(ym[z * wide : (z + 1) * wide, :full])
        applied = dot(bx_hi, jnp.concatenate([p_hi, q_hi, p_lo, q_lo], axis=0))
        applied = applied + dot(bx_lo, jnp.concatenate([p_hi, q_hi], axis=0))
        r0.append(act_w * (lf[z] - applied[:, :ry]))
        r1 = jnp.where(group_w == z, applied[:, ry:], r1)
    r1 = act_t * (load_t - r1)

    for k in range(PATCH):
        rows = pl.ds(k * wide, wide)
        v = None
        for z in range(nz):
            term = basis_s[0, QUARTER + z, k] * r0[z]
            v = term if v is None else v + term
        put3(r3, rows, 0, full, v)
        put3(r3, rows, ry, full, r1 * v_vec[k])

    for z in range(nz):
        rs[z, :, pl.ds(0, ry)] = r0[z]
        rs[z, :, pl.ds(ry, LANES)] = jnp.where(group_w == z, r1, 0.0)
    vz = basis[0, pl.ds(QUARTER, nz), :]
    for m in range(slots):
        window = rs[:, pl.ds(0, near), :]
        for a in range(1, blocks_x):
            window = jnp.where(cut_a[m] == a, rs[:, pl.ds(a * HALF, near), :], window)
        h, l = split(window.reshape(nz * near, full))
        taken = (dot(h, sel[m]) + dot(l, sel[m])).reshape(nz, near, cells)
        patch = jnp.sum(jnp.where(spot[None], taken, 0.0), axis=1)
        zmodes = None
        for z in range(nz):
            term = vz_t[z] * patch[z : z + 1, :]
            zmodes = term if zmodes is None else zmodes + term
        zmodes = zmodes.T.astype(bf16)
        dense = jnp.zeros((cells, PATCH), f32)
        for k in range(PATCH):
            dense = jnp.where(iota((1, PATCH), 1) == k, dot(inv[m, k], zmodes), dense)
        corr = lax.dot_general(
            vz, dense, (((1,), (1,)), ((), ())), precision=highest, preferred_element_type=f32
        )
        corr = jnp.where(cut[m] >= 0, corr, 0.0)
        h, l = split(jnp.where(spot[None], corr[:, None, :], 0.0).reshape(nz * near, cells))
        placed = (dot(h, sel_t[m]) + dot(l, sel_t[m])).reshape(nz, near, full)
        cw[m] = placed

    t1 = dot(r3[...], wy3[...])
    for k in range(PATCH):
        h, l = split(t1[k * wide : (k + 1) * wide])
        h, l = split(dot(g3, jnp.concatenate([h, l, h], axis=0)) * dinv[k])
        back = dot(b3, jnp.concatenate([h, l, h], axis=0))
        put3(tb3, pl.ds(k * wide, wide), 0, qy, back)
    fast = dot(tb3[...], wyt3[...]).reshape(PATCH, wide, full)

    def cut_part(z, start, count, lanes):
        tiles = []
        for r in range(start // HALF, (start + count) // HALF):
            out = jnp.zeros((HALF, LANES), f32)
            for m in range(slots):
                for a in range(blocks_x):
                    if 0 <= r - a < near // HALF:
                        out = out + jnp.where(cut_a[m] == a, cw[m, z, pl.ds((r - a) * HALF, HALF), lanes], 0.0)
            tiles.append(out)
        return jnp.concatenate(tiles, axis=0)

    def total_rows(z, start, count):
        t = cut_part(z, start, count, pl.ds(0, ry))
        for k in range(PATCH):
            t = t + basis_s[0, QUARTER + z, k] * fast[k, start : start + count, :ry]
        tot[z, pl.ds(start, count), :] = t

    packed = jnp.zeros((wide, LANES), f32)
    for z in range(nz):
        packed = jnp.where(group_w == z, cut_part(z, 0, wide, pl.ds(ry, LANES)), packed)
    for k in range(PATCH):
        packed = packed + v_vec[k] * fast[k, :, ry:]
    edge[...] = packed
    for z in range(nz):
        total_rows(z, 0, HALO)
        total_rows(z, HALO + rx, HALO)
    for j in range(nz // 2):
        for i, r, natural in ((0, HALO + rx, top), (1, 0, ~top)):
            odd = pltpu.roll(tot[2 * j + 1, pl.ds(r, HALO), :], QUARTER, 0)
            rim_x[i, j] = jnp.where(natural, tot[2 * j, pl.ds(r, HALO), :], odd)

    start_all(copy2)
    for z in range(nz):
        total_rows(z, HALO, rx)
    wait_send_all(copy1)
    wait_recv_all(copy2)

    gap = jnp.zeros((rx - 2 * HALO, LANES), f32)
    l2 = left2[...] + jnp.concatenate([corners[0], gap, corners[2]], axis=0)
    r2 = right2[...] + jnp.concatenate([corners[1], gap, corners[3]], axis=0)
    both = jnp.where(lows, r2, l2)
    rim = (lane < QUARTER) | (lane >= ry - QUARTER)
    scale = damping * ext[nz, own, :]
    for z in range(nz):
        moved = pltpu.roll(both, (LANES - QUARTER - half - HALF * z) % LANES, 1)
        u, d = up[z // 2], down[z // 2]
        if z % 2:
            u, d = pltpu.roll(u, QUARTER, 0), pltpu.roll(d, QUARTER, 0)
        t = tot[z, own, :] + jnp.concatenate([jnp.where(top, u, 0.0), gap, jnp.where(top, 0.0, d)], axis=0)
        t = t + jnp.where(rim, moved, 0.0)
        out[z] = state[z] + scale * t

    wait_send_all(copy2)


def on_device(
    sizes, state, load_vector, active, stiff_band, mass_band, eig_basis, eig_values, cut_cols, cut_inverse
):
    nz, rx, ry = state.shape
    slots = cut_cols.shape[-1]
    assert nz == HALF and ry == LANES and rx % PATCH == 0
    inverse = cut_inverse.reshape(cut_inverse.shape[2:])
    wide = rx + 2 * HALO
    full = ry + LANES
    qx, qy = (rx // HALF) * PATCH, (ry // HALF) * PATCH
    cells = PATCH * PATCH
    anyspace = pl.BlockSpec(memory_space=pltpu.HBM)
    V, S = pltpu.VMEM, pltpu.SMEM
    dma = pltpu.SemaphoreType.DMA
    n = len(DIRS)
    return pl.pallas_call(
        functools.partial(kernel, sizes),
        out_shape=pltpu.VMEM(state.shape, f32),
        in_specs=[anyspace] * 9,
        out_specs=pl.BlockSpec(memory_space=pltpu.VMEM),
        scratch_shapes=[
            V(state.shape, f32), V(load_vector.shape, load_vector.dtype), V(active.shape, active.dtype),
            S(stiff_band.shape, f32), S(mass_band.shape, f32), S(eig_basis.shape, f32),
            V(eig_basis.shape, f32), S(eig_values.shape, f32), S(cut_cols.shape, cut_cols.dtype),
            V((slots, PATCH, cells, cells), bf16),
            V((nz + 1 + nz // 2, wide, ry), f32), V((nz, wide, ry), f32),
            V((wide, LANES), f32), V((wide, LANES), f32),
            V((rx, LANES), f32), V((rx, LANES), f32),
            V((3 * full, 2 * full), bf16), V((3 * full, qy), bf16), V((3 * qy, full), bf16),
            V((slots, full, cells), bf16), V((slots, cells, full), bf16),
            V((PATCH, qx, qy), f32),
            V((nz, wide, full), f32), V((slots, nz, PATCH + HALF, full), f32),
            V((nz, wide, ry), f32), V((nz, wide, ry), f32),
            V((nz * wide, 3 * full), bf16), V((nz * wide, 3 * full), bf16),
            V((PATCH * wide, 3 * full), bf16), V((PATCH * wide, 3 * qy), bf16),
            V((nz, wide, ry), f32), V((wide, LANES), f32),
            V((2, nz // 2, HALO, ry), f32),
            V((nz // 2, HALO, ry), f32), V((nz // 2, HALO, ry), f32),
            V((rx, LANES), f32), V((rx, LANES), f32),
            V((4, HALO, LANES), f32),
            dma((10,)), dma((n,)), dma((n,)), dma((n,)), dma((n,)),
        ],
        compiler_params=pltpu.CompilerParams(
            collective_id=0, has_side_effects=True, vmem_limit_bytes=56 * 1024 * 1024
        ),
    )(state, load_vector, active, stiff_band, mass_band, eig_basis, eig_values, cut_cols, inverse)


def solution(mesh):
    placed = (
        P(None, "gx", "gy"),
        P(None, "gx", "gy"),
        P("gx", "gy"),
        P(),
        P(),
        P(),
        P(),
        P("gx", "gy", None),
        P("gx", "gy", None, None, None, None),
    )
    sizes = (mesh.shape["gx"], mesh.shape["gy"])
    return jax.shard_map(
        functools.partial(on_device, sizes),
        mesh=mesh, in_specs=placed, out_specs=P(None, "gx", "gy"), check_vma=False,
    )
```

```python
import functools

import jax
import jax.numpy as jnp
from jax import lax
from jax.experimental import pallas as pl
from jax.experimental.pallas import tpu as pltpu
from jax.sharding import PartitionSpec as P

BAND = 4
PATCH = 16
HALF = PATCH // 2
QUARTER = PATCH // 4
HALO = BAND + QUARTER
LANES = 128
MESH = pl.DeviceIdType.MESH
DIRS = [(1, 0), (-1, 0), (1, 1), (1, -1), (-1, 1), (-1, -1), (0, 1), (0, -1)]

damping = 0.5
f32 = jnp.float32
bf16 = jnp.bfloat16


def iota(shape, dim):
    return lax.broadcasted_iota(jnp.int32, shape, dim)


def split(v):
    hi = v.astype(bf16)
    return hi, (v - hi.astype(f32)).astype(bf16)


def dot(a, b):
    return jnp.dot(a, b, preferred_element_type=f32)


def dot_nt(a, b):
    return lax.dot_general(a, b, (((1,), (1,)), ((), ())), preferred_element_type=f32)


def band_of(distance, taps):
    out = jnp.zeros(distance.shape, f32)
    for k in range(BAND + 1):
        out = jnp.where(distance == k, taps[k], out)
    return out


def inner_y(c, ry):
    u = (c - ry) & (HALF - 1)
    halo = jnp.where(u < QUARTER, u - QUARTER, ry + u - QUARTER)
    return jnp.where(c < ry, c, jnp.where(c < ry + LANES // 2, -1000, halo))


def outer_y(r, ry):
    u = (r - ry) & (HALF - 1)
    return jnp.where(r < ry, r, jnp.where(r < ry + LANES // 2, u - HALO, ry + u))


def wrap(v, n, reps):
    out = v
    for j in range(1, reps):
        out = out - jnp.where(v >= n * j, n, 0)
    return out


def kernel(
    sizes,
    state_h, load_h, active_h, stiff_h, mass_h, basis_h, values_h, cols_h, inverse_h,
    out,
    state, load, active, stiff, mass, basis_s, basis, values, cols, inv,
    ext, lf, from_left, from_right, pack_left, pack_right,
    yb, wy3, wyt3, sel, sel_t, dinv, rs, cw,
    zk, zm, sk3, sm3, r3, tb3, tot, edge,
    rim_x, up, down, left2, right2, corners,
    in_sem, send1, recv1, send2, recv2,
):
    n_x, n_y = sizes
    nz, rx, ry = state.shape
    wide = rx + 2 * HALO
    slots = inv.shape[0]
    blocks_x, blocks_y = rx // HALF, ry // HALF
    qx, qy = blocks_x * PATCH, blocks_y * PATCH
    full = ry + LANES
    half = LANES // 2
    groups = half // HALF
    me_x, me_y = lax.axis_index("gx"), lax.axis_index("gy")

    def exists(dx, dy):
        ok = None
        for d, me, n in ((dx, me_x, n_x), (dy, me_y, n_y)):
            if d:
                part = (me + d >= 0) & (me + d < n)
                ok = part if ok is None else ok & part
        return ok

    def device(dx, dy):
        return (jnp.clip(me_x + dx, 0, n_x - 1), jnp.clip(me_y + dy, 0, n_y - 1))

    fetches = [
        pltpu.make_async_copy(src, dst, in_sem.at[i])
        for i, (src, dst) in enumerate((
            (state_h, state), (load_h, load), (active_h, active),
            (stiff_h, stiff), (mass_h, mass), (basis_h, basis_s), (basis_h, basis),
            (values_h, values), (cols_h, cols), (inverse_h, inv),
        ))
    ]
    for fetch in fetches:
        fetch.start()

    own = pl.ds(HALO, rx)
    planes = nz + 1 + nz // 2
    zeros = jnp.zeros((planes, HALO, ry), f32)
    ext[:, pl.ds(0, HALO), :] = zeros
    ext[:, pl.ds(HALO + rx, HALO), :] = zeros
    for ref in (from_left, from_right, up, down, left2, right2, corners):
        ref[...] = jnp.zeros(ref.shape, f32)

    barrier = pltpu.get_barrier_semaphore()
    count = jnp.int32(0)
    for d in DIRS:
        ok = exists(*d)
        count = count + ok.astype(jnp.int32)

        @pl.when(ok)
        def _(d=d):
            pl.semaphore_signal(barrier, inc=1, device_id=device(*d), device_id_type=MESH)

    for fetch in fetches[:3]:
        fetch.wait()
    for z in range(nz):
        ext[z, own, :] = state[z]
        lf[z, own, :] = load[z].astype(f32)
    ext[nz, own, :] = active[...].astype(f32)
    top = iota((HALO, ry), 0) < QUARTER
    for j in range(nz // 2):
        for r, natural in ((HALO, top), (rx, ~top)):
            odd = pltpu.roll(lf[2 * j + 1, pl.ds(r, HALO), :], QUARTER, 0)
            ext[nz + 1 + j, pl.ds(r, HALO), :] = jnp.where(natural, lf[2 * j, pl.ds(r, HALO), :], odd)

    lane = iota((rx, LANES), 1)
    group = (lane & (half - 1)) >> 3
    high = lane >= half
    lows = (lane & (HALF - 1)) < QUARTER
    to_right = jnp.zeros((rx, LANES), f32)
    to_left = jnp.zeros((rx, LANES), f32)
    act = ext[nz, own, :]
    for z in range(nz):
        s = ext[z, own, :]
        l = pltpu.roll(lf[z, own, :], (half + QUARTER + HALF * z) % LANES, 1)
        mine = group == z
        first = mine & high & lows
        second = mine & high & ~lows
        to_right = jnp.where(mine & ~high, pltpu.roll(s, (HALF + HALF * z) % LANES, 1), to_right)
        to_right = jnp.where(first, l, to_right)
        to_right = jnp.where(second, pltpu.roll(act, (half + HALF + HALF * z) % LANES, 1), to_right)
        to_left = jnp.where(mine & ~high, pltpu.roll(s, HALF * z, 1) if z else s, to_left)
        to_left = jnp.where(second, l, to_left)
        to_left = jnp.where(first, pltpu.roll(act, (half + HALF * z) % LANES, 1), to_left)
    pack_right[...] = to_right
    pack_left[...] = to_left

    def copy1(i):
        dx, dy = DIRS[i]
        if dy == 0:
            src = ext.at[:, pl.ds(rx if dx > 0 else HALO, HALO), :]
            dst = ext.at[:, pl.ds(0 if dx > 0 else HALO + rx, HALO), :]
        else:
            pack = pack_right if dy > 0 else pack_left
            land = from_left if dy > 0 else from_right
            if dx == 0:
                src, dst = pack, land.at[pl.ds(HALO, rx), :]
            else:
                src = pack.at[pl.ds(rx - HALO if dx > 0 else 0, HALO), :]
                dst = land.at[pl.ds(0 if dx > 0 else HALO + rx, HALO), :]
        return pltpu.make_async_remote_copy(
            src_ref=src, dst_ref=dst, send_sem=send1.at[i], recv_sem=recv1.at[i],
            device_id=device(dx, dy), device_id_type=MESH,
        )

    def copy2(i):
        dx, dy = DIRS[i]
        if dy == 0:
            src = rim_x.at[0 if dx > 0 else 1]
            dst = up if dx > 0 else down
        elif dx == 0:
            src = edge.at[pl.ds(HALO, rx), :]
            dst = left2 if dy > 0 else right2
        else:
            src = edge.at[pl.ds(HALO + rx if dx > 0 else 0, HALO), :]
            dst = corners.at[(dx < 0) * 2 + (dy < 0)]
        return pltpu.make_async_remote_copy(
            src_ref=src, dst_ref=dst, send_sem=send2.at[i], recv_sem=recv2.at[i],
            device_id=device(dx, dy), device_id_type=MESH,
        )

    def start_all(copy):
        for i, d in enumerate(DIRS):
            @pl.when(exists(*d))
            def _(i=i):
                copy(i).start()

    def wait_recv_all(copy):
        for i, (dx, dy) in enumerate(DIRS):
            @pl.when(exists(-dx, -dy))
            def _(i=i):
                copy(i).wait_recv()

    def wait_send_all(copy):
        for i, d in enumerate(DIRS):
            @pl.when(exists(*d))
            def _(i=i):
                copy(i).wait_send()

    pl.semaphore_wait(barrier, count)
    start_all(copy1)

    for fetch in fetches[3:9]:
        fetch.wait()
    distance = jnp.abs(outer_y(iota((full, 1), 0), ry) - inner_y(iota((1, full), 1), ry))
    for j, taps in enumerate((mass, stiff)):
        h, l = split(band_of(distance, [taps[2, k] for k in range(BAND + 1)]))
        for i, part in enumerate((h, h, l)):
            yb[pl.ds(i * full, full), pl.ds(j * full, full)] = part

    highest = lax.Precision.HIGHEST
    tile_y = jnp.dot(
        basis[2], (iota((PATCH, qy), 0) == (iota((PATCH, qy), 1) & (PATCH - 1))).astype(f32),
        precision=highest, preferred_element_type=f32,
    )
    place = inner_y(iota((full, 1), 0), ry) + QUARTER - HALF * (iota((1, qy), 1) >> 4)
    wy = jnp.zeros((full, qy), f32)
    for t in range(PATCH):
        wy = jnp.where(place == t, tile_y[t : t + 1, :], wy)
    h, l = split(wy)
    for i, part in enumerate((h, h, l)):
        wy3[pl.ds(i * full, full), :] = part

    h, l = split(wy.T)
    for i, part in enumerate((h, h, l)):
        wyt3[pl.ds(i * qy, qy), :] = part

    def wx_of(shape, reps_r, reps_c):
        r, c = iota((shape[0], 1), 0), iota((1, shape[1]), 1)
        t = wrap(r, wide, reps_r) - (HALO - QUARTER) - HALF * (wrap(c, qx, reps_c) >> 4)
        t = jnp.where((r < wide * reps_r) & (c < qx * reps_c), t, -1)
        tile = jnp.dot(
            basis[1], (iota((PATCH, shape[1]), 0) == (iota((PATCH, shape[1]), 1) & (PATCH - 1))).astype(f32),
            precision=highest, preferred_element_type=f32,
        )
        w = jnp.zeros(shape, f32)
        for k in range(PATCH):
            w = jnp.where(t == k, tile[k : k + 1, :], w)
        return w

    def split3(v, width):
        h, l = split(v)
        return jnp.where(iota((1, v.shape[1]), 1) < 2 * width, h.astype(f32), l.astype(f32)).astype(bf16)

    pad_r = -(-3 * wide // LANES) * LANES
    pad_c = -(-qx // LANES) * LANES
    g3 = split3(wx_of((pad_r, pad_c), 3, 1).T[:qx, : 3 * wide], wide)
    b3 = split3(wx_of((wide, 3 * qx), 1, 3), qx)

    c = iota((1, 4 * wide), 1)
    dist_x = jnp.abs(iota((wide, 1), 0) - wrap(c, wide, 4))
    bx = jnp.where(
        (c < wide) | ((c >= 2 * wide) & (c < 3 * wide)),
        band_of(dist_x, [mass[1, k] for k in range(BAND + 1)]),
        band_of(dist_x, [stiff[1, k] for k in range(BAND + 1)]),
    )
    bx_hi, bx_lo = split(bx)
    bx_lo = bx_lo[:, : 2 * wide]

    cells = PATCH * PATCH
    cut = [cols[0, 0, m] for m in range(slots)]
    cut_a = [lax.div(jnp.maximum(v, 0), jnp.int32(blocks_y)) for v in cut]
    cut_b = [lax.rem(jnp.maximum(v, 0), jnp.int32(blocks_y)) for v in cut]
    y_in = inner_y(iota((full, 1), 0), ry)
    y_to = iota((1, cells), 1) & (PATCH - 1)
    y_in_t = inner_y(iota((1, full), 1), ry)
    y_to_t = iota((cells, 1), 0) & (PATCH - 1)
    for m in range(slots):
        sel[m] = jnp.where(y_in + QUARTER - HALF * cut_b[m] == y_to, 1.0, 0.0).astype(bf16)
        sel_t[m] = jnp.where(y_in_t + QUARTER - HALF * cut_b[m] == y_to_t, 1.0, 0.0).astype(bf16)

    near = PATCH + HALF
    spot = iota((near, 1), 0) - QUARTER == (iota((1, cells), 1) >> 4)
    vz_t = []
    for z in range(nz):
        v = jnp.zeros((PATCH, 1), f32)
        for k in range(PATCH):
            v = jnp.where(iota((PATCH, 1), 0) == k, basis_s[0, QUARTER + z, k], v)
        vz_t.append(v)

    def pick(shape, dim, row):
        index = iota(shape, dim) & (PATCH - 1)
        v = jnp.zeros(shape, f32)
        for k in range(PATCH):
            v = jnp.where(index == k, values[row, k], v)
        return v

    lam = pick((qx, 1), 0, 1) + pick((1, qy), 1, 2)
    column = (iota((qx, 1), 0) >> 4) * blocks_y + (iota((1, qy), 1) >> 4)
    keep = jnp.ones((qx, qy), f32)
    for m in range(slots):
        keep = jnp.where(column == cut[m], 0.0, keep)
    for k in range(PATCH):
        dinv[k] = keep / (values[0, k] + lam)

    lane1 = iota((1, LANES), 1)
    group1 = (lane1 & (half - 1)) >> 3
    far = [jnp.abs(group1 - z) for z in range(nz)]
    k_vec = [band_of(far[z], [stiff[0, k] for k in range(BAND + 1)]) for z in range(nz)]
    m_vec = [band_of(far[z], [mass[0, k] for k in range(BAND + 1)]) for z in range(nz)]
    v_vec = []
    for k in range(PATCH):
        v = jnp.zeros((1, LANES), f32)
        for z in range(nz):
            v = jnp.where((group1 == z) & (lane1 >= half), basis_s[0, QUARTER + z, k], v)
        v_vec.append(v)

    def put3(ref, rows, start, width, v):
        h, l = split(v)
        for i, part in enumerate((h, l, h)):
            ref[rows, pl.ds(i * width + start, v.shape[1])] = part

    def mix_z(start, count):
        for r in range(start, start + count, HALF):
            rows = pl.ds(r, HALF)
            s = [ext[z, rows, :] for z in range(nz)]
            for z in range(nz):
                p = q = None
                for w in range(nz):
                    k = abs(z - w)
                    if k > BAND:
                        continue
                    a, b = stiff[0, k] * s[w], mass[0, k] * s[w]
                    p = a if p is None else p + a
                    q = b if q is None else q + b
                zk[z, rows, :] = p
                zm[z, rows, :] = q

    mix_z(HALO, rx)
    fetches[9].wait()
    wait_recv_all(copy1)
    mix_z(0, HALO)
    mix_z(HALO + rx, HALO)

    lane_w = iota((wide, LANES), 1)
    group_w = (lane_w & (half - 1)) >> 3
    halo_l, halo_r = from_left[...], from_right[...]
    comb = jnp.where(lane_w < half, halo_l, pltpu.roll(halo_r, half, 1))
    low = (lane_w & (HALF - 1)) < QUARTER
    load_t = jnp.where(low, halo_l, halo_r)
    act_t = jnp.where(low, pltpu.roll(halo_l, LANES - QUARTER, 1), pltpu.roll(halo_r, QUARTER, 1))
    act_t = jnp.where(lane_w >= half, act_t, 0.0)
    act_w = ext[nz]
    for z in range(nz):
        for r in (0, HALO + rx):
            tile = ext[nz + 1 + z // 2, pl.ds(r, HALO), :]
            lf[z, pl.ds(r, HALO), :] = pltpu.roll(tile, QUARTER, 0) if z % 2 else tile
    r0 = []
    r1 = jnp.zeros((wide, LANES), f32)
    part_z = nz // 2

    def spread_y(g):
        for z in range(g * part_z, (g + 1) * part_z):
            rows = pl.ds(z * wide, wide)
            for s3, mixed, vec in ((sk3, zk, k_vec), (sm3, zm, m_vec)):
                put3(s3, rows, 0, full, mixed[z])
                put3(s3, rows, ry, full, comb * vec[z])

    def band_y(g):
        rows = pl.ds(g * part_z * wide, part_z * wide)
        ym = dot(sm3[rows, :], yb[...])
        return ym[:, :full], ym[:, full:] + dot(sk3[rows, :], yb[:, pl.ds(0, full)])

    def band_x(g, ym, yp, r1):
        for i in range(part_z):
            z = g * part_z + i
            p_hi, p_lo = split(yp[i * wide : (i + 1) * wide])
            q_hi, q_lo = split(ym[i * wide : (i + 1) * wide])
            applied = dot(bx_hi, jnp.concatenate([p_hi, q_hi, p_lo, q_lo], axis=0))
            applied = applied + dot(bx_lo, jnp.concatenate([p_hi, q_hi], axis=0))
            r0.append(act_w * (lf[z] - applied[:, :ry]))
            r1 = jnp.where(group_w == z, applied[:, ry:], r1)
        return r1

    spread_y(0)
    first_half = band_y(0)
    spread_y(1)
    second_half = band_y(1)
    r1 = band_x(0, *first_half, r1)
    r1 = band_x(1, *second_half, r1)
    r1 = act_t * (load_t - r1)

    per = PATCH // 4
    vz = basis[0, pl.ds(QUARTER, nz), :]
    t1, fast = {}, {}
    zmodes, corr = {}, {}

    def to_modes(g):
        for k in range(g * per, (g + 1) * per):
            rows = pl.ds(k * wide, wide)
            v = None
            for z in range(nz):
                term = basis_s[0, QUARTER + z, k] * r0[z]
                v = term if v is None else v + term
            put3(r3, rows, 0, full, v)
            put3(r3, rows, ry, full, r1 * v_vec[k])

    def to_y(g):
        t1[g] = dot(r3[pl.ds(g * per * wide, per * wide), :], wy3[...])

    def solve_x(g):
        for i in range(per):
            k = g * per + i
            h, l = split(t1[g][i * wide : (i + 1) * wide])
            h, l = split(dot(g3, jnp.concatenate([h, l, h], axis=0)) * dinv[k])
            back = dot(b3, jnp.concatenate([h, l, h], axis=0))
            put3(tb3, pl.ds(k * wide, wide), 0, qy, back)

    def from_y(g):
        fast[g] = dot(tb3[pl.ds(g * per * wide, per * wide), :], wyt3[...])

    def cut_take(m):
        window = rs[:, pl.ds(0, near), :]
        for a in range(1, blocks_x):
            window = jnp.where(cut_a[m] == a, rs[:, pl.ds(a * HALF, near), :], window)
        h, l = split(window.reshape(nz * near, full))
        taken = (dot(h, sel[m]) + dot(l, sel[m])).reshape(nz, near, cells)
        patch = jnp.sum(jnp.where(spot[None], taken, 0.0), axis=1)
        modes = None
        for z in range(nz):
            term = vz_t[z] * patch[z : z + 1, :]
            modes = term if modes is None else modes + term
        zmodes[m] = modes.astype(bf16)

    def cut_solve(m):
        c = jnp.zeros((nz, cells), f32)
        for k in range(PATCH):
            c = c + vz[:, k : k + 1] * dot_nt(zmodes[m], inv[m, k])[k : k + 1, :]
        corr[m] = jnp.where(cut[m] >= 0, c, 0.0)

    def cut_place(m):
        h, l = split(jnp.where(spot[None], corr[m][:, None, :], 0.0).reshape(nz * near, cells))
        cw[m] = (dot(h, sel_t[m]) + dot(l, sel_t[m])).reshape(nz, near, full)

    def per_slot(step):
        for m in range(slots):
            step(m)

    to_modes(0)
    to_y(0)
    for z in range(nz):
        rs[z, :, pl.ds(0, ry)] = r0[z]
        rs[z, :, pl.ds(ry, LANES)] = jnp.where(group_w == z, r1, 0.0)
    to_modes(1)
    per_slot(cut_take)
    to_y(1)
    solve_x(0)
    to_modes(2)
    to_y(2)
    solve_x(1)
    from_y(0)
    to_modes(3)
    per_slot(cut_solve)
    to_y(3)
    solve_x(2)
    from_y(1)
    per_slot(cut_place)
    solve_x(3)
    from_y(2)
    from_y(3)

    def fast_rows(k):
        return fast[k // per][(k % per) * wide : (k % per + 1) * wide]

    def cut_part(z, start, count, lanes):
        tiles = []
        for r in range(start // HALF, (start + count) // HALF):
            out = jnp.zeros((HALF, LANES), f32)
            for m in range(slots):
                for a in range(blocks_x):
                    if 0 <= r - a < near // HALF:
                        out = out + jnp.where(cut_a[m] == a, cw[m, z, pl.ds((r - a) * HALF, HALF), lanes], 0.0)
            tiles.append(out)
        return jnp.concatenate(tiles, axis=0)

    def total_rows(z, start, count):
        t = cut_part(z, start, count, pl.ds(0, ry))
        for k in range(PATCH):
            t = t + basis_s[0, QUARTER + z, k] * fast_rows(k)[start : start + count, :ry]
        tot[z, pl.ds(start, count), :] = t

    packed = jnp.zeros((wide, LANES), f32)
    for z in range(nz):
        packed = jnp.where(group_w == z, cut_part(z, 0, wide, pl.ds(ry, LANES)), packed)
    for k in range(PATCH):
        packed = packed + v_vec[k] * fast_rows(k)[:, ry:]
    edge[...] = packed
    for z in range(nz):
        total_rows(z, 0, HALO)
        total_rows(z, HALO + rx, HALO)
    for j in range(nz // 2):
        for i, r, natural in ((0, HALO + rx, top), (1, 0, ~top)):
            odd = pltpu.roll(tot[2 * j + 1, pl.ds(r, HALO), :], QUARTER, 0)
            rim_x[i, j] = jnp.where(natural, tot[2 * j, pl.ds(r, HALO), :], odd)

    start_all(copy2)
    for z in range(nz):
        total_rows(z, HALO, rx)
    wait_send_all(copy1)
    wait_recv_all(copy2)

    gap = jnp.zeros((rx - 2 * HALO, LANES), f32)
    l2 = left2[...] + jnp.concatenate([corners[0], gap, corners[2]], axis=0)
    r2 = right2[...] + jnp.concatenate([corners[1], gap, corners[3]], axis=0)
    both = jnp.where(lows, r2, l2)
    rim = (lane < QUARTER) | (lane >= ry - QUARTER)
    scale = damping * ext[nz, own, :]
    for z in range(nz):
        moved = pltpu.roll(both, (LANES - QUARTER - half - HALF * z) % LANES, 1)
        u, d = up[z // 2], down[z // 2]
        if z % 2:
            u, d = pltpu.roll(u, QUARTER, 0), pltpu.roll(d, QUARTER, 0)
        t = tot[z, own, :] + jnp.concatenate([jnp.where(top, u, 0.0), gap, jnp.where(top, 0.0, d)], axis=0)
        t = t + jnp.where(rim, moved, 0.0)
        out[z] = state[z] + scale * t

    wait_send_all(copy2)


def on_device(
    sizes, state, load_vector, active, stiff_band, mass_band, eig_basis, eig_values, cut_cols, cut_inverse
):
    nz, rx, ry = state.shape
    slots = cut_cols.shape[-1]
    assert nz == HALF and ry == LANES and rx % PATCH == 0
    inverse = cut_inverse.reshape(cut_inverse.shape[2:])
    wide = rx + 2 * HALO
    full = ry + LANES
    qx, qy = (rx // HALF) * PATCH, (ry // HALF) * PATCH
    cells = PATCH * PATCH
    anyspace = pl.BlockSpec(memory_space=pltpu.HBM)
    V, S = pltpu.VMEM, pltpu.SMEM
    dma = pltpu.SemaphoreType.DMA
    n = len(DIRS)
    return pl.pallas_call(
        functools.partial(kernel, sizes),
        out_shape=pltpu.VMEM(state.shape, f32),
        in_specs=[anyspace] * 9,
        out_specs=pl.BlockSpec(memory_space=pltpu.VMEM),
        scratch_shapes=[
            V(state.shape, f32), V(load_vector.shape, load_vector.dtype), V(active.shape, active.dtype),
            S(stiff_band.shape, f32), S(mass_band.shape, f32), S(eig_basis.shape, f32),
            V(eig_basis.shape, f32), S(eig_values.shape, f32), S(cut_cols.shape, cut_cols.dtype),
            V((slots, PATCH, cells, cells), bf16),
            V((nz + 1 + nz // 2, wide, ry), f32), V((nz, wide, ry), f32),
            V((wide, LANES), f32), V((wide, LANES), f32),
            V((rx, LANES), f32), V((rx, LANES), f32),
            V((3 * full, 2 * full), bf16), V((3 * full, qy), bf16), V((3 * qy, full), bf16),
            V((slots, full, cells), bf16), V((slots, cells, full), bf16),
            V((PATCH, qx, qy), f32),
            V((nz, wide, full), f32), V((slots, nz, PATCH + HALF, full), f32),
            V((nz, wide, ry), f32), V((nz, wide, ry), f32),
            V((nz * wide, 3 * full), bf16), V((nz * wide, 3 * full), bf16),
            V((PATCH * wide, 3 * full), bf16), V((PATCH * wide, 3 * qy), bf16),
            V((nz, wide, ry), f32), V((wide, LANES), f32),
            V((2, nz // 2, HALO, ry), f32),
            V((nz // 2, HALO, ry), f32), V((nz // 2, HALO, ry), f32),
            V((rx, LANES), f32), V((rx, LANES), f32),
            V((4, HALO, LANES), f32),
            dma((10,)), dma((n,)), dma((n,)), dma((n,)), dma((n,)),
        ],
        compiler_params=pltpu.CompilerParams(
            collective_id=0, has_side_effects=True, vmem_limit_bytes=56 * 1024 * 1024
        ),
    )(state, load_vector, active, stiff_band, mass_band, eig_basis, eig_values, cut_cols, inverse)


def solution(mesh):
    placed = (
        P(None, "gx", "gy"),
        P(None, "gx", "gy"),
        P("gx", "gy"),
        P(),
        P(),
        P(),
        P(),
        P("gx", "gy", None),
        P("gx", "gy", None, None, None, None),
    )
    sizes = (mesh.shape["gx"], mesh.shape["gy"])
    return jax.shard_map(
        functools.partial(on_device, sizes),
        mesh=mesh, in_specs=placed, out_specs=P(None, "gx", "gy"), check_vma=False,
    )
```

```python
import functools

import jax
import jax.numpy as jnp
from jax import lax
from jax.experimental import pallas as pl
from jax.experimental.pallas import tpu as pltpu
from jax.sharding import PartitionSpec as P

BAND = 4
PATCH = 16
HALF = PATCH // 2
QUARTER = PATCH // 4
HALO = BAND + QUARTER
LANES = 128
MESH = pl.DeviceIdType.MESH
DIRS = [(1, 0), (-1, 0), (1, 1), (1, -1), (-1, 1), (-1, -1), (0, 1), (0, -1)]

damping = 0.5
f32 = jnp.float32
bf16 = jnp.bfloat16


def iota(shape, dim):
    return lax.broadcasted_iota(jnp.int32, shape, dim)


def split(v):
    hi = v.astype(bf16)
    return hi, (v - hi.astype(f32)).astype(bf16)


def dot(a, b):
    return jnp.dot(a, b, preferred_element_type=f32)


def dot_nt(a, b):
    return lax.dot_general(a, b, (((1,), (1,)), ((), ())), preferred_element_type=f32)


def band_of(distance, taps):
    out = jnp.zeros(distance.shape, f32)
    for k in range(BAND + 1):
        out = jnp.where(distance == k, taps[k], out)
    return out


def inner_y(c, ry):
    u = (c - ry) & (HALF - 1)
    halo = jnp.where(u < QUARTER, u - QUARTER, ry + u - QUARTER)
    return jnp.where(c < ry, c, jnp.where(c < ry + LANES // 2, -1000, halo))


def outer_y(r, ry):
    u = (r - ry) & (HALF - 1)
    return jnp.where(r < ry, r, jnp.where(r < ry + LANES // 2, u - HALO, ry + u))


def wrap(v, n, reps):
    out = v
    for j in range(1, reps):
        out = out - jnp.where(v >= n * j, n, 0)
    return out


def kernel(
    sizes,
    state_h, load_h, active_h, stiff_h, mass_h, basis_h, values_h, cols_h, inverse_h,
    out,
    state, load, active, stiff, mass, basis_s, basis, values, cols, inv,
    ext, lf, from_left, from_right, pack_left, pack_right,
    yb, wy3, wyt3, sel, sel_t, dinv, rs, cw,
    zk, zm, sk3, sm3, r3, tb3, tot, edge,
    rim_x, up, down, left2, right2, corners,
    in_sem, send1, recv1, send2, recv2,
):
    n_x, n_y = sizes
    nz, rx, ry = state.shape
    wide = rx + 2 * HALO
    slots = inv.shape[0]
    blocks_x, blocks_y = rx // HALF, ry // HALF
    qx, qy = blocks_x * PATCH, blocks_y * PATCH
    full = ry + LANES
    half = LANES // 2
    groups = half // HALF
    me_x, me_y = lax.axis_index("gx"), lax.axis_index("gy")

    def exists(dx, dy):
        ok = None
        for d, me, n in ((dx, me_x, n_x), (dy, me_y, n_y)):
            if d:
                part = (me + d >= 0) & (me + d < n)
                ok = part if ok is None else ok & part
        return ok

    def device(dx, dy):
        return (jnp.clip(me_x + dx, 0, n_x - 1), jnp.clip(me_y + dy, 0, n_y - 1))

    fetches = [
        pltpu.make_async_copy(src, dst, in_sem.at[i])
        for i, (src, dst) in enumerate((
            (state_h, state), (load_h, load), (active_h, active),
            (stiff_h, stiff), (mass_h, mass), (basis_h, basis_s), (basis_h, basis),
            (values_h, values), (cols_h, cols), (inverse_h, inv),
        ))
    ]
    for fetch in fetches[:3]:
        fetch.start()

    own = pl.ds(HALO, rx)
    planes = nz + 1 + nz // 2
    zeros = jnp.zeros((planes, HALO, ry), f32)
    ext[:, pl.ds(0, HALO), :] = zeros
    ext[:, pl.ds(HALO + rx, HALO), :] = zeros
    for ref in (from_left, from_right, up, down, left2, right2, corners):
        ref[...] = jnp.zeros(ref.shape, f32)

    barrier = pltpu.get_barrier_semaphore()
    count = jnp.int32(0)
    for d in DIRS:
        ok = exists(*d)
        count = count + ok.astype(jnp.int32)

        @pl.when(ok)
        def _(d=d):
            pl.semaphore_signal(barrier, inc=1, device_id=device(*d), device_id_type=MESH)

    for fetch in fetches[3:]:
        fetch.start()
    for fetch in fetches[:3]:
        fetch.wait()
    for z in range(nz):
        ext[z, own, :] = state[z]
        lf[z, own, :] = load[z].astype(f32)
    ext[nz, own, :] = active[...].astype(f32)
    top = iota((HALO, ry), 0) < QUARTER
    for j in range(nz // 2):
        for r, natural in ((HALO, top), (rx, ~top)):
            odd = pltpu.roll(lf[2 * j + 1, pl.ds(r, HALO), :], QUARTER, 0)
            ext[nz + 1 + j, pl.ds(r, HALO), :] = jnp.where(natural, lf[2 * j, pl.ds(r, HALO), :], odd)

    lane = iota((rx, LANES), 1)
    group = (lane & (half - 1)) >> 3
    high = lane >= half
    lows = (lane & (HALF - 1)) < QUARTER
    to_right = jnp.zeros((rx, LANES), f32)
    to_left = jnp.zeros((rx, LANES), f32)
    act = ext[nz, own, :]
    for z in range(nz):
        s = ext[z, own, :]
        l = pltpu.roll(lf[z, own, :], (half + QUARTER + HALF * z) % LANES, 1)
        mine = group == z
        first = mine & high & lows
        second = mine & high & ~lows
        to_right = jnp.where(mine & ~high, pltpu.roll(s, (HALF + HALF * z) % LANES, 1), to_right)
        to_right = jnp.where(first, l, to_right)
        to_right = jnp.where(second, pltpu.roll(act, (half + HALF + HALF * z) % LANES, 1), to_right)
        to_left = jnp.where(mine & ~high, pltpu.roll(s, HALF * z, 1) if z else s, to_left)
        to_left = jnp.where(second, l, to_left)
        to_left = jnp.where(first, pltpu.roll(act, (half + HALF * z) % LANES, 1), to_left)
    pack_right[...] = to_right
    pack_left[...] = to_left

    def copy1(i):
        dx, dy = DIRS[i]
        if dy == 0:
            src = ext.at[:, pl.ds(rx if dx > 0 else HALO, HALO), :]
            dst = ext.at[:, pl.ds(0 if dx > 0 else HALO + rx, HALO), :]
        else:
            pack = pack_right if dy > 0 else pack_left
            land = from_left if dy > 0 else from_right
            if dx == 0:
                src, dst = pack, land.at[pl.ds(HALO, rx), :]
            else:
                src = pack.at[pl.ds(rx - HALO if dx > 0 else 0, HALO), :]
                dst = land.at[pl.ds(0 if dx > 0 else HALO + rx, HALO), :]
        return pltpu.make_async_remote_copy(
            src_ref=src, dst_ref=dst, send_sem=send1.at[i], recv_sem=recv1.at[i],
            device_id=device(dx, dy), device_id_type=MESH,
        )

    def copy2(i):
        dx, dy = DIRS[i]
        if dy == 0:
            src = rim_x.at[0 if dx > 0 else 1]
            dst = up if dx > 0 else down
        elif dx == 0:
            src = edge.at[pl.ds(HALO, rx), :]
            dst = left2 if dy > 0 else right2
        else:
            src = edge.at[pl.ds(HALO + rx if dx > 0 else 0, HALO), :]
            dst = corners.at[(dx < 0) * 2 + (dy < 0)]
        return pltpu.make_async_remote_copy(
            src_ref=src, dst_ref=dst, send_sem=send2.at[i], recv_sem=recv2.at[i],
            device_id=device(dx, dy), device_id_type=MESH,
        )

    def start_all(copy):
        for i, d in enumerate(DIRS):
            @pl.when(exists(*d))
            def _(i=i):
                copy(i).start()

    def wait_recv_all(copy):
        for i, (dx, dy) in enumerate(DIRS):
            @pl.when(exists(-dx, -dy))
            def _(i=i):
                copy(i).wait_recv()

    def wait_send_all(copy):
        for i, d in enumerate(DIRS):
            @pl.when(exists(*d))
            def _(i=i):
                copy(i).wait_send()

    pl.semaphore_wait(barrier, count)
    start_all(copy1)

    for fetch in fetches[3:9]:
        fetch.wait()
    distance = jnp.abs(outer_y(iota((full, 1), 0), ry) - inner_y(iota((1, full), 1), ry))
    for j, taps in enumerate((mass, stiff)):
        h, l = split(band_of(distance, [taps[2, k] for k in range(BAND + 1)]))
        for i, part in enumerate((h, h, l)):
            yb[pl.ds(i * full, full), pl.ds(j * full, full)] = part

    highest = lax.Precision.HIGHEST
    tile_y = jnp.dot(
        basis[2], (iota((PATCH, qy), 0) == (iota((PATCH, qy), 1) & (PATCH - 1))).astype(f32),
        precision=highest, preferred_element_type=f32,
    )
    place = inner_y(iota((full, 1), 0), ry) + QUARTER - HALF * (iota((1, qy), 1) >> 4)
    wy = jnp.zeros((full, qy), f32)
    for t in range(PATCH):
        wy = jnp.where(place == t, tile_y[t : t + 1, :], wy)
    h, l = split(wy)
    for i, part in enumerate((h, h, l)):
        wy3[pl.ds(i * full, full), :] = part

    h, l = split(wy.T)
    for i, part in enumerate((h, h, l)):
        wyt3[pl.ds(i * qy, qy), :] = part

    def wx_of(shape, reps_r, reps_c):
        r, c = iota((shape[0], 1), 0), iota((1, shape[1]), 1)
        t = wrap(r, wide, reps_r) - (HALO - QUARTER) - HALF * (wrap(c, qx, reps_c) >> 4)
        t = jnp.where((r < wide * reps_r) & (c < qx * reps_c), t, -1)
        tile = jnp.dot(
            basis[1], (iota((PATCH, shape[1]), 0) == (iota((PATCH, shape[1]), 1) & (PATCH - 1))).astype(f32),
            precision=highest, preferred_element_type=f32,
        )
        w = jnp.zeros(shape, f32)
        for k in range(PATCH):
            w = jnp.where(t == k, tile[k : k + 1, :], w)
        return w

    def split3(v, width):
        h, l = split(v)
        return jnp.where(iota((1, v.shape[1]), 1) < 2 * width, h.astype(f32), l.astype(f32)).astype(bf16)

    pad_r = -(-3 * wide // LANES) * LANES
    pad_c = -(-qx // LANES) * LANES
    g3 = split3(wx_of((pad_r, pad_c), 3, 1).T[:qx, : 3 * wide], wide)
    b3 = split3(wx_of((wide, 3 * qx), 1, 3), qx)

    c = iota((1, 4 * wide), 1)
    dist_x = jnp.abs(iota((wide, 1), 0) - wrap(c, wide, 4))
    bx = jnp.where(
        (c < wide) | ((c >= 2 * wide) & (c < 3 * wide)),
        band_of(dist_x, [mass[1, k] for k in range(BAND + 1)]),
        band_of(dist_x, [stiff[1, k] for k in range(BAND + 1)]),
    )
    bx_hi, bx_lo = split(bx)
    bx_lo = bx_lo[:, : 2 * wide]

    cells = PATCH * PATCH
    cut = [cols[0, 0, m] for m in range(slots)]
    cut_a = [lax.div(jnp.maximum(v, 0), jnp.int32(blocks_y)) for v in cut]
    cut_b = [lax.rem(jnp.maximum(v, 0), jnp.int32(blocks_y)) for v in cut]
    y_in = inner_y(iota((full, 1), 0), ry)
    y_to = iota((1, cells), 1) & (PATCH - 1)
    y_in_t = inner_y(iota((1, full), 1), ry)
    y_to_t = iota((cells, 1), 0) & (PATCH - 1)
    for m in range(slots):
        sel[m] = jnp.where(y_in + QUARTER - HALF * cut_b[m] == y_to, 1.0, 0.0).astype(bf16)
        sel_t[m] = jnp.where(y_in_t + QUARTER - HALF * cut_b[m] == y_to_t, 1.0, 0.0).astype(bf16)

    near = PATCH + HALF
    spot = iota((near, 1), 0) - QUARTER == (iota((1, cells), 1) >> 4)
    vz_t = []
    for z in range(nz):
        v = jnp.zeros((PATCH, 1), f32)
        for k in range(PATCH):
            v = jnp.where(iota((PATCH, 1), 0) == k, basis_s[0, QUARTER + z, k], v)
        vz_t.append(v)

    def pick(shape, dim, row):
        index = iota(shape, dim) & (PATCH - 1)
        v = jnp.zeros(shape, f32)
        for k in range(PATCH):
            v = jnp.where(index == k, values[row, k], v)
        return v

    lam = pick((qx, 1), 0, 1) + pick((1, qy), 1, 2)
    column = (iota((qx, 1), 0) >> 4) * blocks_y + (iota((1, qy), 1) >> 4)
    keep = jnp.ones((qx, qy), f32)
    for m in range(slots):
        keep = jnp.where(column == cut[m], 0.0, keep)
    for k in range(PATCH):
        dinv[k] = keep / (values[0, k] + lam)

    lane1 = iota((1, LANES), 1)
    group1 = (lane1 & (half - 1)) >> 3
    far = [jnp.abs(group1 - z) for z in range(nz)]
    k_vec = [band_of(far[z], [stiff[0, k] for k in range(BAND + 1)]) for z in range(nz)]
    m_vec = [band_of(far[z], [mass[0, k] for k in range(BAND + 1)]) for z in range(nz)]
    v_vec = []
    for k in range(PATCH):
        v = jnp.zeros((1, LANES), f32)
        for z in range(nz):
            v = jnp.where((group1 == z) & (lane1 >= half), basis_s[0, QUARTER + z, k], v)
        v_vec.append(v)

    def put3(ref, rows, start, width, v):
        h, l = split(v)
        for i, part in enumerate((h, l, h)):
            ref[rows, pl.ds(i * width + start, v.shape[1])] = part

    def mix_z(start, count):
        for r in range(start, start + count, HALF):
            rows = pl.ds(r, HALF)
            s = [ext[z, rows, :] for z in range(nz)]
            for z in range(nz):
                p = q = None
                for w in range(nz):
                    k = abs(z - w)
                    if k > BAND:
                        continue
                    a, b = stiff[0, k] * s[w], mass[0, k] * s[w]
                    p = a if p is None else p + a
                    q = b if q is None else q + b
                zk[z, rows, :] = p
                zm[z, rows, :] = q

    mix_z(HALO, rx)
    fetches[9].wait()
    wait_recv_all(copy1)
    mix_z(0, HALO)
    mix_z(HALO + rx, HALO)

    lane_w = iota((wide, LANES), 1)
    group_w = (lane_w & (half - 1)) >> 3
    halo_l, halo_r = from_left[...], from_right[...]
    comb = jnp.where(lane_w < half, halo_l, pltpu.roll(halo_r, half, 1))
    low = (lane_w & (HALF - 1)) < QUARTER
    load_t = jnp.where(low, halo_l, halo_r)
    act_t = jnp.where(low, pltpu.roll(halo_l, LANES - QUARTER, 1), pltpu.roll(halo_r, QUARTER, 1))
    act_t = jnp.where(lane_w >= half, act_t, 0.0)
    act_w = ext[nz]
    for z in range(nz):
        for r in (0, HALO + rx):
            tile = ext[nz + 1 + z // 2, pl.ds(r, HALO), :]
            lf[z, pl.ds(r, HALO), :] = pltpu.roll(tile, QUARTER, 0) if z % 2 else tile
    r0 = []
    r1 = jnp.zeros((wide, LANES), f32)
    part_z = nz // 4

    def spread_y(g):
        for z in range(g * part_z, (g + 1) * part_z):
            rows = pl.ds(z * wide, wide)
            for s3, mixed, vec in ((sk3, zk, k_vec), (sm3, zm, m_vec)):
                put3(s3, rows, 0, full, mixed[z])
                put3(s3, rows, ry, full, comb * vec[z])

    def band_y(g):
        rows = pl.ds(g * part_z * wide, part_z * wide)
        ym = dot(sm3[rows, :], yb[...])
        return ym[:, :full], ym[:, full:] + dot(sk3[rows, :], yb[:, pl.ds(0, full)])

    def band_x(g, ym, yp, r1):
        for i in range(part_z):
            z = g * part_z + i
            p_hi, p_lo = split(yp[i * wide : (i + 1) * wide])
            q_hi, q_lo = split(ym[i * wide : (i + 1) * wide])
            applied = dot(bx_hi, jnp.concatenate([p_hi, q_hi, p_lo, q_lo], axis=0))
            applied = applied + dot(bx_lo, jnp.concatenate([p_hi, q_hi], axis=0))
            r0.append(act_w * (lf[z] - applied[:, :ry]))
            r1 = jnp.where(group_w == z, applied[:, ry:], r1)
        return r1

    parts = nz // part_z
    bands = []
    spread_y(0)
    for g in range(parts):
        bands.append(band_y(g))
        if g + 1 < parts:
            spread_y(g + 1)
        if g:
            r1 = band_x(g - 1, *bands[g - 1], r1)
    r1 = band_x(parts - 1, *bands[-1], r1)
    r1 = act_t * (load_t - r1)

    per = PATCH // 4
    vz = basis[0, pl.ds(QUARTER, nz), :]
    t1, fast = {}, {}
    zmodes, corr = {}, {}

    def to_modes(g):
        for k in range(g * per, (g + 1) * per):
            rows = pl.ds(k * wide, wide)
            v = None
            for z in range(nz):
                term = basis_s[0, QUARTER + z, k] * r0[z]
                v = term if v is None else v + term
            put3(r3, rows, 0, full, v)
            put3(r3, rows, ry, full, r1 * v_vec[k])

    def to_y(g):
        t1[g] = dot(r3[pl.ds(g * per * wide, per * wide), :], wy3[...])

    def solve_x(g):
        for i in range(per):
            k = g * per + i
            h, l = split(t1[g][i * wide : (i + 1) * wide])
            h, l = split(dot(g3, jnp.concatenate([h, l, h], axis=0)) * dinv[k])
            back = dot(b3, jnp.concatenate([h, l, h], axis=0))
            put3(tb3, pl.ds(k * wide, wide), 0, qy, back)

    def from_y(g):
        fast[g] = dot(tb3[pl.ds(g * per * wide, per * wide), :], wyt3[...])

    def cut_take(m):
        window = rs[:, pl.ds(0, near), :]
        for a in range(1, blocks_x):
            window = jnp.where(cut_a[m] == a, rs[:, pl.ds(a * HALF, near), :], window)
        h, l = split(window.reshape(nz * near, full))
        taken = (dot(h, sel[m]) + dot(l, sel[m])).reshape(nz, near, cells)
        patch = jnp.sum(jnp.where(spot[None], taken, 0.0), axis=1)
        modes = None
        for z in range(nz):
            term = vz_t[z] * patch[z : z + 1, :]
            modes = term if modes is None else modes + term
        zmodes[m] = modes.astype(bf16)

    def cut_solve(m):
        c = jnp.zeros((nz, cells), f32)
        for k in range(PATCH):
            c = c + vz[:, k : k + 1] * dot_nt(zmodes[m], inv[m, k])[k : k + 1, :]
        corr[m] = jnp.where(cut[m] >= 0, c, 0.0)

    def cut_place(m):
        h, l = split(jnp.where(spot[None], corr[m][:, None, :], 0.0).reshape(nz * near, cells))
        cw[m] = (dot(h, sel_t[m]) + dot(l, sel_t[m])).reshape(nz, near, full)

    def per_slot(step):
        for m in range(slots):
            step(m)

    def fast_rows(k):
        return fast[k // per][(k % per) * wide : (k % per + 1) * wide]

    sums = {"edge": jnp.zeros((wide, LANES), f32)}
    rims = [(z, start) for z in range(nz) for start in (0, HALO + rx)]
    for key in rims:
        sums[key] = jnp.zeros((HALO, ry), f32)

    def add_group(g):
        for k in range(g * per, (g + 1) * per):
            rows = fast_rows(k)
            sums["edge"] = sums["edge"] + v_vec[k] * rows[:, ry:]
            for z, start in rims:
                sums[z, start] = sums[z, start] + basis_s[0, QUARTER + z, k] * rows[start : start + HALO, :ry]

    to_modes(0)
    to_y(0)
    for z in range(nz):
        rs[z, :, pl.ds(0, ry)] = r0[z]
        rs[z, :, pl.ds(ry, LANES)] = jnp.where(group_w == z, r1, 0.0)
    to_modes(1)
    per_slot(cut_take)
    to_y(1)
    solve_x(0)
    to_modes(2)
    to_y(2)
    solve_x(1)
    from_y(0)
    to_modes(3)
    per_slot(cut_solve)
    to_y(3)
    solve_x(2)
    from_y(1)
    per_slot(cut_place)
    solve_x(3)
    add_group(0)
    from_y(2)
    add_group(1)
    from_y(3)
    add_group(2)
    add_group(3)

    def cut_part(z, start, count, lanes):
        tiles = []
        for r in range(start // HALF, (start + count) // HALF):
            out = jnp.zeros((HALF, LANES), f32)
            for m in range(slots):
                for a in range(blocks_x):
                    if 0 <= r - a < near // HALF:
                        out = out + jnp.where(cut_a[m] == a, cw[m, z, pl.ds((r - a) * HALF, HALF), lanes], 0.0)
            tiles.append(out)
        return jnp.concatenate(tiles, axis=0)

    def total_rows(z, start, count):
        t = cut_part(z, start, count, pl.ds(0, ry))
        for k in range(PATCH):
            t = t + basis_s[0, QUARTER + z, k] * fast_rows(k)[start : start + count, :ry]
        tot[z, pl.ds(start, count), :] = t

    packed = jnp.zeros((wide, LANES), f32)
    for z in range(nz):
        packed = jnp.where(group_w == z, cut_part(z, 0, wide, pl.ds(ry, LANES)), packed)
    edge[...] = packed + sums["edge"]
    for z, start in rims:
        tot[z, pl.ds(start, HALO), :] = sums[z, start] + cut_part(z, start, HALO, pl.ds(0, ry))
    for j in range(nz // 2):
        for i, r, natural in ((0, HALO + rx, top), (1, 0, ~top)):
            odd = pltpu.roll(tot[2 * j + 1, pl.ds(r, HALO), :], QUARTER, 0)
            rim_x[i, j] = jnp.where(natural, tot[2 * j, pl.ds(r, HALO), :], odd)

    start_all(copy2)
    for z in range(nz):
        total_rows(z, HALO, rx)
    wait_send_all(copy1)
    wait_recv_all(copy2)

    gap = jnp.zeros((rx - 2 * HALO, LANES), f32)
    l2 = left2[...] + jnp.concatenate([corners[0], gap, corners[2]], axis=0)
    r2 = right2[...] + jnp.concatenate([corners[1], gap, corners[3]], axis=0)
    both = jnp.where(lows, r2, l2)
    rim = (lane < QUARTER) | (lane >= ry - QUARTER)
    scale = damping * ext[nz, own, :]
    for z in range(nz):
        moved = pltpu.roll(both, (LANES - QUARTER - half - HALF * z) % LANES, 1)
        u, d = up[z // 2], down[z // 2]
        if z % 2:
            u, d = pltpu.roll(u, QUARTER, 0), pltpu.roll(d, QUARTER, 0)
        t = tot[z, own, :] + jnp.concatenate([jnp.where(top, u, 0.0), gap, jnp.where(top, 0.0, d)], axis=0)
        t = t + jnp.where(rim, moved, 0.0)
        out[z] = state[z] + scale * t

    wait_send_all(copy2)


def on_device(
    sizes, state, load_vector, active, stiff_band, mass_band, eig_basis, eig_values, cut_cols, cut_inverse
):
    nz, rx, ry = state.shape
    slots = cut_cols.shape[-1]
    assert nz == HALF and ry == LANES and rx % PATCH == 0
    inverse = cut_inverse.reshape(cut_inverse.shape[2:])
    wide = rx + 2 * HALO
    full = ry + LANES
    qx, qy = (rx // HALF) * PATCH, (ry // HALF) * PATCH
    cells = PATCH * PATCH
    anyspace = pl.BlockSpec(memory_space=pltpu.HBM)
    V, S = pltpu.VMEM, pltpu.SMEM
    dma = pltpu.SemaphoreType.DMA
    n = len(DIRS)
    return pl.pallas_call(
        functools.partial(kernel, sizes),
        out_shape=pltpu.VMEM(state.shape, f32),
        in_specs=[anyspace] * 9,
        out_specs=pl.BlockSpec(memory_space=pltpu.VMEM),
        scratch_shapes=[
            V(state.shape, f32), V(load_vector.shape, load_vector.dtype), V(active.shape, active.dtype),
            S(stiff_band.shape, f32), S(mass_band.shape, f32), S(eig_basis.shape, f32),
            V(eig_basis.shape, f32), S(eig_values.shape, f32), S(cut_cols.shape, cut_cols.dtype),
            V((slots, PATCH, cells, cells), bf16),
            V((nz + 1 + nz // 2, wide, ry), f32), V((nz, wide, ry), f32),
            V((wide, LANES), f32), V((wide, LANES), f32),
            V((rx, LANES), f32), V((rx, LANES), f32),
            V((3 * full, 2 * full), bf16), V((3 * full, qy), bf16), V((3 * qy, full), bf16),
            V((slots, full, cells), bf16), V((slots, cells, full), bf16),
            V((PATCH, qx, qy), f32),
            V((nz, wide, full), f32), V((slots, nz, PATCH + HALF, full), f32),
            V((nz, wide, ry), f32), V((nz, wide, ry), f32),
            V((nz * wide, 3 * full), bf16), V((nz * wide, 3 * full), bf16),
            V((PATCH * wide, 3 * full), bf16), V((PATCH * wide, 3 * qy), bf16),
            V((nz, wide, ry), f32), V((wide, LANES), f32),
            V((2, nz // 2, HALO, ry), f32),
            V((nz // 2, HALO, ry), f32), V((nz // 2, HALO, ry), f32),
            V((rx, LANES), f32), V((rx, LANES), f32),
            V((4, HALO, LANES), f32),
            dma((10,)), dma((n,)), dma((n,)), dma((n,)), dma((n,)),
        ],
        compiler_params=pltpu.CompilerParams(
            collective_id=0, has_side_effects=True, vmem_limit_bytes=56 * 1024 * 1024
        ),
    )(state, load_vector, active, stiff_band, mass_band, eig_basis, eig_values, cut_cols, inverse)


def solution(mesh):
    placed = (
        P(None, "gx", "gy"),
        P(None, "gx", "gy"),
        P("gx", "gy"),
        P(),
        P(),
        P(),
        P(),
        P("gx", "gy", None),
        P("gx", "gy", None, None, None, None),
    )
    sizes = (mesh.shape["gx"], mesh.shape["gy"])
    return jax.shard_map(
        functools.partial(on_device, sizes),
        mesh=mesh, in_specs=placed, out_specs=P(None, "gx", "gy"), check_vma=False,
    )
```

```python
import functools

import jax
import jax.numpy as jnp
from jax import lax
from jax.experimental import pallas as pl
from jax.experimental.pallas import tpu as pltpu
from jax.sharding import PartitionSpec as P

BAND = 4
PATCH = 16
HALF = PATCH // 2
QUARTER = PATCH // 4
HALO = BAND + QUARTER
LANES = 128
MESH = pl.DeviceIdType.MESH
DIRS = [(1, 0), (-1, 0), (1, 1), (1, -1), (-1, 1), (-1, -1), (0, 1), (0, -1)]

damping = 0.5
f32 = jnp.float32
bf16 = jnp.bfloat16


def iota(shape, dim):
    return lax.broadcasted_iota(jnp.int32, shape, dim)


def split(v):
    hi = v.astype(bf16)
    return hi, (v - hi.astype(f32)).astype(bf16)


def dot(a, b):
    return jnp.dot(a, b, preferred_element_type=f32)


def dot_nt(a, b):
    return lax.dot_general(a, b, (((1,), (1,)), ((), ())), preferred_element_type=f32)


def band_of(distance, taps):
    out = jnp.zeros(distance.shape, f32)
    for k in range(BAND + 1):
        out = jnp.where(distance == k, taps[k], out)
    return out


def inner_y(c, ry):
    u = (c - ry) & (HALF - 1)
    halo = jnp.where(u < QUARTER, u - QUARTER, ry + u - QUARTER)
    return jnp.where(c < ry, c, jnp.where(c < ry + LANES // 2, -1000, halo))


def wrap(v, n, reps):
    out = v
    for j in range(1, reps):
        out = out - jnp.where(v >= n * j, n, 0)
    return out


def kernel(
    sizes,
    state_h, load_h, active_h, stiff_h, mass_h, basis_h, values_h, cols_h, inverse_h,
    out,
    state, load, active, stiff, mass, basis_s, basis, values, cols, inv,
    ext, lf, from_left, from_right, pack_left, pack_right,
    yb, wy3, wyt3, sel, sel_t, dinv, rs, cw,
    zk, zm, sk3, sm3, r3, tb3, tot, edge,
    rim_x, up, down, left2, right2, corners,
    in_sem, send1, recv1, send2, recv2,
):
    n_x, n_y = sizes
    nz, rx, ry = state.shape
    wide = rx + 2 * HALO
    slots = inv.shape[0]
    blocks_x, blocks_y = rx // HALF, ry // HALF
    qx, qy = blocks_x * PATCH, blocks_y * PATCH
    full = ry + LANES
    half = LANES // 2
    groups = half // HALF
    me_x, me_y = lax.axis_index("gx"), lax.axis_index("gy")

    def exists(dx, dy):
        ok = None
        for d, me, n in ((dx, me_x, n_x), (dy, me_y, n_y)):
            if d:
                part = (me + d >= 0) & (me + d < n)
                ok = part if ok is None else ok & part
        return ok

    def device(dx, dy):
        return (jnp.clip(me_x + dx, 0, n_x - 1), jnp.clip(me_y + dy, 0, n_y - 1))

    fetches = [
        pltpu.make_async_copy(src, dst, in_sem.at[i])
        for i, (src, dst) in enumerate((
            (state_h, state), (load_h, load), (active_h, active),
            (stiff_h, stiff), (mass_h, mass), (basis_h, basis_s), (basis_h, basis),
            (values_h, values), (cols_h, cols), (inverse_h, inv),
        ))
    ]
    for fetch in fetches[:3]:
        fetch.start()

    own = pl.ds(HALO, rx)
    planes = nz + 1 + nz // 2
    zeros = jnp.zeros((planes, HALO, ry), f32)
    ext[:, pl.ds(0, HALO), :] = zeros
    ext[:, pl.ds(HALO + rx, HALO), :] = zeros
    for ref in (from_left, from_right, up, down, left2, right2, corners):
        ref[...] = jnp.zeros(ref.shape, f32)

    barrier = pltpu.get_barrier_semaphore()
    count = jnp.int32(0)
    for d in DIRS:
        ok = exists(*d)
        count = count + ok.astype(jnp.int32)

        @pl.when(ok)
        def _(d=d):
            pl.semaphore_signal(barrier, inc=1, device_id=device(*d), device_id_type=MESH)

    for fetch in fetches[3:]:
        fetch.start()
    for fetch in fetches[:3]:
        fetch.wait()
    for z in range(nz):
        ext[z, own, :] = state[z]
        lf[z, own, :] = load[z].astype(f32)
    ext[nz, own, :] = active[...].astype(f32)
    top = iota((HALO, ry), 0) < QUARTER
    for j in range(nz // 2):
        for r, natural in ((HALO, top), (rx, ~top)):
            odd = pltpu.roll(lf[2 * j + 1, pl.ds(r, HALO), :], QUARTER, 0)
            ext[nz + 1 + j, pl.ds(r, HALO), :] = jnp.where(natural, lf[2 * j, pl.ds(r, HALO), :], odd)

    lane = iota((rx, LANES), 1)
    group = (lane & (half - 1)) >> 3
    high = lane >= half
    lows = (lane & (HALF - 1)) < QUARTER
    to_right = jnp.zeros((rx, LANES), f32)
    to_left = jnp.zeros((rx, LANES), f32)
    act = ext[nz, own, :]
    for z in range(nz):
        s = ext[z, own, :]
        l = pltpu.roll(lf[z, own, :], (half + QUARTER + HALF * z) % LANES, 1)
        mine = group == z
        first = mine & high & lows
        second = mine & high & ~lows
        to_right = jnp.where(mine & ~high, pltpu.roll(s, (HALF + HALF * z) % LANES, 1), to_right)
        to_right = jnp.where(first, l, to_right)
        to_right = jnp.where(second, pltpu.roll(act, (half + HALF + HALF * z) % LANES, 1), to_right)
        to_left = jnp.where(mine & ~high, pltpu.roll(s, HALF * z, 1) if z else s, to_left)
        to_left = jnp.where(second, l, to_left)
        to_left = jnp.where(first, pltpu.roll(act, (half + HALF * z) % LANES, 1), to_left)
    pack_right[...] = to_right
    pack_left[...] = to_left

    def copy1(i):
        dx, dy = DIRS[i]
        if dy == 0:
            src = ext.at[:, pl.ds(rx if dx > 0 else HALO, HALO), :]
            dst = ext.at[:, pl.ds(0 if dx > 0 else HALO + rx, HALO), :]
        else:
            pack = pack_right if dy > 0 else pack_left
            land = from_left if dy > 0 else from_right
            if dx == 0:
                src, dst = pack, land.at[pl.ds(HALO, rx), :]
            else:
                src = pack.at[pl.ds(rx - HALO if dx > 0 else 0, HALO), :]
                dst = land.at[pl.ds(0 if dx > 0 else HALO + rx, HALO), :]
        return pltpu.make_async_remote_copy(
            src_ref=src, dst_ref=dst, send_sem=send1.at[i], recv_sem=recv1.at[i],
            device_id=device(dx, dy), device_id_type=MESH,
        )

    def copy2(i):
        dx, dy = DIRS[i]
        if dy == 0:
            src = rim_x.at[0 if dx > 0 else 1]
            dst = up if dx > 0 else down
        elif dx == 0:
            src = edge.at[pl.ds(HALO, rx), :]
            dst = left2 if dy > 0 else right2
        else:
            src = edge.at[pl.ds(HALO + rx if dx > 0 else 0, HALO), :]
            dst = corners.at[(dx < 0) * 2 + (dy < 0)]
        return pltpu.make_async_remote_copy(
            src_ref=src, dst_ref=dst, send_sem=send2.at[i], recv_sem=recv2.at[i],
            device_id=device(dx, dy), device_id_type=MESH,
        )

    def start_all(copy):
        for i, d in enumerate(DIRS):
            @pl.when(exists(*d))
            def _(i=i):
                copy(i).start()

    def wait_recv_all(copy):
        for i, (dx, dy) in enumerate(DIRS):
            @pl.when(exists(-dx, -dy))
            def _(i=i):
                copy(i).wait_recv()

    def wait_send_all(copy):
        for i, d in enumerate(DIRS):
            @pl.when(exists(*d))
            def _(i=i):
                copy(i).wait_send()

    pl.semaphore_wait(barrier, count)
    start_all(copy1)

    for fetch in fetches[3:9]:
        fetch.wait()
    pairs = groups // 2
    short = iota((ry + 2 * PATCH, 1), 0)
    spare = short & (HALF - 1)
    reach = jnp.where(short < ry, short, jnp.where(short < ry + PATCH, spare - HALO, ry + spare))
    distance = jnp.abs(reach - inner_y(iota((1, full), 1), ry))
    for j, taps in enumerate((mass, stiff)):
        h, l = split(band_of(distance, [taps[2, k] for k in range(BAND + 1)]))
        cols_j = pl.ds(j * full, full)
        for i, part in enumerate((h, h, l)):
            yb[pl.ds(i * full, ry), cols_j] = part[:ry]
            for side in range(2):
                tile = part[ry + side * PATCH : ry + (side + 1) * PATCH]
                for g in range(pairs):
                    yb[pl.ds(i * full + ry + side * half + g * PATCH, PATCH), cols_j] = tile

    highest = lax.Precision.HIGHEST
    tile_y = jnp.dot(
        basis[2], (iota((PATCH, qy), 0) == (iota((PATCH, qy), 1) & (PATCH - 1))).astype(f32),
        precision=highest, preferred_element_type=f32,
    )
    lane_b = iota((1, qy), 1) >> 4

    def wy_tile(y):
        place = y + QUARTER - HALF * lane_b
        w = jnp.zeros((HALF, qy), f32)
        for t in range(PATCH):
            w = jnp.where(place == t, tile_y[t : t + 1, :], w)
        return w

    row8 = iota((HALF, 1), 0)
    base = wy_tile(row8 + HALF)
    tiles = []
    for g in range(blocks_y):
        shift = (PATCH * (g - 1)) % qy
        moved = pltpu.roll(base, shift, 1) if shift else base
        tiles.append(jnp.where(jnp.abs(lane_b - g) <= 1, moved, 0.0))
    halo_tile = wy_tile(jnp.where(row8 < QUARTER, row8 - QUARTER, ry + row8 - QUARTER))
    wy = jnp.concatenate(tiles + [jnp.zeros((half, qy), f32)] + [halo_tile] * groups, axis=0)
    h, l = split(wy)
    for i, part in enumerate((h, h, l)):
        wy3[pl.ds(i * full, full), :] = part
    h, l = split(wy.T)
    for i, part in enumerate((h, h, l)):
        wyt3[pl.ds(i * qy, qy), :] = part

    def wx_of(shape, reps_r, reps_c):
        r, c = iota((shape[0], 1), 0), iota((1, shape[1]), 1)
        t = wrap(r, wide, reps_r) - (HALO - QUARTER) - HALF * (wrap(c, qx, reps_c) >> 4)
        t = jnp.where((r < wide * reps_r) & (c < qx * reps_c), t, -1)
        tile = jnp.dot(
            basis[1], (iota((PATCH, shape[1]), 0) == (iota((PATCH, shape[1]), 1) & (PATCH - 1))).astype(f32),
            precision=highest, preferred_element_type=f32,
        )
        w = jnp.zeros(shape, f32)
        for k in range(PATCH):
            w = jnp.where(t == k, tile[k : k + 1, :], w)
        return w

    def split3(v, width):
        h, l = split(v)
        return jnp.where(iota((1, v.shape[1]), 1) < 2 * width, h.astype(f32), l.astype(f32)).astype(bf16)

    pad_r = -(-3 * wide // LANES) * LANES
    pad_c = -(-qx // LANES) * LANES
    wx = wx_of((wide, pad_c), 1, 1)
    wx = jnp.concatenate([wx] * 3 + [jnp.zeros((pad_r - 3 * wide, pad_c), f32)], axis=0)
    g3 = split3(wx.T[:qx, : 3 * wide], wide)
    b3 = split3(wx_of((wide, 3 * qx), 1, 3), qx)

    c = iota((1, 4 * wide), 1)
    dist_x = jnp.abs(iota((wide, 1), 0) - wrap(c, wide, 4))
    bx = jnp.where(
        (c < wide) | ((c >= 2 * wide) & (c < 3 * wide)),
        band_of(dist_x, [mass[1, k] for k in range(BAND + 1)]),
        band_of(dist_x, [stiff[1, k] for k in range(BAND + 1)]),
    )
    bx_hi, bx_lo = split(bx)
    bx_lo = bx_lo[:, : 2 * wide]

    cells = PATCH * PATCH
    cut = [cols[0, 0, m] for m in range(slots)]
    cut_a = [lax.div(jnp.maximum(v, 0), jnp.int32(blocks_y)) for v in cut]
    cut_b = [lax.rem(jnp.maximum(v, 0), jnp.int32(blocks_y)) for v in cut]
    y_in = inner_y(iota((full, 1), 0), ry)
    y_to = iota((1, cells), 1) & (PATCH - 1)
    y_in_t = inner_y(iota((1, full), 1), ry)
    y_to_t = iota((cells, 1), 0) & (PATCH - 1)
    for m in range(slots):
        sel[m] = jnp.where(y_in + QUARTER - HALF * cut_b[m] == y_to, 1.0, 0.0).astype(bf16)
        sel_t[m] = jnp.where(y_in_t + QUARTER - HALF * cut_b[m] == y_to_t, 1.0, 0.0).astype(bf16)

    near = PATCH + HALF
    spot = iota((near, 1), 0) - QUARTER == (iota((1, cells), 1) >> 4)
    vz_t = []
    for z in range(nz):
        v = jnp.zeros((PATCH, 1), f32)
        for k in range(PATCH):
            v = jnp.where(iota((PATCH, 1), 0) == k, basis_s[0, QUARTER + z, k], v)
        vz_t.append(v)

    def pick(shape, dim, row):
        index = iota(shape, dim) & (PATCH - 1)
        v = jnp.zeros(shape, f32)
        for k in range(PATCH):
            v = jnp.where(index == k, values[row, k], v)
        return v

    lam = pick((PATCH, 1), 0, 1) + pick((1, qy), 1, 2)
    column = (iota((qx, 1), 0) >> 4) * blocks_y + (iota((1, qy), 1) >> 4)
    keep = jnp.ones((qx, qy), f32)
    for m in range(slots):
        keep = jnp.where(column == cut[m], 0.0, keep)
    for k in range(PATCH):
        dinv[k] = keep * jnp.concatenate([1.0 / (values[0, k] + lam)] * blocks_x, axis=0)

    lane1 = iota((1, LANES), 1)
    group1 = (lane1 & (half - 1)) >> 3
    far = [jnp.abs(group1 - z) for z in range(nz)]
    k_vec = [band_of(far[z], [stiff[0, k] for k in range(BAND + 1)]) for z in range(nz)]
    m_vec = [band_of(far[z], [mass[0, k] for k in range(BAND + 1)]) for z in range(nz)]
    v_vec = []
    for k in range(PATCH):
        v = jnp.zeros((1, LANES), f32)
        for z in range(nz):
            v = jnp.where((group1 == z) & (lane1 >= half), basis_s[0, QUARTER + z, k], v)
        v_vec.append(v)

    def put3(ref, rows, start, width, v):
        h, l = split(v)
        for i, part in enumerate((h, l, h)):
            ref[rows, pl.ds(i * width + start, v.shape[1])] = part

    def mix_z(start, count):
        for r in range(start, start + count, HALF):
            rows = pl.ds(r, HALF)
            s = [ext[z, rows, :] for z in range(nz)]
            for z in range(nz):
                p = q = None
                for w in range(nz):
                    k = abs(z - w)
                    if k > BAND:
                        continue
                    a, b = stiff[0, k] * s[w], mass[0, k] * s[w]
                    p = a if p is None else p + a
                    q = b if q is None else q + b
                zk[z, rows, :] = p
                zm[z, rows, :] = q

    mix_z(HALO, rx)
    fetches[9].wait()
    wait_recv_all(copy1)
    mix_z(0, HALO)
    mix_z(HALO + rx, HALO)

    lane_w = iota((wide, LANES), 1)
    group_w = (lane_w & (half - 1)) >> 3
    halo_l, halo_r = from_left[...], from_right[...]
    comb = jnp.where(lane_w < half, halo_l, pltpu.roll(halo_r, half, 1))
    low = (lane_w & (HALF - 1)) < QUARTER
    load_t = jnp.where(low, halo_l, halo_r)
    act_t = jnp.where(low, pltpu.roll(halo_l, LANES - QUARTER, 1), pltpu.roll(halo_r, QUARTER, 1))
    act_t = jnp.where(lane_w >= half, act_t, 0.0)
    act_w = ext[nz]
    for z in range(nz):
        for r in (0, HALO + rx):
            tile = ext[nz + 1 + z // 2, pl.ds(r, HALO), :]
            lf[z, pl.ds(r, HALO), :] = pltpu.roll(tile, QUARTER, 0) if z % 2 else tile
    r0 = []
    r1 = jnp.zeros((wide, LANES), f32)
    part_z = nz // 4

    def spread_y(g):
        for z in range(g * part_z, (g + 1) * part_z):
            rows = pl.ds(z * wide, wide)
            for s3, mixed, vec in ((sk3, zk, k_vec), (sm3, zm, m_vec)):
                put3(s3, rows, 0, full, mixed[z])
                put3(s3, rows, ry, full, comb * vec[z])

    def band_y(g):
        rows = pl.ds(g * part_z * wide, part_z * wide)
        ym = dot(sm3[rows, :], yb[...])
        return ym[:, :full], ym[:, full:] + dot(sk3[rows, :], yb[:, pl.ds(0, full)])

    def band_x(g, ym, yp, r1):
        for i in range(part_z):
            z = g * part_z + i
            p_hi, p_lo = split(yp[i * wide : (i + 1) * wide])
            q_hi, q_lo = split(ym[i * wide : (i + 1) * wide])
            applied = dot(bx_hi, jnp.concatenate([p_hi, q_hi, p_lo, q_lo], axis=0))
            applied = applied + dot(bx_lo, jnp.concatenate([p_hi, q_hi], axis=0))
            r0.append(act_w * (lf[z] - applied[:, :ry]))
            r1 = jnp.where(group_w == z, applied[:, ry:], r1)
        return r1

    parts = nz // part_z
    bands = []
    spread_y(0)
    for g in range(parts):
        bands.append(band_y(g))
        if g + 1 < parts:
            spread_y(g + 1)
        if g:
            r1 = band_x(g - 1, *bands[g - 1], r1)
    r1 = band_x(parts - 1, *bands[-1], r1)
    r1 = act_t * (load_t - r1)

    per = PATCH // 4
    vz = basis[0, pl.ds(QUARTER, nz), :]
    t1, fast = {}, {}
    zmodes, corr = {}, {}

    def to_modes(g):
        for k in range(g * per, (g + 1) * per):
            rows = pl.ds(k * wide, wide)
            v = None
            for z in range(nz):
                term = basis_s[0, QUARTER + z, k] * r0[z]
                v = term if v is None else v + term
            put3(r3, rows, 0, full, v)
            put3(r3, rows, ry, full, r1 * v_vec[k])

    def to_y(g):
        t1[g] = dot(r3[pl.ds(g * per * wide, per * wide), :], wy3[...])

    def solve_x(g):
        for i in range(per):
            k = g * per + i
            h, l = split(t1[g][i * wide : (i + 1) * wide])
            h, l = split(dot(g3, jnp.concatenate([h, l, h], axis=0)) * dinv[k])
            back = dot(b3, jnp.concatenate([h, l, h], axis=0))
            put3(tb3, pl.ds(k * wide, wide), 0, qy, back)

    def from_y(g):
        fast[g] = dot(tb3[pl.ds(g * per * wide, per * wide), :], wyt3[...])

    def cut_take(m):
        window = rs[:, pl.ds(0, near), :]
        for a in range(1, blocks_x):
            window = jnp.where(cut_a[m] == a, rs[:, pl.ds(a * HALF, near), :], window)
        h, l = split(window.reshape(nz * near, full))
        taken = (dot(h, sel[m]) + dot(l, sel[m])).reshape(nz, near, cells)
        patch = jnp.sum(jnp.where(spot[None], taken, 0.0), axis=1)
        modes = None
        for z in range(nz):
            term = vz_t[z] * patch[z : z + 1, :]
            modes = term if modes is None else modes + term
        zmodes[m] = modes.astype(bf16)

    def cut_solve(m):
        c = jnp.zeros((nz, cells), f32)
        for k in range(PATCH):
            c = c + vz[:, k : k + 1] * dot_nt(zmodes[m], inv[m, k])[k : k + 1, :]
        corr[m] = jnp.where(cut[m] >= 0, c, 0.0)

    def cut_place(m):
        h, l = split(jnp.where(spot[None], corr[m][:, None, :], 0.0).reshape(nz * near, cells))
        cw[m] = (dot(h, sel_t[m]) + dot(l, sel_t[m])).reshape(nz, near, full)

    def per_slot(step):
        for m in range(slots):
            step(m)

    def fast_rows(k):
        return fast[k // per][(k % per) * wide : (k % per + 1) * wide]

    sums = {"edge": jnp.zeros((wide, LANES), f32)}
    rims = [(z, start) for z in range(nz) for start in (0, HALO + rx)]
    for key in rims:
        sums[key] = jnp.zeros((HALO, ry), f32)

    def add_group(g):
        for k in range(g * per, (g + 1) * per):
            rows = fast_rows(k)
            sums["edge"] = sums["edge"] + v_vec[k] * rows[:, ry:]
            for z, start in rims:
                sums[z, start] = sums[z, start] + basis_s[0, QUARTER + z, k] * rows[start : start + HALO, :ry]

    to_modes(0)
    to_y(0)
    for z in range(nz):
        rs[z, :, pl.ds(0, ry)] = r0[z]
        rs[z, :, pl.ds(ry, LANES)] = jnp.where(group_w == z, r1, 0.0)
    to_modes(1)
    per_slot(cut_take)
    to_y(1)
    solve_x(0)
    to_modes(2)
    to_y(2)
    solve_x(1)
    from_y(0)
    to_modes(3)
    per_slot(cut_solve)
    to_y(3)
    solve_x(2)
    from_y(1)
    per_slot(cut_place)
    solve_x(3)
    add_group(0)
    from_y(2)
    add_group(1)
    from_y(3)
    add_group(2)
    add_group(3)

    def cut_part(z, start, count, lanes):
        tiles = []
        for r in range(start // HALF, (start + count) // HALF):
            out = jnp.zeros((HALF, LANES), f32)
            for m in range(slots):
                for a in range(blocks_x):
                    if 0 <= r - a < near // HALF:
                        out = out + jnp.where(cut_a[m] == a, cw[m, z, pl.ds((r - a) * HALF, HALF), lanes], 0.0)
            tiles.append(out)
        return jnp.concatenate(tiles, axis=0)

    def total_rows(z, start, count):
        t = cut_part(z, start, count, pl.ds(0, ry))
        for k in range(PATCH):
            t = t + basis_s[0, QUARTER + z, k] * fast_rows(k)[start : start + count, :ry]
        tot[z, pl.ds(start, count), :] = t

    packed = jnp.zeros((wide, LANES), f32)
    for z in range(nz):
        packed = jnp.where(group_w == z, cut_part(z, 0, wide, pl.ds(ry, LANES)), packed)
    edge[...] = packed + sums["edge"]
    for z, start in rims:
        tot[z, pl.ds(start, HALO), :] = sums[z, start] + cut_part(z, start, HALO, pl.ds(0, ry))
    for j in range(nz // 2):
        for i, r, natural in ((0, HALO + rx, top), (1, 0, ~top)):
            odd = pltpu.roll(tot[2 * j + 1, pl.ds(r, HALO), :], QUARTER, 0)
            rim_x[i, j] = jnp.where(natural, tot[2 * j, pl.ds(r, HALO), :], odd)

    start_all(copy2)
    for z in range(nz):
        total_rows(z, HALO, rx)
    wait_send_all(copy1)
    wait_recv_all(copy2)

    gap = jnp.zeros((rx - 2 * HALO, LANES), f32)
    l2 = left2[...] + jnp.concatenate([corners[0], gap, corners[2]], axis=0)
    r2 = right2[...] + jnp.concatenate([corners[1], gap, corners[3]], axis=0)
    both = jnp.where(lows, r2, l2)
    rim = (lane < QUARTER) | (lane >= ry - QUARTER)
    scale = damping * ext[nz, own, :]
    for z in range(nz):
        moved = pltpu.roll(both, (LANES - QUARTER - half - HALF * z) % LANES, 1)
        u, d = up[z // 2], down[z // 2]
        if z % 2:
            u, d = pltpu.roll(u, QUARTER, 0), pltpu.roll(d, QUARTER, 0)
        t = tot[z, own, :] + jnp.concatenate([jnp.where(top, u, 0.0), gap, jnp.where(top, 0.0, d)], axis=0)
        t = t + jnp.where(rim, moved, 0.0)
        out[z] = state[z] + scale * t

    wait_send_all(copy2)


def on_device(
    sizes, state, load_vector, active, stiff_band, mass_band, eig_basis, eig_values, cut_cols, cut_inverse
):
    nz, rx, ry = state.shape
    slots = cut_cols.shape[-1]
    assert nz == HALF and ry == LANES and rx % PATCH == 0
    inverse = cut_inverse.reshape(cut_inverse.shape[2:])
    wide = rx + 2 * HALO
    full = ry + LANES
    qx, qy = (rx // HALF) * PATCH, (ry // HALF) * PATCH
    cells = PATCH * PATCH
    anyspace = pl.BlockSpec(memory_space=pltpu.HBM)
    V, S = pltpu.VMEM, pltpu.SMEM
    dma = pltpu.SemaphoreType.DMA
    n = len(DIRS)
    return pl.pallas_call(
        functools.partial(kernel, sizes),
        out_shape=pltpu.VMEM(state.shape, f32),
        in_specs=[anyspace] * 9,
        out_specs=pl.BlockSpec(memory_space=pltpu.VMEM),
        scratch_shapes=[
            V(state.shape, f32), V(load_vector.shape, load_vector.dtype), V(active.shape, active.dtype),
            S(stiff_band.shape, f32), S(mass_band.shape, f32), S(eig_basis.shape, f32),
            V(eig_basis.shape, f32), S(eig_values.shape, f32), S(cut_cols.shape, cut_cols.dtype),
            V((slots, PATCH, cells, cells), bf16),
            V((nz + 1 + nz // 2, wide, ry), f32), V((nz, wide, ry), f32),
            V((wide, LANES), f32), V((wide, LANES), f32),
            V((rx, LANES), f32), V((rx, LANES), f32),
            V((3 * full, 2 * full), bf16), V((3 * full, qy), bf16), V((3 * qy, full), bf16),
            V((slots, full, cells), bf16), V((slots, cells, full), bf16),
            V((PATCH, qx, qy), f32),
            V((nz, wide, full), f32), V((slots, nz, PATCH + HALF, full), f32),
            V((nz, wide, ry), f32), V((nz, wide, ry), f32),
            V((nz * wide, 3 * full), bf16), V((nz * wide, 3 * full), bf16),
            V((PATCH * wide, 3 * full), bf16), V((PATCH * wide, 3 * qy), bf16),
            V((nz, wide, ry), f32), V((wide, LANES), f32),
            V((2, nz // 2, HALO, ry), f32),
            V((nz // 2, HALO, ry), f32), V((nz // 2, HALO, ry), f32),
            V((rx, LANES), f32), V((rx, LANES), f32),
            V((4, HALO, LANES), f32),
            dma((10,)), dma((n,)), dma((n,)), dma((n,)), dma((n,)),
        ],
        compiler_params=pltpu.CompilerParams(
            collective_id=0, has_side_effects=True, vmem_limit_bytes=56 * 1024 * 1024
        ),
    )(state, load_vector, active, stiff_band, mass_band, eig_basis, eig_values, cut_cols, inverse)


def solution(mesh):
    placed = (
        P(None, "gx", "gy"),
        P(None, "gx", "gy"),
        P("gx", "gy"),
        P(),
        P(),
        P(),
        P(),
        P("gx", "gy", None),
        P("gx", "gy", None, None, None, None),
    )
    sizes = (mesh.shape["gx"], mesh.shape["gy"])
    return jax.shard_map(
        functools.partial(on_device, sizes),
        mesh=mesh, in_specs=placed, out_specs=P(None, "gx", "gy"), check_vma=False,
    )
```

```python
import functools

import jax
import jax.numpy as jnp
from jax import lax
from jax.experimental import pallas as pl
from jax.experimental.pallas import tpu as pltpu
from jax.sharding import PartitionSpec as P

BAND = 4
PATCH = 16
HALF = PATCH // 2
QUARTER = PATCH // 4
HALO = BAND + QUARTER
LANES = 128
MESH = pl.DeviceIdType.MESH
DIRS = [(1, 0), (-1, 0), (1, 1), (1, -1), (-1, 1), (-1, -1), (0, 1), (0, -1)]

damping = 0.5
f32 = jnp.float32
bf16 = jnp.bfloat16


def iota(shape, dim):
    return lax.broadcasted_iota(jnp.int32, shape, dim)


def split(v):
    hi = v.astype(bf16)
    return hi, (v - hi.astype(f32)).astype(bf16)


def dot(a, b):
    return jnp.dot(a, b, preferred_element_type=f32)


def dot_nt(a, b):
    return lax.dot_general(a, b, (((1,), (1,)), ((), ())), preferred_element_type=f32)


def band_of(distance, taps):
    out = jnp.zeros(distance.shape, f32)
    for k in range(BAND + 1):
        out = jnp.where(distance == k, taps[k], out)
    return out


def inner_y(c, ry):
    u = (c - ry) & (HALF - 1)
    halo = jnp.where(u < QUARTER, u - QUARTER, ry + u - QUARTER)
    return jnp.where(c < ry, c, jnp.where(c < ry + LANES // 2, -1000, halo))


def wrap(v, n, reps):
    out = v
    for j in range(1, reps):
        out = out - jnp.where(v >= n * j, n, 0)
    return out


def kernel(
    sizes,
    state_h, load_h, active_h, stiff_h, mass_h, basis_h, values_h, cols_h, inverse_h,
    out,
    state, load, active, stiff, mass, basis_s, basis, values, cols, inv,
    ext, lf, from_left, from_right, pack_left, pack_right,
    yb, wy3, wyt3, sel, sel_t, dinv, rs, cw,
    zk, zm, sk3, sm3, r3, tb3, tot, edge,
    rim_x, up, down, left2, right2, corners,
    in_sem, send1, recv1, send2, recv2,
):
    n_x, n_y = sizes
    nz, rx, ry = state.shape
    wide = rx + 2 * HALO
    slots = inv.shape[0]
    blocks_x, blocks_y = rx // HALF, ry // HALF
    qx, qy = blocks_x * PATCH, blocks_y * PATCH
    full = ry + LANES
    half = LANES // 2
    groups = half // HALF
    me_x, me_y = lax.axis_index("gx"), lax.axis_index("gy")

    def exists(dx, dy):
        ok = None
        for d, me, n in ((dx, me_x, n_x), (dy, me_y, n_y)):
            if d:
                part = (me + d >= 0) & (me + d < n)
                ok = part if ok is None else ok & part
        return ok

    def device(dx, dy):
        return (jnp.clip(me_x + dx, 0, n_x - 1), jnp.clip(me_y + dy, 0, n_y - 1))

    fetches = [
        pltpu.make_async_copy(src, dst, in_sem.at[i])
        for i, (src, dst) in enumerate((
            (state_h, state), (load_h, load), (active_h, active),
            (stiff_h, stiff), (mass_h, mass), (basis_h, basis_s), (basis_h, basis),
            (values_h, values), (cols_h, cols), (inverse_h, inv),
        ))
    ]
    for fetch in fetches[:3]:
        fetch.start()

    own = pl.ds(HALO, rx)
    planes = nz + 1 + nz // 2
    zeros = jnp.zeros((planes, HALO, ry), f32)
    ext[:, pl.ds(0, HALO), :] = zeros
    ext[:, pl.ds(HALO + rx, HALO), :] = zeros
    for ref in (from_left, from_right, up, down, left2, right2, corners):
        ref[...] = jnp.zeros(ref.shape, f32)

    barrier = pltpu.get_barrier_semaphore()
    count = jnp.int32(0)
    for d in DIRS:
        ok = exists(*d)
        count = count + ok.astype(jnp.int32)

        @pl.when(ok)
        def _(d=d):
            pl.semaphore_signal(barrier, inc=1, device_id=device(*d), device_id_type=MESH)

    for fetch in fetches[3:]:
        fetch.start()
    for fetch in fetches[:3]:
        fetch.wait()
    for z in range(nz):
        ext[z, own, :] = state[z]
        lf[z, own, :] = load[z].astype(f32)
    ext[nz, own, :] = active[...].astype(f32)
    top = iota((HALO, ry), 0) < QUARTER
    for j in range(nz // 2):
        for r, natural in ((HALO, top), (rx, ~top)):
            odd = pltpu.roll(lf[2 * j + 1, pl.ds(r, HALO), :], QUARTER, 0)
            ext[nz + 1 + j, pl.ds(r, HALO), :] = jnp.where(natural, lf[2 * j, pl.ds(r, HALO), :], odd)

    def copy1(i):
        dx, dy = DIRS[i]
        if dy == 0:
            src = ext.at[:, pl.ds(rx if dx > 0 else HALO, HALO), :]
            dst = ext.at[:, pl.ds(0 if dx > 0 else HALO + rx, HALO), :]
        else:
            pack = pack_right if dy > 0 else pack_left
            land = from_left if dy > 0 else from_right
            if dx == 0:
                src, dst = pack, land.at[pl.ds(HALO, rx), :]
            else:
                src = pack.at[pl.ds(rx - HALO if dx > 0 else 0, HALO), :]
                dst = land.at[pl.ds(0 if dx > 0 else HALO + rx, HALO), :]
        return pltpu.make_async_remote_copy(
            src_ref=src, dst_ref=dst, send_sem=send1.at[i], recv_sem=recv1.at[i],
            device_id=device(dx, dy), device_id_type=MESH,
        )

    def copy2(i):
        dx, dy = DIRS[i]
        if dy == 0:
            src = rim_x.at[0 if dx > 0 else 1]
            dst = up if dx > 0 else down
        elif dx == 0:
            src = edge.at[pl.ds(HALO, rx), :]
            dst = left2 if dy > 0 else right2
        else:
            src = edge.at[pl.ds(HALO + rx if dx > 0 else 0, HALO), :]
            dst = corners.at[(dx < 0) * 2 + (dy < 0)]
        return pltpu.make_async_remote_copy(
            src_ref=src, dst_ref=dst, send_sem=send2.at[i], recv_sem=recv2.at[i],
            device_id=device(dx, dy), device_id_type=MESH,
        )

    def start_all(copy, first=0, last=len(DIRS)):
        for i, d in enumerate(DIRS[first:last], first):
            @pl.when(exists(*d))
            def _(i=i):
                copy(i).start()

    def wait_recv_all(copy):
        for i, (dx, dy) in enumerate(DIRS):
            @pl.when(exists(-dx, -dy))
            def _(i=i):
                copy(i).wait_recv()

    def wait_send_all(copy):
        for i, d in enumerate(DIRS):
            @pl.when(exists(*d))
            def _(i=i):
                copy(i).wait_send()

    pl.semaphore_wait(barrier, count)
    start_all(copy1, last=2)

    lane = iota((rx, LANES), 1)
    group = (lane & (half - 1)) >> 3
    high = lane >= half
    lows = (lane & (HALF - 1)) < QUARTER
    to_right = jnp.zeros((rx, LANES), f32)
    to_left = jnp.zeros((rx, LANES), f32)
    act = ext[nz, own, :]
    for z in range(nz):
        s = ext[z, own, :]
        l = pltpu.roll(lf[z, own, :], (half + QUARTER + HALF * z) % LANES, 1)
        mine = group == z
        first = mine & high & lows
        second = mine & high & ~lows
        to_right = jnp.where(mine & ~high, pltpu.roll(s, (HALF + HALF * z) % LANES, 1), to_right)
        to_right = jnp.where(first, l, to_right)
        to_right = jnp.where(second, pltpu.roll(act, (half + HALF + HALF * z) % LANES, 1), to_right)
        to_left = jnp.where(mine & ~high, pltpu.roll(s, HALF * z, 1) if z else s, to_left)
        to_left = jnp.where(second, l, to_left)
        to_left = jnp.where(first, pltpu.roll(act, (half + HALF * z) % LANES, 1), to_left)
    pack_right[...] = to_right
    pack_left[...] = to_left
    start_all(copy1, first=2)

    for fetch in fetches[3:9]:
        fetch.wait()
    pairs = groups // 2
    short = iota((ry + 2 * PATCH, 1), 0)
    spare = short & (HALF - 1)
    reach = jnp.where(short < ry, short, jnp.where(short < ry + PATCH, spare - HALO, ry + spare))
    distance = jnp.abs(reach - inner_y(iota((1, full), 1), ry))
    for j, taps in enumerate((mass, stiff)):
        h, l = split(band_of(distance, [taps[2, k] for k in range(BAND + 1)]))
        cols_j = pl.ds(j * full, full)
        for i, part in enumerate((h, h, l)):
            yb[pl.ds(i * full, ry), cols_j] = part[:ry]
            for side in range(2):
                tile = part[ry + side * PATCH : ry + (side + 1) * PATCH]
                for g in range(pairs):
                    yb[pl.ds(i * full + ry + side * half + g * PATCH, PATCH), cols_j] = tile

    highest = lax.Precision.HIGHEST
    tile_y = jnp.dot(
        basis[2], (iota((PATCH, qy), 0) == (iota((PATCH, qy), 1) & (PATCH - 1))).astype(f32),
        precision=highest, preferred_element_type=f32,
    )
    lane_b = iota((1, qy), 1) >> 4

    def wy_tile(y):
        place = y + QUARTER - HALF * lane_b
        w = jnp.zeros((HALF, qy), f32)
        for t in range(PATCH):
            w = jnp.where(place == t, tile_y[t : t + 1, :], w)
        return w

    row8 = iota((HALF, 1), 0)
    base = wy_tile(row8 + HALF)
    tiles = []
    for g in range(blocks_y):
        shift = (PATCH * (g - 1)) % qy
        moved = pltpu.roll(base, shift, 1) if shift else base
        tiles.append(jnp.where(jnp.abs(lane_b - g) <= 1, moved, 0.0))
    halo_tile = wy_tile(jnp.where(row8 < QUARTER, row8 - QUARTER, ry + row8 - QUARTER))
    wy = jnp.concatenate(tiles + [jnp.zeros((half, qy), f32)] + [halo_tile] * groups, axis=0)
    h, l = split(wy)
    for i, part in enumerate((h, h, l)):
        wy3[pl.ds(i * full, full), :] = part
    h, l = split(wy.T)
    for i, part in enumerate((h, h, l)):
        wyt3[pl.ds(i * qy, qy), :] = part

    def wx_of(shape, reps_r, reps_c):
        r, c = iota((shape[0], 1), 0), iota((1, shape[1]), 1)
        t = wrap(r, wide, reps_r) - (HALO - QUARTER) - HALF * (wrap(c, qx, reps_c) >> 4)
        t = jnp.where((r < wide * reps_r) & (c < qx * reps_c), t, -1)
        tile = jnp.dot(
            basis[1], (iota((PATCH, shape[1]), 0) == (iota((PATCH, shape[1]), 1) & (PATCH - 1))).astype(f32),
            precision=highest, preferred_element_type=f32,
        )
        w = jnp.zeros(shape, f32)
        for k in range(PATCH):
            w = jnp.where(t == k, tile[k : k + 1, :], w)
        return w

    def split3(v, width):
        h, l = split(v)
        return jnp.where(iota((1, v.shape[1]), 1) < 2 * width, h.astype(f32), l.astype(f32)).astype(bf16)

    pad_r = -(-3 * wide // LANES) * LANES
    pad_c = -(-qx // LANES) * LANES
    wx = wx_of((wide, pad_c), 1, 1)
    wx = jnp.concatenate([wx] * 3 + [jnp.zeros((pad_r - 3 * wide, pad_c), f32)], axis=0)
    g3 = split3(wx.T[:qx, : 3 * wide], wide)
    b3 = split3(wx_of((wide, 3 * qx), 1, 3), qx)

    c = iota((1, 4 * wide), 1)
    dist_x = jnp.abs(iota((wide, 1), 0) - wrap(c, wide, 4))
    bx = jnp.where(
        (c < wide) | ((c >= 2 * wide) & (c < 3 * wide)),
        band_of(dist_x, [mass[1, k] for k in range(BAND + 1)]),
        band_of(dist_x, [stiff[1, k] for k in range(BAND + 1)]),
    )
    bx_hi, bx_lo = split(bx)
    bx_lo = bx_lo[:, : 2 * wide]

    cells = PATCH * PATCH
    cut = [cols[0, 0, m] for m in range(slots)]
    cut_a = [lax.div(jnp.maximum(v, 0), jnp.int32(blocks_y)) for v in cut]
    cut_b = [lax.rem(jnp.maximum(v, 0), jnp.int32(blocks_y)) for v in cut]
    y_in = inner_y(iota((full, 1), 0), ry)
    y_to = iota((1, cells), 1) & (PATCH - 1)
    y_in_t = inner_y(iota((1, full), 1), ry)
    y_to_t = iota((cells, 1), 0) & (PATCH - 1)
    for m in range(slots):
        sel[m] = jnp.where(y_in + QUARTER - HALF * cut_b[m] == y_to, 1.0, 0.0).astype(bf16)
        sel_t[m] = jnp.where(y_in_t + QUARTER - HALF * cut_b[m] == y_to_t, 1.0, 0.0).astype(bf16)

    near = PATCH + HALF
    spot = iota((near, 1), 0) - QUARTER == (iota((1, cells), 1) >> 4)
    vz_t = []
    for z in range(nz):
        v = jnp.zeros((PATCH, 1), f32)
        for k in range(PATCH):
            v = jnp.where(iota((PATCH, 1), 0) == k, basis_s[0, QUARTER + z, k], v)
        vz_t.append(v)

    def pick(shape, dim, row):
        index = iota(shape, dim) & (PATCH - 1)
        v = jnp.zeros(shape, f32)
        for k in range(PATCH):
            v = jnp.where(index == k, values[row, k], v)
        return v

    lam = pick((PATCH, 1), 0, 1) + pick((1, qy), 1, 2)
    column = (iota((qx, 1), 0) >> 4) * blocks_y + (iota((1, qy), 1) >> 4)
    keep = jnp.ones((qx, qy), f32)
    for m in range(slots):
        keep = jnp.where(column == cut[m], 0.0, keep)
    for k in range(PATCH):
        dinv[k] = keep * jnp.concatenate([1.0 / (values[0, k] + lam)] * blocks_x, axis=0)

    lane1 = iota((1, LANES), 1)
    group1 = (lane1 & (half - 1)) >> 3
    far = [jnp.abs(group1 - z) for z in range(nz)]
    k_vec = [band_of(far[z], [stiff[0, k] for k in range(BAND + 1)]) for z in range(nz)]
    m_vec = [band_of(far[z], [mass[0, k] for k in range(BAND + 1)]) for z in range(nz)]
    v_vec = []
    for k in range(PATCH):
        v = jnp.zeros((1, LANES), f32)
        for z in range(nz):
            v = jnp.where((group1 == z) & (lane1 >= half), basis_s[0, QUARTER + z, k], v)
        v_vec.append(v)

    def put3(ref, rows, start, width, v):
        h, l = split(v)
        for i, part in enumerate((h, l, h)):
            ref[rows, pl.ds(i * width + start, v.shape[1])] = part

    def mix_z(start, count):
        for r in range(start, start + count, HALF):
            rows = pl.ds(r, HALF)
            s = [ext[z, rows, :] for z in range(nz)]
            for z in range(nz):
                p = q = None
                for w in range(nz):
                    k = abs(z - w)
                    if k > BAND:
                        continue
                    a, b = stiff[0, k] * s[w], mass[0, k] * s[w]
                    p = a if p is None else p + a
                    q = b if q is None else q + b
                zk[z, rows, :] = p
                zm[z, rows, :] = q

    mix_z(HALO, rx)
    fetches[9].wait()
    wait_recv_all(copy1)
    mix_z(0, HALO)
    mix_z(HALO + rx, HALO)

    lane_w = iota((wide, LANES), 1)
    group_w = (lane_w & (half - 1)) >> 3
    halo_l, halo_r = from_left[...], from_right[...]
    comb = jnp.where(lane_w < half, halo_l, pltpu.roll(halo_r, half, 1))
    low = (lane_w & (HALF - 1)) < QUARTER
    load_t = jnp.where(low, halo_l, halo_r)
    act_t = jnp.where(low, pltpu.roll(halo_l, LANES - QUARTER, 1), pltpu.roll(halo_r, QUARTER, 1))
    act_t = jnp.where(lane_w >= half, act_t, 0.0)
    act_w = ext[nz]
    for z in range(nz):
        for r in (0, HALO + rx):
            tile = ext[nz + 1 + z // 2, pl.ds(r, HALO), :]
            lf[z, pl.ds(r, HALO), :] = pltpu.roll(tile, QUARTER, 0) if z % 2 else tile
    r0 = []
    r1 = jnp.zeros((wide, LANES), f32)
    part_z = nz // 4

    def spread_y(g):
        for z in range(g * part_z, (g + 1) * part_z):
            rows = pl.ds(z * wide, wide)
            for s3, mixed, vec in ((sk3, zk, k_vec), (sm3, zm, m_vec)):
                put3(s3, rows, 0, full, mixed[z])
                put3(s3, rows, ry, full, comb * vec[z])

    def band_y(g):
        rows = pl.ds(g * part_z * wide, part_z * wide)
        ym = dot(sm3[rows, :], yb[...])
        return ym[:, :full], ym[:, full:] + dot(sk3[rows, :], yb[:, pl.ds(0, full)])

    def band_x(g, ym, yp, r1):
        for i in range(part_z):
            z = g * part_z + i
            p_hi, p_lo = split(yp[i * wide : (i + 1) * wide])
            q_hi, q_lo = split(ym[i * wide : (i + 1) * wide])
            applied = dot(bx_hi, jnp.concatenate([p_hi, q_hi, p_lo, q_lo], axis=0))
            applied = applied + dot(bx_lo, jnp.concatenate([p_hi, q_hi], axis=0))
            r0.append(act_w * (lf[z] - applied[:, :ry]))
            r1 = jnp.where(group_w == z, applied[:, ry:], r1)
        return r1

    parts = nz // part_z
    bands = []
    spread_y(0)
    for g in range(parts):
        bands.append(band_y(g))
        if g + 1 < parts:
            spread_y(g + 1)
        if g:
            r1 = band_x(g - 1, *bands[g - 1], r1)
    r1 = band_x(parts - 1, *bands[-1], r1)
    r1 = act_t * (load_t - r1)

    per = PATCH // 4
    vz = basis[0, pl.ds(QUARTER, nz), :]
    t1, fast = {}, {}
    zmodes, corr = {}, {}

    def to_modes(g):
        for k in range(g * per, (g + 1) * per):
            rows = pl.ds(k * wide, wide)
            v = None
            for z in range(nz):
                term = basis_s[0, QUARTER + z, k] * r0[z]
                v = term if v is None else v + term
            put3(r3, rows, 0, full, v)
            put3(r3, rows, ry, full, r1 * v_vec[k])

    def to_y(g):
        t1[g] = dot(r3[pl.ds(g * per * wide, per * wide), :], wy3[...])

    def solve_x(g):
        for i in range(per):
            k = g * per + i
            h, l = split(t1[g][i * wide : (i + 1) * wide])
            h, l = split(dot(g3, jnp.concatenate([h, l, h], axis=0)) * dinv[k])
            back = dot(b3, jnp.concatenate([h, l, h], axis=0))
            put3(tb3, pl.ds(k * wide, wide), 0, qy, back)

    def from_y(g):
        fast[g] = dot(tb3[pl.ds(g * per * wide, per * wide), :], wyt3[...])

    def cut_take(m):
        window = rs[:, pl.ds(0, near), :]
        for a in range(1, blocks_x):
            window = jnp.where(cut_a[m] == a, rs[:, pl.ds(a * HALF, near), :], window)
        h, l = split(window.reshape(nz * near, full))
        taken = (dot(h, sel[m]) + dot(l, sel[m])).reshape(nz, near, cells)
        patch = jnp.sum(jnp.where(spot[None], taken, 0.0), axis=1)
        modes = None
        for z in range(nz):
            term = vz_t[z] * patch[z : z + 1, :]
            modes = term if modes is None else modes + term
        zmodes[m] = modes.astype(bf16)

    def cut_solve(m):
        c = jnp.zeros((nz, cells), f32)
        for k in range(PATCH):
            c = c + vz[:, k : k + 1] * dot_nt(zmodes[m], inv[m, k])[k : k + 1, :]
        corr[m] = jnp.where(cut[m] >= 0, c, 0.0)

    def cut_place(m):
        h, l = split(jnp.where(spot[None], corr[m][:, None, :], 0.0).reshape(nz * near, cells))
        cw[m] = (dot(h, sel_t[m]) + dot(l, sel_t[m])).reshape(nz, near, full)

    def per_slot(step):
        for m in range(slots):
            step(m)

    def fast_rows(k):
        return fast[k // per][(k % per) * wide : (k % per + 1) * wide]

    sums = {"edge": jnp.zeros((wide, LANES), f32)}
    rims = [(z, start) for z in range(nz) for start in (0, HALO + rx)]
    for key in rims:
        sums[key] = jnp.zeros((HALO, ry), f32)

    def add_group(g):
        for k in range(g * per, (g + 1) * per):
            rows = fast_rows(k)
            sums["edge"] = sums["edge"] + v_vec[k] * rows[:, ry:]
            for z, start in rims:
                sums[z, start] = sums[z, start] + basis_s[0, QUARTER + z, k] * rows[start : start + HALO, :ry]

    to_modes(0)
    to_y(0)
    for z in range(nz):
        rs[z, :, pl.ds(0, ry)] = r0[z]
        rs[z, :, pl.ds(ry, LANES)] = jnp.where(group_w == z, r1, 0.0)
    to_modes(1)
    per_slot(cut_take)
    to_y(1)
    solve_x(0)
    to_modes(2)
    to_y(2)
    solve_x(1)
    from_y(0)
    to_modes(3)
    per_slot(cut_solve)
    to_y(3)
    solve_x(2)
    from_y(1)
    per_slot(cut_place)
    solve_x(3)
    add_group(0)
    from_y(2)
    add_group(1)
    from_y(3)
    add_group(2)
    add_group(3)

    def cut_part(z, start, count, lanes):
        tiles = []
        for r in range(start // HALF, (start + count) // HALF):
            out = jnp.zeros((HALF, LANES), f32)
            for m in range(slots):
                for a in range(blocks_x):
                    if 0 <= r - a < near // HALF:
                        out = out + jnp.where(cut_a[m] == a, cw[m, z, pl.ds((r - a) * HALF, HALF), lanes], 0.0)
            tiles.append(out)
        return jnp.concatenate(tiles, axis=0)

    def total_rows(z, start, count):
        t = cut_part(z, start, count, pl.ds(0, ry))
        for k in range(PATCH):
            t = t + basis_s[0, QUARTER + z, k] * fast_rows(k)[start : start + count, :ry]
        tot[z, pl.ds(start, count), :] = t

    packed = jnp.zeros((wide, LANES), f32)
    for z in range(nz):
        packed = jnp.where(group_w == z, cut_part(z, 0, wide, pl.ds(ry, LANES)), packed)
    edge[...] = packed + sums["edge"]
    for z, start in rims:
        tot[z, pl.ds(start, HALO), :] = sums[z, start] + cut_part(z, start, HALO, pl.ds(0, ry))
    for j in range(nz // 2):
        for i, r, natural in ((0, HALO + rx, top), (1, 0, ~top)):
            odd = pltpu.roll(tot[2 * j + 1, pl.ds(r, HALO), :], QUARTER, 0)
            rim_x[i, j] = jnp.where(natural, tot[2 * j, pl.ds(r, HALO), :], odd)

    start_all(copy2)
    for z in range(nz):
        total_rows(z, HALO, rx)
    wait_send_all(copy1)
    wait_recv_all(copy2)

    gap = jnp.zeros((rx - 2 * HALO, LANES), f32)
    l2 = left2[...] + jnp.concatenate([corners[0], gap, corners[2]], axis=0)
    r2 = right2[...] + jnp.concatenate([corners[1], gap, corners[3]], axis=0)
    both = jnp.where(lows, r2, l2)
    rim = (lane < QUARTER) | (lane >= ry - QUARTER)
    scale = damping * ext[nz, own, :]
    for z in range(nz):
        moved = pltpu.roll(both, (LANES - QUARTER - half - HALF * z) % LANES, 1)
        u, d = up[z // 2], down[z // 2]
        if z % 2:
            u, d = pltpu.roll(u, QUARTER, 0), pltpu.roll(d, QUARTER, 0)
        t = tot[z, own, :] + jnp.concatenate([jnp.where(top, u, 0.0), gap, jnp.where(top, 0.0, d)], axis=0)
        t = t + jnp.where(rim, moved, 0.0)
        out[z] = state[z] + scale * t

    wait_send_all(copy2)


def on_device(
    sizes, state, load_vector, active, stiff_band, mass_band, eig_basis, eig_values, cut_cols, cut_inverse
):
    nz, rx, ry = state.shape
    slots = cut_cols.shape[-1]
    assert nz == HALF and ry == LANES and rx % PATCH == 0
    inverse = cut_inverse.reshape(cut_inverse.shape[2:])
    wide = rx + 2 * HALO
    full = ry + LANES
    qx, qy = (rx // HALF) * PATCH, (ry // HALF) * PATCH
    cells = PATCH * PATCH
    anyspace = pl.BlockSpec(memory_space=pltpu.HBM)
    V, S = pltpu.VMEM, pltpu.SMEM
    dma = pltpu.SemaphoreType.DMA
    n = len(DIRS)
    return pl.pallas_call(
        functools.partial(kernel, sizes),
        out_shape=pltpu.VMEM(state.shape, f32),
        in_specs=[anyspace] * 9,
        out_specs=pl.BlockSpec(memory_space=pltpu.VMEM),
        scratch_shapes=[
            V(state.shape, f32), V(load_vector.shape, load_vector.dtype), V(active.shape, active.dtype),
            S(stiff_band.shape, f32), S(mass_band.shape, f32), S(eig_basis.shape, f32),
            V(eig_basis.shape, f32), S(eig_values.shape, f32), S(cut_cols.shape, cut_cols.dtype),
            V((slots, PATCH, cells, cells), bf16),
            V((nz + 1 + nz // 2, wide, ry), f32), V((nz, wide, ry), f32),
            V((wide, LANES), f32), V((wide, LANES), f32),
            V((rx, LANES), f32), V((rx, LANES), f32),
            V((3 * full, 2 * full), bf16), V((3 * full, qy), bf16), V((3 * qy, full), bf16),
            V((slots, full, cells), bf16), V((slots, cells, full), bf16),
            V((PATCH, qx, qy), f32),
            V((nz, wide, full), f32), V((slots, nz, PATCH + HALF, full), f32),
            V((nz, wide, ry), f32), V((nz, wide, ry), f32),
            V((nz * wide, 3 * full), bf16), V((nz * wide, 3 * full), bf16),
            V((PATCH * wide, 3 * full), bf16), V((PATCH * wide, 3 * qy), bf16),
            V((nz, wide, ry), f32), V((wide, LANES), f32),
            V((2, nz // 2, HALO, ry), f32),
            V((nz // 2, HALO, ry), f32), V((nz // 2, HALO, ry), f32),
            V((rx, LANES), f32), V((rx, LANES), f32),
            V((4, HALO, LANES), f32),
            dma((10,)), dma((n,)), dma((n,)), dma((n,)), dma((n,)),
        ],
        compiler_params=pltpu.CompilerParams(
            collective_id=0, has_side_effects=True, vmem_limit_bytes=56 * 1024 * 1024
        ),
    )(state, load_vector, active, stiff_band, mass_band, eig_basis, eig_values, cut_cols, inverse)


def solution(mesh):
    placed = (
        P(None, "gx", "gy"),
        P(None, "gx", "gy"),
        P("gx", "gy"),
        P(),
        P(),
        P(),
        P(),
        P("gx", "gy", None),
        P("gx", "gy", None, None, None, None),
    )
    sizes = (mesh.shape["gx"], mesh.shape["gy"])
    return jax.shard_map(
        functools.partial(on_device, sizes),
        mesh=mesh, in_specs=placed, out_specs=P(None, "gx", "gy"), check_vma=False,
    )
```
